32 devices in a mesh: dp: 8 (over z, core), expert: 4 (over y, x).
Axes of the slice: x: 2, y: 2, z: 4, core: 2. Of those that a mesh axis runs over, the one named last changes fastest.
Arguments:
- gen_rows: bfloat16 [4096, 2048], P(('dp', 'expert')), may hold values from -6 to 6
- gen_lengths: int32 [8, 4, 8], P('dp', 'expert'), may hold values from 1 to 16, as said below
- gen_adv: bfloat16 [8, 4, 8], P('dp', 'expert'), may hold values from -4 to 4
- destination: int32 [8, 4, 8], P('dp', 'expert'), may hold values from 0 to 7, as said below
- expert_ids: int32 [4096, 2], P(('dp', 'expert')), may hold values from 0 to 3, all different within a row; in each aligned block of 128 rows (0 to 127, 128 to 255, ...) at most 128 rows name the same one
- gate_values: float32 [4096, 2], P(('dp', 'expert')), may hold values from 0.1 to 1
- cotangent: bfloat16 [4096, 2048], P(('dp', 'expert')), may hold values from -6 to 6
- w_gate: bfloat16 [4, 2048, 768], P('expert'), may hold values from -0.125 to 0.125
- w_up: bfloat16 [4, 2048, 768], P('expert'), may hold values from -0.125 to 0.125
- w_down: bfloat16 [4, 768, 2048], P('expert'), may hold values from -0.21875 to 0.21875
Outputs:
- layer_out: bfloat16 [4096, 2048], P(('dp', 'expert'))
- input_grad: bfloat16 [4096, 2048], P(('dp', 'expert'))
- grad_gate: bfloat16 [4, 2048, 768], P('expert', 'dp')
- grad_up: bfloat16 [4, 2048, 768], P('expert', 'dp')
- grad_down: bfloat16 [4, 768, 2048], P('expert', 'dp')
The draws below stay inside these ranges and needn't reach their ends.
Inputs may be any that keep to these rules, and one draw needn't show every extreme that they name: `gen_lengths`: every device holds a sequence of exactly 16 tokens. `destination`: the sequences of one generation device go to distinct trainer ranks, and each trainer device receives exactly 8 sequences. `expert_ids`: within the rows of one device, no expert is named more than 128 times, a bound that some block reaches.
All inputs are finite; a program needn't handle non-finite values.
Results may differ from the reference program's by a relative error of at most 0.017.
Values may be sent and summed in bfloat16 or wider, within the bound.
No kernel may reach another device: no remote copies, remote signals or barrier semaphores. Data moves between devices by JAX's collectives and lax.ppermute only.
A program may use at most 128 MiB of HBM per device.

```python
import math
import jax
import jax.numpy as jnp
import numpy as np
from jax import lax

D = 2048
FF = 768
TOP = 2
SEQ_DEV = 8
SLOT = 16
EXPERTS = 4
CAPE = 128
ROWS = 4096
N_DP = 8
N_EXPERT = 4


def draw_gen_lengths(key, part):
    subkeys = jax.random.split(key, 2)
    lengths = jax.random.randint(subkeys[0], (N_DP, N_EXPERT, SEQ_DEV), 1, SLOT + 1)
    longest = jax.random.randint(subkeys[1], (N_DP, N_EXPERT, 1), 0, SEQ_DEV)
    places = jnp.arange(SEQ_DEV, dtype=jnp.int32)[None, None, :]
    return jnp.where(places == longest, SLOT, lengths).astype(jnp.int32)


def draw_destination(key, part):
    subkeys = jax.random.split(key, 3)
    first_perm = jax.vmap(lambda k: jax.random.permutation(k, N_DP))(jax.random.split(subkeys[0], N_EXPERT))
    second_perm = jax.vmap(lambda k: jax.random.permutation(k, N_DP))(jax.random.split(subkeys[1], N_EXPERT))
    rotation = jax.random.randint(subkeys[2], (N_DP, N_EXPERT), 0, SEQ_DEV)
    offset = (jnp.arange(SEQ_DEV, dtype=jnp.int32)[None, None, :] + rotation[:, :, None]) % SEQ_DEV
    circle = (first_perm.T[:, :, None] + offset) % N_DP
    trainer = second_perm[jnp.arange(N_EXPERT, dtype=jnp.int32)[None, :, None], circle]
    return trainer.astype(jnp.int32)


def levels(stream_key, extent, cuts, smallest, high):
    loudness, own = 1.0, jax.random.fold_in(stream_key, 6)
    for dim, shards_of in cuts:
        heights = jnp.exp(jax.random.uniform(jax.random.fold_in(own, dim), (shards_of,), jnp.float32, smallest / len(cuts), high / len(cuts)))
        loudness = loudness * jnp.repeat(heights, extent[dim] // shards_of).reshape([-1 if axis == dim else 1 for axis in range(len(extent))])
    return loudness


def deal_out(own_key, own, number, rows, count, top, bound, lean):
    sequence = jax.random.permutation(own_key, count)
    crowded, common = load_shares(count, rows * top, bound, lean, True), load_shares(count, rows * top, bound, lean, False)
    places = jnp.arange(count)

    def named(sizes, turn):
        used = int((sizes > 0).sum())
        fixed = max(1, used // 4)
        passed = fixed + (places - fixed + turn * (used - fixed)) % max(1, count - fixed)
        return jnp.zeros((count,), jnp.int32).at[sequence[jnp.where(places < fixed, places, passed)]].set(jnp.asarray(sizes, jnp.int32))

    sizes = jnp.where(number % 4 == 0, named(crowded, number // 4), named(common, number - number // 4 - 1))
    mixed = jax.random.permutation(jax.random.fold_in(own, 3), count)
    giver, receiver = mixed[0:count // 2 * 2:2], mixed[1:count // 2 * 2:2]
    room = jnp.minimum(sizes[giver] - 1, bound - sizes[receiver]) // 2
    room = jnp.where((giver == sequence[0]) | (receiver == sequence[0]) | (sizes[receiver] == 0), 0, jnp.maximum(room, 0))
    passed = jax.random.randint(jax.random.fold_in(own, 4), (count // 2,), 0, 1 << 20) % (room + 1)
    sizes = sizes.at[giver].add(-passed).at[receiver].add(passed)
    items = jnp.searchsorted(jnp.cumsum(sizes), jnp.arange(rows * top), side="right").astype(jnp.int32)
    table = items.reshape(top, rows).T
    table = table[jax.random.permutation(jax.random.fold_in(own, 1), rows)]
    turn = jax.random.randint(jax.random.fold_in(own, 2), (rows, 1), 0, top)
    return jnp.take_along_axis(table, (jnp.arange(top)[None, :] + turn) % top, axis=1)


def load_shares(number_of, total, limit, skew, full):
    portions = [(1 << 20) // math.isqrt(standing ** skew) + 1 for standing in range(1, number_of + 1)]
    largest = limit if full else min(limit, max(-(-total // number_of), total * portions[0] // sum(portions)))
    least = 1 if total - largest >= number_of - 1 else 0
    counts, spare = [largest] + [least] * (number_of - 1), total - largest - least * (number_of - 1)
    while spare > 0:
        movable = [i for i in range(1, number_of) if counts[i] < largest] or [i for i in range(1, number_of) if counts[i] < limit]
        whole, budget = sum([portions[i] for i in movable]), spare
        for i in movable:
            addition = min(limit - counts[i], max(1, budget * portions[i] // whole), spare)
            counts[i] = counts[i] + addition
            spare = spare - addition
    return np.array(counts)


def scatter_about(stream_key, dims, deviation, bound, cuts=(), held_as=jnp.bfloat16):
    values = jax.random.normal(stream_key, dims, jnp.float32) * deviation
    if len(cuts) > 0:
        values = levels(stream_key, dims, cuts, -0.22, 0.18) * values
    return jnp.clip(values, min=-bound, max=bound).astype(held_as)


def setup_inputs(seed: int = 0) -> dict:
    seeds = jax.random.split(jax.random.key(seed), 11)
    gen_rows = scatter_about(seeds[0], (ROWS, D), 1.0, 6.0, ((0, 32),))
    gen_lengths = draw_gen_lengths(jax.random.fold_in(seeds[10], 71), 0)
    gen_adv = scatter_about(seeds[2], (N_DP, N_EXPERT, SEQ_DEV), 1.0, 4.0, ((0, 8), (1, 4)))
    destination = draw_destination(jax.random.fold_in(seeds[10], 71), 0)
    expert_ids_keys = jax.random.split(jax.random.fold_in(seeds[4], 1), ROWS // (SEQ_DEV * SLOT))
    expert_ids_turns = jax.random.permutation(jax.random.fold_in(seeds[4], 3), ROWS // (SEQ_DEV * SLOT))
    expert_ids = jax.vmap(lambda own, number: deal_out(jax.random.fold_in(seeds[4], 2), own, number, SEQ_DEV * SLOT, EXPERTS, TOP, CAPE, 2))(expert_ids_keys, expert_ids_turns).reshape((ROWS, TOP))
    gate_values = jnp.clip(0.1 + 0.9 * jax.random.uniform(seeds[5], (ROWS, TOP), jnp.float32) ** levels(seeds[5], (ROWS, TOP), ((0, 32),), -0.2, 0.2), 0.1, 1.0)
    cotangent = scatter_about(seeds[6], (ROWS, D), 1.0, 6.0, ((0, 32),))
    w_gate = scatter_about(seeds[7], (EXPERTS, D, FF), D ** -0.5, 0.125, ((0, 4),))
    w_up = scatter_about(seeds[8], (EXPERTS, D, FF), D ** -0.5, 0.125, ((0, 4),))
    w_down = scatter_about(seeds[9], (EXPERTS, FF, D), FF ** -0.5, 0.21875, ((0, 4),))
    return dict(gen_rows=gen_rows, gen_lengths=gen_lengths, gen_adv=gen_adv, destination=destination, expert_ids=expert_ids, gate_values=gate_values, cotangent=cotangent, w_gate=w_gate, w_up=w_up, w_down=w_down)


def contract(left, right, left_dim, right_dim):
    return lax.dot_general(left, right, (((left_dim,), (right_dim,)), ((), ())), preferred_element_type=jnp.float32)


def expert_pass(expert_in, expert_dy, weight_gate, weight_up, weight_down):
    gate_pre = jnp.dot(expert_in, weight_gate, preferred_element_type=jnp.float32)
    up_pre = jnp.dot(expert_in, weight_up, preferred_element_type=jnp.float32)
    sigmoid_g = jax.nn.sigmoid(gate_pre)
    activated = gate_pre * sigmoid_g
    hidden = (activated * up_pre).astype(jnp.bfloat16)
    outputs = jnp.dot(hidden, weight_down, preferred_element_type=jnp.float32).astype(jnp.bfloat16)
    hidden_grad = contract(expert_dy, weight_down, 1, 1)
    gate_grad = (hidden_grad * up_pre * sigmoid_g * (1.0 + gate_pre * (1.0 - sigmoid_g))).astype(jnp.bfloat16)
    up_grad = (hidden_grad * activated).astype(jnp.bfloat16)
    input_rows = (contract(gate_grad, weight_gate, 1, 1) + contract(up_grad, weight_up, 1, 1)).astype(jnp.bfloat16)
    grad_g = contract(expert_in, gate_grad, 0, 0).astype(jnp.bfloat16)
    grad_u = contract(expert_in, up_grad, 0, 0).astype(jnp.bfloat16)
    grad_d = contract(hidden, expert_dy, 0, 0).astype(jnp.bfloat16)
    return outputs, input_rows, grad_g, grad_u, grad_d


def reference(gen_rows, gen_lengths, gen_adv, destination, expert_ids, gate_values, cotangent, w_gate, w_up, w_down):
    n_gen, n_ex, seq_dev = destination.shape
    model_width = gen_rows.shape[1]
    total_rows = gen_rows.shape[0]
    slot_len = total_rows // (n_gen * n_ex * seq_dev)
    per_token = expert_ids.shape[1]
    experts = w_gate.shape[0]
    hidden_units = w_gate.shape[2]
    tok_rows = seq_dev * slot_len
    capacity = 2 * tok_rows * per_token // experts
    send_table = (destination[..., None] == jnp.arange(n_gen, dtype=jnp.int32)).astype(jnp.int32)
    to_peer = jnp.sum(send_table, axis=2)
    before = jnp.cumsum(to_peer, axis=0) - to_peer
    arrival = jnp.take_along_axis(before, destination, axis=2)
    ex_idx = jnp.arange(n_ex, dtype=jnp.int32)[None, :, None]
    train_seq = ((destination * n_ex + ex_idx) * seq_dev + arrival).reshape(-1).astype(jnp.int32)
    row_index = (train_seq[:, None] * slot_len + jnp.arange(slot_len, dtype=jnp.int32)[None, :]).reshape(-1)
    train_rows = jnp.zeros_like(gen_rows).at[row_index].set(gen_rows)
    total_seq = n_gen * n_ex * seq_dev
    train_len = jnp.zeros((total_seq,), jnp.int32).at[train_seq].set(gen_lengths.reshape(-1))
    train_adv = jnp.zeros((total_seq,), jnp.float32).at[train_seq].set(gen_adv.reshape(-1).astype(jnp.float32))
    position = jnp.arange(total_rows, dtype=jnp.int32) % slot_len
    seq_of = jnp.arange(total_rows, dtype=jnp.int32) // slot_len
    in_length = position < train_len[seq_of]
    seq_scale = jnp.where(in_length, train_adv[seq_of] / train_len[seq_of].astype(jnp.float32), jnp.float32(0.0))
    token_dy = seq_scale[:, None] * cotangent.astype(jnp.float32)
    pair_dy = (gate_values[:, :, None] * token_dy[:, None, :]).astype(jnp.bfloat16)
    rows_d = n_ex * tok_rows
    pair_count = rows_d * per_token
    buffer_rows = n_ex * capacity

    def row_step(totals, inputs):
        x_rows, ids_rows, gates_rows, dy_rows = inputs
        flat_ids = ids_rows.reshape(-1)
        dy_flat = dy_rows.reshape(pair_count, model_width)

        def per_expert(expert):
            is_hit = flat_ids == expert
            running = jnp.cumsum(is_hit.astype(jnp.int32)) - 1
            target = jnp.where(is_hit, running, buffer_rows)
            source = jnp.full((buffer_rows,), pair_count, jnp.int32).at[target].set(jnp.arange(pair_count, dtype=jnp.int32), mode="drop")
            is_valid = source < pair_count
            safe_index = jnp.minimum(source, pair_count - 1)
            expert_in = jnp.where(is_valid[:, None], x_rows[safe_index // per_token], jnp.zeros((), jnp.bfloat16))
            expert_dy = jnp.where(is_valid[:, None], dy_flat[safe_index], jnp.zeros((), jnp.bfloat16))
            outputs, input_rows, grad_g, grad_u, grad_d = expert_pass(expert_in, expert_dy, w_gate[expert], w_up[expert], w_down[expert])
            return outputs, input_rows, source, grad_g, grad_u, grad_d

        outputs, input_rows, source, grad_g, grad_u, grad_d = lax.map(per_expert, jnp.arange(experts, dtype=jnp.int32))
        flat_source = source.reshape(-1)
        pair_out = jnp.zeros((pair_count + 1, model_width), jnp.bfloat16).at[flat_source].set(outputs.reshape(-1, model_width))[:pair_count]
        pair_dx = jnp.zeros((pair_count + 1, model_width), jnp.bfloat16).at[flat_source].set(input_rows.reshape(-1, model_width))[:pair_count]
        out_rows = jnp.sum(gates_rows[:, :, None] * pair_out.reshape(rows_d, per_token, model_width).astype(jnp.float32), axis=1).astype(jnp.bfloat16)
        dx_rows = jnp.sum(pair_dx.reshape(rows_d, per_token, model_width).astype(jnp.float32), axis=1).astype(jnp.bfloat16)
        totals = (totals[0] + grad_g.astype(jnp.float32), totals[1] + grad_u.astype(jnp.float32), totals[2] + grad_d.astype(jnp.float32))
        return totals, (out_rows, dx_rows)

    start = (jnp.zeros((experts, model_width, hidden_units), jnp.float32), jnp.zeros((experts, model_width, hidden_units), jnp.float32), jnp.zeros((experts, hidden_units, model_width), jnp.float32))
    inputs = (train_rows.reshape(n_gen, rows_d, model_width), expert_ids.reshape(n_gen, rows_d, per_token), gate_values.reshape(n_gen, rows_d, per_token), pair_dy.reshape(n_gen, rows_d, per_token, model_width))
    totals, stacked = lax.scan(row_step, start, inputs)
    layer_out = stacked[0].reshape(total_rows, model_width)
    input_grad = stacked[1].reshape(total_rows, model_width)
    return layer_out, input_grad, totals[0].astype(jnp.bfloat16), totals[1].astype(jnp.bfloat16), totals[2].astype(jnp.bfloat16)
```

```python
import functools

import jax
import jax.numpy as jnp
from jax import lax
from jax.experimental import pallas as pl
from jax.experimental.pallas import tpu as pltpu
from jax.sharding import PartitionSpec as P

CORES = 2
LANES = 128
F32 = jnp.float32
BF16 = jnp.bfloat16
MIB = 1 << 20


def contract(left, right, left_dim, right_dim):
    return lax.dot_general(left, right, (((left_dim,), (right_dim,)), ((), ())), preferred_element_type=F32)


def params(mib, **more):
    return pltpu.CompilerParams(vmem_limit_bytes=mib * MIB, **more)


def vmem():
    return pl.BlockSpec(memory_space=pltpu.VMEM)


def smem():
    return pl.BlockSpec(memory_space=pltpu.SMEM)


def hbm():
    return pl.BlockSpec(memory_space=pl.ANY)


def pick_kernel(me_ref, dest_ref, len_ref, adv_ref, rows_ref, *outs):
    seqs, slot, width = rows_ref.shape
    lane = lax.broadcasted_iota(jnp.int32, (slot, LANES), 1)
    for i, out in enumerate(outs):
        target = me_ref[0] ^ i
        seq = jnp.int32(0)
        live = jnp.int32(0)
        for s in range(seqs):
            hit = dest_ref[s] == target
            seq = jnp.where(hit, s, seq)
            live = jnp.where(hit, 1, live)
        rows = rows_ref[pl.ds(seq, 1)][0]
        length = jnp.where(live == 1, len_ref[seq], 0.0)
        notes = jnp.where(lane == 0, length, jnp.where(lane == 1, adv_ref[seq], 0.0))
        out[:, :width] = rows
        out[:, width:] = notes.astype(BF16)


def pick(me, dest, lengths, adv, rows, n_dp):
    seqs, slot, width = rows.shape
    return pl.pallas_call(
        pick_kernel,
        out_shape=[jax.ShapeDtypeStruct((slot, width + LANES), BF16)] * n_dp,
        in_specs=[smem(), smem(), smem(), smem(), vmem()],
        out_specs=[vmem()] * n_dp,
        compiler_params=params(16),
        name="pick",
    )(me, dest, lengths, adv, rows)


def assemble_kernel(me_ref, *refs):
    pieces, (x_ref, scale_ref) = refs[:-2], refs[-2:]
    slot = pieces[0].shape[0]
    width = x_ref.shape[1]
    position = lax.broadcasted_iota(jnp.int32, (slot, 1), 0).astype(F32)
    for i, piece in enumerate(pieces):
        at = pl.multiple_of((me_ref[0] ^ i) * slot, slot)
        x_ref[pl.ds(at, slot), :] = piece[:, :width]
        notes = piece[:, width:].astype(F32)
        length, adv = notes[:, 0:1], notes[:, 1:2]
        scale_ref[pl.ds(at, slot), :] = jnp.where(position < length, adv / length, 0.0)


def assemble(me, pieces, width):
    slot = pieces[0].shape[0]
    rows = slot * len(pieces)
    return pl.pallas_call(
        assemble_kernel,
        out_shape=[jax.ShapeDtypeStruct((rows, width), BF16), jax.ShapeDtypeStruct((rows, 1), F32)],
        in_specs=[smem()] + [vmem()] * len(pieces),
        out_specs=[vmem()] * 2,
        compiler_params=params(16),
        name="assemble",
    )(me, *pieces)


def reassign(gen_rows, gen_lengths, gen_adv, destination, n_dp):
    seq_dev = destination.shape[2]
    width = gen_rows.shape[1]
    slot = gen_rows.shape[0] // seq_dev
    g = lax.axis_index("dp")
    me = g.reshape(1).astype(jnp.int32)
    pieces = pick(
        me,
        destination[0, 0],
        gen_lengths[0, 0].astype(F32),
        gen_adv[0, 0].astype(F32),
        gen_rows.reshape(seq_dev, slot, width),
        n_dp,
    )
    got = [pieces[0]]
    for i in range(1, n_dp):
        got.append(lax.ppermute(pieces[i], "dp", [(d, d ^ i) for d in range(n_dp)]))
    if n_dp == seq_dev:
        return assemble(me, got, width)
    stack = jnp.stack(got)[jnp.arange(n_dp, dtype=jnp.int32) ^ g]
    lengths = stack[:, 0, width].astype(F32)
    adv = stack[:, 0, width + 1].astype(F32)
    arrived = lengths > 0
    arrival = jnp.cumsum(arrived.astype(jnp.int32)) - 1
    chosen = arrived[None, :] & (arrival[None, :] == jnp.arange(seq_dev, dtype=jnp.int32)[:, None])
    from_peer = jnp.sum(jnp.where(chosen, jnp.arange(n_dp, dtype=jnp.int32)[None, :], 0), axis=1)
    x = stack[from_peer][:, :, :width].reshape(seq_dev * slot, width)
    position = jnp.arange(slot, dtype=jnp.int32).astype(F32)
    length = lengths[from_peer][:, None]
    scale = jnp.where(position[None, :] < length, adv[from_peer][:, None] / length, 0.0)
    return x, scale.reshape(seq_dev * slot, 1)


def swap(value, i, n_ex):
    return lax.ppermute(value, "expert", [(d, d ^ i) for d in range(n_ex)])


def gather_rows(rows, n_ex):
    if n_ex != 4:
        return [rows] + [swap(rows, i, n_ex) for i in range(1, n_ex)]
    half = rows.shape[0] // 2
    first = swap(rows, 1, n_ex)
    second = swap(rows, 2, n_ex)
    return [rows, first, second, swap(first[:half], 2, n_ex), swap(second[half:], 1, n_ex)]


def load_pieces(pieces, whole, sems):
    at, copies = 0, []
    for i, piece in enumerate(pieces):
        size = piece.shape[0]
        copies.append(pltpu.make_async_copy(piece, whole.at[pl.ds(at, size)], sems.at[i]))
        at += size
    for copy in copies:
        copy.start()
    for copy in copies:
        copy.wait()


def hidden_grad_kernel(count, w_ref, *refs):
    pieces, (out, whole_out, whole, sems, out_sem) = refs[:count], refs[count:]
    step = pl.program_id(0)

    @pl.when(step == 0)
    def _():
        load_pieces(pieces, whole, sems)
        pltpu.make_async_copy(whole, whole_out, out_sem).start()

    out[...] = contract(whole[...], w_ref[...], 1, 1)

    @pl.when(step == pl.num_programs(0) - 1)
    def _():
        pltpu.make_async_copy(whole, whole_out, out_sem).wait()


def hidden_grad(pieces, w_down):
    rows = sum(p.shape[0] for p in pieces)
    units, width = w_down.shape
    tile = 256
    return pl.pallas_call(
        functools.partial(hidden_grad_kernel, len(pieces)),
        grid=(units // tile,),
        out_shape=[jax.ShapeDtypeStruct((rows, units), F32), jax.ShapeDtypeStruct((rows, width), BF16)],
        in_specs=[pl.BlockSpec((tile, width), lambda j: (j, 0))] + [hbm()] * len(pieces),
        out_specs=[pl.BlockSpec((rows, tile), lambda j: (0, j)), hbm()],
        scratch_shapes=[
            pltpu.VMEM((rows, width), BF16),
            pltpu.SemaphoreType.DMA((len(pieces),)),
            pltpu.SemaphoreType.DMA,
        ],
        compiler_params=params(32),
        cost_estimate=pl.CostEstimate(
            flops=2 * rows * units * width, bytes_accessed=2 * units * width + 4 * rows * width, transcendentals=0
        ),
        name="hidden_grad",
    )(w_down, *pieces)


def units_kernel(count, wg_ref, wu_ref, hg_ref, gs_ref, *refs):
    pieces, (gate_out, up_out, hid_out, hs_out, whole_out, whole, sems, out_sem) = refs[:count], refs[count:]
    step = pl.program_id(0)

    @pl.when(step == 0)
    def _():
        load_pieces(pieces, whole, sems)
        pltpu.make_async_copy(whole, whole_out, out_sem).start()

    x = whole[...]
    gate = jnp.dot(x, wg_ref[...], preferred_element_type=F32)
    up = jnp.dot(x, wu_ref[...], preferred_element_type=F32)
    gs = gs_ref[...]
    sig = jax.nn.sigmoid(gate)
    act = gate * sig
    hid = (act * up).astype(BF16)
    hid_out[...] = hid
    hs_out[...] = (hid.astype(F32) * gs).astype(BF16)
    hg = hg_ref[...] * gs
    gate_out[...] = (hg * up * sig * (1.0 + gate * (1.0 - sig))).astype(BF16)
    up_out[...] = (hg * act).astype(BF16)

    @pl.when(step == pl.num_programs(0) - 1)
    def _():
        pltpu.make_async_copy(whole, whole_out, out_sem).wait()


def hidden_units(pieces, w_gate, w_up, hg, gs):
    rows, units = hg.shape
    width = w_gate.shape[0]
    tile = 256
    columns = pl.BlockSpec((rows, tile), lambda j: (0, j))
    weights = pl.BlockSpec((width, tile), lambda j: (0, j))
    return pl.pallas_call(
        functools.partial(units_kernel, len(pieces)),
        grid=(units // tile,),
        out_shape=[jax.ShapeDtypeStruct((rows, units), BF16)] * 4 + [jax.ShapeDtypeStruct((rows, width), BF16)],
        in_specs=[weights, weights, columns, pl.BlockSpec((rows, 1), lambda j: (0, 0))] + [hbm()] * len(pieces),
        out_specs=[columns] * 4 + [hbm()],
        scratch_shapes=[
            pltpu.VMEM((rows, width), BF16),
            pltpu.SemaphoreType.DMA((len(pieces),)),
            pltpu.SemaphoreType.DMA,
        ],
        compiler_params=params(44),
        cost_estimate=pl.CostEstimate(
            flops=4 * rows * units * width, bytes_accessed=4 * units * width + 4 * rows * width, transcendentals=rows * units
        ),
        name="hidden_units",
    )(w_gate, w_up, hg, gs, *pieces)


def column_grad_kernel(core_ref, x_ref, grad_ref, other, mine):
    value = contract(x_ref[...], grad_ref[...], 0, 0).astype(BF16)

    @pl.when(pl.program_id(0) == 0)
    def _():
        other[0] = value

    @pl.when(pl.program_id(0) == 1)
    def _():
        mine[0] = value


def column_grad(core, x, grad, n_dp):
    rows, width = x.shape
    units = grad.shape[1]
    n_z, shard = n_dp // CORES, width // n_dp
    out = jax.ShapeDtypeStruct((n_z, shard, units), BF16)
    return pl.pallas_call(
        column_grad_kernel,
        grid_spec=pltpu.PrefetchScalarGridSpec(
            num_scalar_prefetch=1,
            grid=(CORES, n_z),
            in_specs=[
                pl.BlockSpec((rows, shard), lambda k, z, core: (0, CORES * z + jnp.where(k == 0, 1 - core[0], core[0]))),
                pl.BlockSpec((rows, units), lambda k, z, core: (0, 0)),
            ],
            out_specs=[
                pl.BlockSpec((1, shard, units), lambda k, z, core: (jnp.where(k == 0, z, n_z - 1), 0, 0)),
                pl.BlockSpec((1, shard, units), lambda k, z, core: (jnp.where(k == 0, 0, z), 0, 0)),
            ],
        ),
        out_shape=[out, out],
        compiler_params=params(24),
        cost_estimate=pl.CostEstimate(
            flops=2 * rows * units * width, bytes_accessed=2 * units * width + 2 * rows * width, transcendentals=0
        ),
        name="column_grad",
    )(core, x, grad)


def row_grad_kernel(core_ref, hid_ref, dy_ref, other, mine):
    value = contract(hid_ref[...], dy_ref[...], 0, 0).astype(BF16)
    n_z, shard, _ = mine.shape

    for z in range(n_z):
        low = value[CORES * z * shard : (CORES * z + 1) * shard]
        high = value[(CORES * z + 1) * shard : (CORES * z + 2) * shard]

        @pl.when(core_ref[0] == 0)
        def _(low=low, high=high, z=z):
            mine[z] = low
            other[z] = high

        @pl.when(core_ref[0] == 1)
        def _(low=low, high=high, z=z):
            mine[z] = high
            other[z] = low


def row_grad(core, hid, dy, n_dp):
    rows, units = hid.shape
    width = dy.shape[1]
    n_z, shard = n_dp // CORES, units // n_dp
    tile = 512
    out = jax.ShapeDtypeStruct((n_z, shard, width), BF16)
    block = pl.BlockSpec((n_z, shard, tile), lambda j, core: (0, 0, j))
    return pl.pallas_call(
        row_grad_kernel,
        grid_spec=pltpu.PrefetchScalarGridSpec(
            num_scalar_prefetch=1,
            grid=(width // tile,),
            in_specs=[
                pl.BlockSpec((rows, units), lambda j, core: (0, 0)),
                pl.BlockSpec((rows, tile), lambda j, core: (0, j)),
            ],
            out_specs=[block, block],
        ),
        out_shape=[out, out],
        compiler_params=params(32),
        cost_estimate=pl.CostEstimate(
            flops=2 * rows * units * width, bytes_accessed=2 * units * width + 2 * rows * width, transcendentals=0
        ),
        name="row_grad",
    )(core, hid, dy)


def outputs_kernel(n_ex, hid_ref, w_ref, *outs):
    value = jnp.dot(hid_ref[...], w_ref[...], preferred_element_type=F32).astype(BF16)
    size = outs[0].shape[0]
    for i in range(n_ex):
        outs[i][...] = value[i * size : (i + 1) * size]


def layer_outputs(hid, w_down, n_ex):
    rows, units = hid.shape
    width = w_down.shape[1]
    tile = 512
    size = rows // n_ex
    return pl.pallas_call(
        functools.partial(outputs_kernel, n_ex),
        grid=(width // tile,),
        out_shape=[jax.ShapeDtypeStruct((size, width), BF16)] * n_ex,
        in_specs=[pl.BlockSpec((rows, units), lambda j: (0, 0)), pl.BlockSpec((units, tile), lambda j: (0, j))],
        out_specs=[pl.BlockSpec((size, tile), lambda j: (0, j))] * n_ex,
        compiler_params=params(32),
        cost_estimate=pl.CostEstimate(
            flops=2 * rows * units * width, bytes_accessed=2 * units * width + 2 * rows * width, transcendentals=0
        ),
        name="layer_outputs",
    )(hid, w_down)


def input_grads_kernel(n_ex, gate_ref, up_ref, wg_ref, wu_ref, *outs):
    value = contract(gate_ref[...], wg_ref[...], 1, 1) + contract(up_ref[...], wu_ref[...], 1, 1)
    value = value.astype(BF16)
    size = outs[0].shape[0]
    for i in range(n_ex):
        outs[i][...] = value[i * size : (i + 1) * size]


def input_grads(gate_grad, up_grad, w_gate, w_up, n_ex):
    rows, units = gate_grad.shape
    width = w_gate.shape[0]
    tile = 512
    size = rows // n_ex
    whole = pl.BlockSpec((rows, units), lambda j: (0, 0))
    weights = pl.BlockSpec((tile, units), lambda j: (j, 0))
    return pl.pallas_call(
        functools.partial(input_grads_kernel, n_ex),
        grid=(width // tile,),
        out_shape=[jax.ShapeDtypeStruct((size, width), BF16)] * n_ex,
        in_specs=[whole, whole, weights, weights],
        out_specs=[pl.BlockSpec((size, tile), lambda j: (0, j))] * n_ex,
        compiler_params=params(40),
        cost_estimate=pl.CostEstimate(
            flops=4 * rows * units * width, bytes_accessed=4 * units * width + 2 * rows * width, transcendentals=0
        ),
        name="input_grads",
    )(gate_grad, up_grad, w_gate, w_up)


def take(parts, at):
    total = None
    for part in parts:
        value = lax.dynamic_index_in_dim(part, at, 0, keepdims=False).astype(F32)
        total = value if total is None else total + value
    return total


def line_steps(all_parts, n_dp):
    n_z = n_dp // CORES
    z = lax.axis_index("dp") // CORES
    right = [None] * len(all_parts)
    left = [None] * len(all_parts)
    for s in range(1, n_z):
        to_right = [(CORES * k + c, CORES * (k + 1) + c) for k in range(s) for c in range(CORES)]
        to_left = [(CORES * (n_z - 1 - k) + c, CORES * (n_z - 2 - k) + c) for k in range(s) for c in range(CORES)]
        for p, parts in enumerate(all_parts):
            up = take(parts, jnp.minimum(n_z - s + z, n_z - 1))
            down = take(parts, jnp.maximum(s + z - n_z, 0))
            if s > 1:
                up = up + right[p].astype(F32)
                down = down + left[p].astype(F32)
            right[p] = lax.ppermute(up.astype(BF16), "dp", to_right)
            left[p] = lax.ppermute(down.astype(BF16), "dp", to_left)
    out = []
    for p, parts in enumerate(all_parts):
        total = take(parts, z)
        if n_z > 1:
            total = total + right[p].astype(F32) + left[p].astype(F32)
        out.append(total.astype(BF16))
    return out


def on_device(
    gen_rows, gen_lengths, gen_adv, destination, expert_ids, gate_values, cotangent, w_gate, w_up, w_down
):
    n_dp = lax.axis_size("dp")
    n_ex = lax.axis_size("expert")
    weight_gate, weight_up, weight_down = w_gate[0], w_up[0], w_down[0]
    g, e = lax.axis_index("dp"), lax.axis_index("expert")
    core = (g % CORES).reshape(1).astype(jnp.int32)
    other_core = [(d, d ^ 1) for d in range(n_dp)]

    cot_pieces = gather_rows(cotangent, n_ex)
    x, scale = reassign(gen_rows, gen_lengths, gen_adv, destination, n_dp)
    x_pieces = gather_rows(x, n_ex)

    gates = [
        jnp.sum(jnp.where(expert_ids == (e ^ i), gate_values, 0.0), axis=1, keepdims=True) for i in range(n_ex)
    ]
    gs = [gates[0] * scale] + [swap(gates[i] * scale, i, n_ex) for i in range(1, n_ex)]
    gs = jnp.concatenate(gs, axis=0)

    hg, dy_all = hidden_grad(cot_pieces, weight_down)
    gate_grad, up_grad, hid, hid_scaled, x_all = hidden_units(x_pieces, weight_gate, weight_up, hg, gs)

    gate_other, gate_mine = column_grad(core, x_all, gate_grad, n_dp)
    gate_got = lax.ppermute(gate_other, "dp", other_core)
    up_other, up_mine = column_grad(core, x_all, up_grad, n_dp)
    up_got = lax.ppermute(up_other, "dp", other_core)
    down_other, down_mine = row_grad(core, hid_scaled, dy_all, n_dp)
    down_got = lax.ppermute(down_other, "dp", other_core)

    outs = layer_outputs(hid, weight_down, n_ex)
    outs = [outs[0]] + [swap(outs[i], i, n_ex) for i in range(1, n_ex)]
    grads = input_grads(gate_grad, up_grad, weight_gate, weight_up, n_ex)
    grads = [grads[0]] + [swap(grads[i], i, n_ex) for i in range(1, n_ex)]

    sums = line_steps([(gate_mine, gate_got), (up_mine, up_got), (down_mine, down_got)], n_dp)
    layer_out = sum(gates[i] * outs[i].astype(F32) for i in range(n_ex)).astype(BF16)
    input_grad = sum(part.astype(F32) for part in grads).astype(BF16)
    return layer_out, input_grad, sums[0][None], sums[1][None], sums[2][None]


def solution(mesh):
    rows = P(("dp", "expert"), None)
    seqs = P("dp", "expert", None)
    weights = P("expert", None, None)
    shards = P("expert", "dp", None)
    return jax.shard_map(
        on_device,
        mesh=mesh,
        in_specs=(rows, seqs, seqs, seqs, rows, rows, rows, weights, weights, weights),
        out_specs=(rows, rows, shards, shards, shards),
        check_vma=False,
    )
```

```python
import functools

import jax
import jax.numpy as jnp
from jax import lax
from jax.experimental import pallas as pl
from jax.experimental.pallas import tpu as pltpu
from jax.sharding import PartitionSpec as P

CORES = 2
LANES = 128
F32 = jnp.float32
BF16 = jnp.bfloat16
MIB = 1 << 20


def contract(left, right, left_dim, right_dim):
    return lax.dot_general(left, right, (((left_dim,), (right_dim,)), ((), ())), preferred_element_type=F32)


def params(mib, **more):
    return pltpu.CompilerParams(vmem_limit_bytes=mib * MIB, **more)


def vmem():
    return pl.BlockSpec(memory_space=pltpu.VMEM)


def hbm():
    return pl.BlockSpec(memory_space=pl.ANY)


LENGTH, ADV, GATES = 0, 1, 2
PARTS = 3


def pick_kernel(n_dp, dest_hbm, len_ref, adv_ref, rows_ref, *refs):
    outs, (dest_ref, sem) = refs[:n_dp], refs[n_dp:]
    copy = pltpu.make_async_copy(dest_hbm, dest_ref, sem)
    copy.start()
    seqs, slot, width = rows_ref.shape
    lane = lax.broadcasted_iota(jnp.int32, (slot, LANES), 1)
    which = lax.broadcasted_iota(jnp.int32, (1, seqs), 1)
    lengths = len_ref[0].astype(F32)
    advs = adv_ref[0].astype(F32)
    me = lax.axis_index("dp")
    copy.wait()
    for i, out in enumerate(outs):
        seq = jnp.int32(0)
        live = jnp.int32(0)
        for s in range(seqs):
            hit = dest_ref[0, 0, s] == (me ^ i)
            seq = jnp.where(hit, s, seq)
            live = jnp.where(hit, 1, live)
        mine = (which == seq) & (live == 1)
        length = jnp.sum(jnp.where(mine, lengths, 0.0), axis=1, keepdims=True)
        adv = jnp.sum(jnp.where(mine, advs, 0.0), axis=1, keepdims=True)
        out[:, :width] = rows_ref[pl.ds(seq, 1)][0]
        out[:, width:] = jnp.where(lane == LENGTH, length, jnp.where(lane == ADV, adv, 0.0)).astype(BF16)


def pick(dest, lengths, adv, rows, n_dp):
    seqs, slot, width = rows.shape
    return pl.pallas_call(
        functools.partial(pick_kernel, n_dp),
        out_shape=[jax.ShapeDtypeStruct((slot, width + LANES), BF16)] * n_dp,
        in_specs=[hbm(), vmem(), vmem(), vmem()],
        out_specs=[vmem()] * n_dp,
        scratch_shapes=[pltpu.SMEM(dest.shape, jnp.int32), pltpu.SemaphoreType.DMA],
        compiler_params=params(16),
        name="pick",
    )(dest, lengths, adv, rows)


def gate_notes(ids, gates):
    lane = lax.broadcasted_iota(jnp.int32, (ids.shape[0], LANES), 1) - GATES
    expert = lane // PARTS
    value = jnp.zeros(lane.shape, F32)
    for k in range(ids.shape[1]):
        value = value + jnp.where(ids[:, k : k + 1] == expert, gates[:, k : k + 1], 0.0)
    value = jnp.where(lane < 0, 0.0, value)
    high = value.astype(BF16).astype(F32)
    middle = (value - high).astype(BF16).astype(F32)
    low = value - high - middle
    part = lane % PARTS
    return jnp.where(part == 0, high, jnp.where(part == 1, middle, low))


def assemble_kernel(n_dp, ids_ref, gates_ref, *refs):
    pieces, x_ref = refs[:n_dp], refs[-1]
    slot, wide = pieces[0].shape
    width = wide - LANES
    me = lax.axis_index("dp")
    for i, piece in enumerate(pieces):
        at = pl.multiple_of((me ^ i) * slot, slot)
        x_ref[pl.ds(at, slot), :] = piece[...]
    notes = gate_notes(ids_ref[...], gates_ref[...])
    x_ref[:, width:] = (x_ref[:, width:].astype(F32) + notes).astype(BF16)


def assemble(pieces, ids, gates, after):
    slot, wide = pieces[0].shape
    n_dp = len(pieces)
    return pl.pallas_call(
        functools.partial(assemble_kernel, n_dp),
        out_shape=jax.ShapeDtypeStruct((slot * n_dp, wide), BF16),
        in_specs=[vmem()] * (2 + n_dp) + [hbm()] * len(after),
        out_specs=vmem(),
        compiler_params=params(16),
        name="assemble",
    )(ids, gates, *pieces, *after)


def reassign(gen_rows, gen_lengths, gen_adv, destination, ids, gates, after, n_dp):
    seq_dev = destination.shape[2]
    width = gen_rows.shape[1]
    slot = gen_rows.shape[0] // seq_dev
    g = lax.axis_index("dp")
    pieces = pick(destination, gen_lengths, gen_adv, gen_rows.reshape(seq_dev, slot, width), n_dp)
    got = [None] * n_dp
    got[0] = pieces[0]
    for i in reversed(range(1, n_dp)):
        got[i] = lax.ppermute(pieces[i], "dp", [(d, d ^ i) for d in range(n_dp)])
    if n_dp == seq_dev:
        return assemble(got, ids, gates, after)
    stack = jnp.stack(got)[jnp.arange(n_dp, dtype=jnp.int32) ^ g]
    arrived = stack[:, 0, width + LENGTH] > 0
    arrival = jnp.cumsum(arrived.astype(jnp.int32)) - 1
    chosen = arrived[None, :] & (arrival[None, :] == jnp.arange(seq_dev, dtype=jnp.int32)[:, None])
    from_peer = jnp.sum(jnp.where(chosen, jnp.arange(n_dp, dtype=jnp.int32)[None, :], 0), axis=1)
    x = stack[from_peer].reshape(seq_dev * slot, width + LANES)
    notes = (x[:, width:].astype(F32) + gate_notes(ids, gates)).astype(BF16)
    return jnp.concatenate([x[:, :width], notes], axis=1)


def swap(value, i, n_ex):
    return lax.ppermute(value, "expert", [(d, d ^ i) for d in range(n_ex)])


def gather_rows(rows, n_ex):
    if n_ex != 4:
        return [rows] + [swap(rows, i, n_ex) for i in range(1, n_ex)]
    half = rows.shape[0] // 2
    first = swap(rows, 1, n_ex)
    second = swap(rows, 2, n_ex)
    return [rows, first, second, swap(first[:half], 2, n_ex), swap(second[half:], 1, n_ex)]


def with_last(pieces, size):
    at, cut = 0, sum(p.shape[0] for p in pieces) - size
    for i, piece in enumerate(pieces):
        if at == cut:
            return pieces[:i], pieces[i:]
        at += piece.shape[0]


def tie(value, *others):
    return lax.optimization_barrier((value,) + others)[0]


def load_pieces(pieces, whole, sems):
    at, copies = 0, []
    for i, piece in enumerate(pieces):
        size = piece.shape[0]
        copies.append(pltpu.make_async_copy(piece, whole.at[pl.ds(at, size)], sems.at[i]))
        at += size
    for copy in copies:
        copy.start()
    for copy in copies:
        copy.wait()


def hidden_grad_kernel(count, w_ref, *refs):
    pieces, (out, whole_out, whole, sems, out_sem) = refs[:count], refs[count:]
    step = pl.program_id(0)

    @pl.when(step == 0)
    def _():
        load_pieces(pieces, whole, sems)
        pltpu.make_async_copy(whole, whole_out, out_sem).start()

    out[...] = contract(whole[...], w_ref[...], 1, 1)

    @pl.when(step == pl.num_programs(0) - 1)
    def _():
        pltpu.make_async_copy(whole, whole_out, out_sem).wait()


def hidden_grad(pieces, w_down):
    rows = sum(p.shape[0] for p in pieces)
    units, width = w_down.shape
    tile = 256
    return pl.pallas_call(
        functools.partial(hidden_grad_kernel, len(pieces)),
        grid=(units // tile,),
        out_shape=[jax.ShapeDtypeStruct((rows, units), F32), jax.ShapeDtypeStruct((rows, width), BF16)],
        in_specs=[pl.BlockSpec((tile, width), lambda j: (j, 0))] + [hbm()] * len(pieces),
        out_specs=[pl.BlockSpec((rows, tile), lambda j: (0, j)), hbm()],
        scratch_shapes=[
            pltpu.VMEM((rows, width), BF16),
            pltpu.SemaphoreType.DMA((len(pieces),)),
            pltpu.SemaphoreType.DMA,
        ],
        compiler_params=params(32),
        cost_estimate=pl.CostEstimate(
            flops=2 * rows * units * width, bytes_accessed=2 * units * width + 4 * rows * width, transcendentals=0
        ),
        name="hidden_grad",
    )(w_down, *pieces)


def units_kernel(count, slot, first, wg_ref, wu_ref, hg_ref, *refs):
    if not first:
        refs = refs[5:]
    pieces, (gate_out, up_out, hid_out, hs_out, whole_out, whole, gs_ref, sems, out_sem) = refs[:count], refs[count:]
    step = pl.program_id(0)
    rows, wide = whole.shape
    width = wide - LANES
    start = 0 if first else whole_out.shape[0] - rows

    @pl.when(step == 0)
    def _():
        load_pieces(pieces, whole, sems)
        pltpu.make_async_copy(whole, whole_out.at[pl.ds(start, rows)], out_sem).start()
        notes = whole[:, width:].astype(F32)
        lane = lax.broadcasted_iota(jnp.int32, notes.shape, 1) - GATES - PARTS * lax.axis_index("expert")
        gate = jnp.sum(jnp.where((lane >= 0) & (lane < PARTS), notes, 0.0), axis=1, keepdims=True)
        length, adv = notes[:, LENGTH : LENGTH + 1], notes[:, ADV : ADV + 1]
        position = lax.broadcasted_iota(jnp.int32, (rows, 1), 0) % slot
        gs_ref[...] = jnp.where(position.astype(F32) < length, gate * (adv / length), 0.0)

    x = whole[:, :width]
    gate = jnp.dot(x, wg_ref[...], preferred_element_type=F32)
    up = jnp.dot(x, wu_ref[...], preferred_element_type=F32)
    gs = gs_ref[...]
    sig = jax.nn.sigmoid(gate)
    act = gate * sig
    hid = (act * up).astype(BF16)
    hid_out[...] = hid
    hs_out[...] = (hid.astype(F32) * gs).astype(BF16)
    hg = hg_ref[...] * gs
    gate_out[...] = (hg * up * sig * (1.0 + gate * (1.0 - sig))).astype(BF16)
    up_out[...] = (hg * act).astype(BF16)

    @pl.when(step == pl.num_programs(0) - 1)
    def _():
        pltpu.make_async_copy(whole, whole_out.at[pl.ds(start, rows)], out_sem).wait()


def hidden_units(pieces, w_gate, w_up, hg, slot, before=None):
    total, units = hg.shape
    width = w_gate.shape[0]
    rows = sum(p.shape[0] for p in pieces)
    tile = 256
    at = 0 if before is None else total // rows - 1
    columns = pl.BlockSpec((rows, tile), lambda j: (at, j))
    weights = pl.BlockSpec((width, tile), lambda j: (0, j))
    before = before or []
    return pl.pallas_call(
        functools.partial(units_kernel, len(pieces), slot, not before),
        grid=(units // tile,),
        out_shape=[jax.ShapeDtypeStruct((total, units), BF16)] * 4 + [jax.ShapeDtypeStruct((total, width + LANES), BF16)],
        in_specs=[weights, weights, columns] + [hbm()] * (len(before) + len(pieces)),
        out_specs=[columns] * 4 + [hbm()],
        scratch_shapes=[
            pltpu.VMEM((rows, width + LANES), BF16),
            pltpu.VMEM((rows, 1), F32),
            pltpu.SemaphoreType.DMA((len(pieces),)),
            pltpu.SemaphoreType.DMA,
        ],
        input_output_aliases={3 + i: i for i in range(len(before))},
        compiler_params=params(48),
        cost_estimate=pl.CostEstimate(
            flops=4 * rows * units * width, bytes_accessed=4 * units * width + 4 * rows * width, transcendentals=rows * units
        ),
        name="hidden_units",
    )(w_gate, w_up, hg, *before, *pieces)


def column_grads_kernel(place_ref, x_ref, gate_ref, up_ref, other, mine):
    turned = x_ref[...].T
    gate = jnp.dot(turned, gate_ref[...], preferred_element_type=F32).astype(BF16)
    up = jnp.dot(turned, up_ref[...], preferred_element_type=F32).astype(BF16)

    @pl.when(pl.program_id(0) == 0)
    def _():
        other[0, 0] = gate
        other[0, 1] = up

    @pl.when(pl.program_id(0) == 1)
    def _():
        mine[0, 0] = gate
        mine[0, 1] = up


def column_grads(place, x, gate_grad, up_grad, n_dp, blocks):
    rows, units = gate_grad.shape
    width = x.shape[1] - LANES
    n_z, shard = n_dp // CORES, width // n_dp
    count, last = len(blocks), blocks[0]
    out = jax.ShapeDtypeStruct((count, 2, shard, units), BF16)

    def column(k, b, place):
        chip = jnp.where(place[1] == 0, last - b, n_z - 1 - (last - b))
        return 0, CORES * chip + jnp.where(k == 0, 1 - place[0], place[0])

    whole = pl.BlockSpec((rows, units), lambda k, b, place: (0, 0))
    return pl.pallas_call(
        column_grads_kernel,
        grid_spec=pltpu.PrefetchScalarGridSpec(
            num_scalar_prefetch=1,
            grid=(CORES, count),
            in_specs=[pl.BlockSpec((rows, shard), column), whole, whole],
            out_specs=[
                pl.BlockSpec((1, 2, shard, units), lambda k, b, place: (jnp.where(k == 0, b, count - 1), 0, 0, 0)),
                pl.BlockSpec((1, 2, shard, units), lambda k, b, place: (jnp.where(k == 0, 0, b), 0, 0, 0)),
            ],
        ),
        out_shape=[out, out],
        compiler_params=params(40),
        cost_estimate=pl.CostEstimate(
            flops=8 * rows * units * shard * count,
            bytes_accessed=16 * units * shard * count + 4 * rows * shard * count + 4 * rows * units,
            transcendentals=0,
        ),
        name="column_grads",
    )(place, x, gate_grad, up_grad)


def row_grad_kernel(place_ref, hid_ref, dy_ref, other, mine):
    value = contract(hid_ref[...], dy_ref[...], 0, 0).astype(BF16)
    n_z, shard, _ = mine.shape

    for z in range(n_z):
        low = value[CORES * z * shard : (CORES * z + 1) * shard]
        high = value[(CORES * z + 1) * shard : (CORES * z + 2) * shard]
        chip = jnp.where(place_ref[1] == 0, z, n_z - 1 - z)
        at = n_z - 1 - chip

        @pl.when(place_ref[0] == 0)
        def _(low=low, high=high, at=at):
            mine[at] = low
            other[at] = high

        @pl.when(place_ref[0] == 1)
        def _(low=low, high=high, at=at):
            mine[at] = high
            other[at] = low


def row_grad(place, hid, dy, n_dp):
    rows, units = hid.shape
    width = dy.shape[1]
    n_z, shard = n_dp // CORES, units // n_dp
    tile = 512
    out = jax.ShapeDtypeStruct((n_z, shard, width), BF16)
    block = pl.BlockSpec((n_z, shard, tile), lambda j, place: (0, 0, j))
    return pl.pallas_call(
        row_grad_kernel,
        grid_spec=pltpu.PrefetchScalarGridSpec(
            num_scalar_prefetch=1,
            grid=(width // tile,),
            in_specs=[
                pl.BlockSpec((rows, units), lambda j, place: (0, 0)),
                pl.BlockSpec((rows, tile), lambda j, place: (0, j)),
            ],
            out_specs=[block, block],
        ),
        out_shape=[out, out],
        compiler_params=params(32),
        cost_estimate=pl.CostEstimate(
            flops=2 * rows * units * width, bytes_accessed=2 * units * width + 2 * rows * width, transcendentals=0
        ),
        name="row_grad",
    )(place, hid, dy)


def outputs_kernel(n_ex, hid_ref, w_ref, *outs):
    value = jnp.dot(hid_ref[...], w_ref[...], preferred_element_type=F32).astype(BF16)
    size = outs[0].shape[0]
    for i in range(n_ex):
        outs[i][...] = value[i * size : (i + 1) * size]


def layer_outputs(hid, w_down, n_ex):
    rows, units = hid.shape
    width = w_down.shape[1]
    tile = 512
    size = rows // n_ex
    return pl.pallas_call(
        functools.partial(outputs_kernel, n_ex),
        grid=(width // tile,),
        out_shape=[jax.ShapeDtypeStruct((size, width), BF16)] * n_ex,
        in_specs=[pl.BlockSpec((rows, units), lambda j: (0, 0)), pl.BlockSpec((units, tile), lambda j: (0, j))],
        out_specs=[pl.BlockSpec((size, tile), lambda j: (0, j))] * n_ex,
        compiler_params=params(32),
        cost_estimate=pl.CostEstimate(
            flops=2 * rows * units * width, bytes_accessed=2 * units * width + 2 * rows * width, transcendentals=0
        ),
        name="layer_outputs",
    )(hid, w_down)


def input_grads_kernel(n_ex, gate_ref, up_ref, wg_ref, wu_ref, *outs):
    value = contract(gate_ref[...], wg_ref[...], 1, 1) + contract(up_ref[...], wu_ref[...], 1, 1)
    value = value.astype(BF16)
    size = outs[0].shape[0]
    for i in range(n_ex):
        outs[i][...] = value[i * size : (i + 1) * size]


def input_grads(gate_grad, up_grad, w_gate, w_up, n_ex):
    rows, units = gate_grad.shape
    width = w_gate.shape[0]
    tile = 512
    size = rows // n_ex
    whole = pl.BlockSpec((rows, units), lambda j: (0, 0))
    weights = pl.BlockSpec((tile, units), lambda j: (j, 0))
    return pl.pallas_call(
        functools.partial(input_grads_kernel, n_ex),
        grid=(width // tile,),
        out_shape=[jax.ShapeDtypeStruct((size, width), BF16)] * n_ex,
        in_specs=[whole, whole, weights, weights],
        out_specs=[pl.BlockSpec((size, tile), lambda j: (0, j))] * n_ex,
        compiler_params=params(40),
        cost_estimate=pl.CostEstimate(
            flops=4 * rows * units * width, bytes_accessed=4 * units * width + 2 * rows * width, transcendentals=0
        ),
        name="input_grads",
    )(gate_grad, up_grad, w_gate, w_up)


def add(*parts):
    return sum(part.astype(F32) for part in parts).astype(BF16)


def line_permute(value, link, n_dp):
    n_z = n_dp // CORES
    pairs = [(link, link + 1), (n_z - 1 - link, n_z - 2 - link)]
    return lax.ppermute(value, "dp", [(CORES * a + c, CORES * b + c) for a, b in pairs for c in range(CORES)])


def on_device(
    gen_rows, gen_lengths, gen_adv, destination, expert_ids, gate_values, cotangent, w_gate, w_up, w_down
):
    n_dp = lax.axis_size("dp")
    n_ex = lax.axis_size("expert")
    n_z = n_dp // CORES
    size = cotangent.shape[0]
    slot = gen_rows.shape[0] // destination.shape[2]
    weight_gate, weight_up, weight_down = w_gate[0], w_up[0], w_down[0]
    g, e = lax.axis_index("dp"), lax.axis_index("expert")
    z = g // CORES
    flipped = z >= n_z // 2
    place = jnp.stack([g % CORES, flipped.astype(jnp.int32)]).astype(jnp.int32)
    near = jnp.where(flipped, n_z - 1 - z, z)
    other_core = [(d, d ^ 1) for d in range(n_dp)]

    def swap_core(value):
        return lax.ppermute(value, "dp", other_core)

    cot_pieces = gather_rows(cotangent, n_ex)
    x = reassign(
        gen_rows, gen_lengths, gen_adv, destination, expert_ids, gate_values, cot_pieces[1:3], n_dp
    )
    x_pieces = gather_rows(x, n_ex)
    hg, dy_all = hidden_grad(cot_pieces, weight_down)
    early, late = with_last(x_pieces, size)
    before = hidden_units(early, weight_gate, weight_up, hg, slot)
    gate_grad, up_grad, hid, hid_scaled, x_all = hidden_units(late, weight_gate, weight_up, hg, slot, before)

    far = n_z - 1
    sums = [[None, None] for _ in range(n_z)]
    other, mine = column_grads(place, x_all, gate_grad, up_grad, n_dp, [far])
    sums[far][0] = add(mine[0], swap_core(other)[0])
    other, mine = row_grad(place, tie(hid_scaled, other), dy_all, n_dp)
    got = swap_core(other)
    for k in range(n_z):
        sums[k][1] = add(mine[far - k], got[far - k])
    rest = list(range(far - 1, -1, -1))
    other, mine = column_grads(place, tie(x_all, other), gate_grad, up_grad, n_dp, rest)
    got = swap_core(other)
    for i, k in enumerate(rest):
        sums[k][0] = add(mine[i], got[i])

    hid, gate_grad, up_grad, _, _ = lax.optimization_barrier((hid, gate_grad, up_grad, other, sums[far][0]))
    outs = layer_outputs(hid, weight_down, n_ex)
    grads = input_grads(gate_grad, up_grad, weight_gate, weight_up, n_ex)
    outs = [outs[0]] + [swap(outs[i], i, n_ex) for i in range(1, n_ex)]
    grads = [grads[0]] + [swap(tie(grads[i], outs[i]), i, n_ex) for i in range(1, n_ex)]

    passed = {}
    ends = [[], []]
    for link in range(n_z - 1):
        issued = []
        for d in range(far, link, -1):
            for p in range(2):
                value = sums[d if link < n_z // 2 else far - d][p]
                if link > 0:
                    value = add(value, passed[link - 1, d, p])
                if len(issued) >= 2:
                    value = tie(value, issued[-2])
                got = line_permute(value, link, n_dp)
                issued.append(got)
                passed[link, d, p] = got
                if d == link + 1:
                    ends[p].append(got)
    totals = []
    for p in range(2):
        own = sum(jnp.where(near == k, sums[k][p].astype(F32), 0.0) for k in range((n_z + 1) // 2))
        totals.append(add(own, *ends[p]))

    gates = [
        jnp.sum(jnp.where(expert_ids == (e ^ i), gate_values, 0.0), axis=1, keepdims=True) for i in range(n_ex)
    ]
    layer_out = sum(gates[i] * outs[i].astype(F32) for i in range(n_ex)).astype(BF16)
    input_grad = add(*grads)
    return layer_out, input_grad, totals[0][0:1], totals[0][1:2], totals[1][None]


def solution(mesh):
    rows = P(("dp", "expert"), None)
    seqs = P("dp", "expert", None)
    weights = P("expert", None, None)
    shards = P("expert", "dp", None)
    return jax.shard_map(
        on_device,
        mesh=mesh,
        in_specs=(rows, seqs, seqs, seqs, rows, rows, rows, weights, weights, weights),
        out_specs=(rows, rows, shards, shards, shards),
        check_vma=False,
    )
```

```python
import functools
import math

import jax
import jax.numpy as jnp
from jax import lax
from jax.experimental import pallas as pl
from jax.experimental.pallas import tpu as pltpu
from jax.sharding import PartitionSpec as P

CORES = 2
LANES = 128
F32 = jnp.float32
BF16 = jnp.bfloat16
MIB = 1 << 20
BIG = 24
EARLY = (1, 2, 7)


def contract(left, right, left_dim, right_dim):
    return lax.dot_general(left, right, (((left_dim,), (right_dim,)), ((), ())), preferred_element_type=F32)


def params(mib, **more):
    return pltpu.CompilerParams(vmem_limit_bytes=mib * MIB, **more)


def room(rows, width):
    return 16 + rows * width * 10 // MIB


def cost(flops, bytes_accessed):
    return pl.CostEstimate(flops=flops, bytes_accessed=bytes_accessed, transcendentals=0)


def vmem():
    return pl.BlockSpec(memory_space=pltpu.VMEM)


def in_hbm(value):
    return pltpu.with_memory_space_constraint(value, pltpu.HBM)


def hbm():
    return pl.BlockSpec(memory_space=pl.ANY)


LENGTH, ADV, GATES = 0, 1, 2
PARTS = 3


def pick_kernel(n_dp, dest_hbm, len_hbm, adv_hbm, rows_hbm, *refs):
    outs, (dest_ref, len_ref, adv_ref, sems, row_sems) = refs[:n_dp], refs[n_dp:]
    small = [
        pltpu.make_async_copy(source, target, sems.at[i])
        for i, (source, target) in enumerate(((dest_hbm, dest_ref), (len_hbm, len_ref), (adv_hbm, adv_ref)))
    ]
    for copy in small:
        copy.start()
    seqs, slot, width = rows_hbm.shape
    lane = lax.broadcasted_iota(jnp.int32, (slot, LANES), 1)
    which = lax.broadcasted_iota(jnp.int32, (1, seqs), 1)
    me = lax.axis_index("dp")
    small[0].wait()
    found, copies = [], []
    for i, out in enumerate(outs):
        seq = jnp.int32(0)
        live = jnp.int32(0)
        for s in range(seqs):
            hit = dest_ref[0, 0, s] == (me ^ i)
            seq = jnp.where(hit, s, seq)
            live = jnp.where(hit, 1, live)
        found.append((seq, live))
        copies.append(pltpu.make_async_copy(rows_hbm.at[seq], out.at[:, pl.ds(0, width)], row_sems.at[i]))
        copies[-1].start()
    small[1].wait()
    small[2].wait()
    lengths = len_ref[0].astype(F32)
    advs = adv_ref[0].astype(F32)
    for (seq, live), out in zip(found, outs):
        mine = (which == seq) & (live == 1)
        length = jnp.sum(jnp.where(mine, lengths, 0.0), axis=1, keepdims=True)
        adv = jnp.sum(jnp.where(mine, advs, 0.0), axis=1, keepdims=True)
        out[:, width:] = jnp.where(lane == LENGTH, length, jnp.where(lane == ADV, adv, 0.0)).astype(BF16)
    for copy in copies:
        copy.wait()


def pick(dest, lengths, adv, rows, n_dp):
    seqs, slot, width = rows.shape
    return pl.pallas_call(
        functools.partial(pick_kernel, n_dp),
        out_shape=[jax.ShapeDtypeStruct((slot, width + LANES), BF16)] * n_dp,
        in_specs=[hbm()] * 4,
        out_specs=[vmem()] * n_dp,
        scratch_shapes=[
            pltpu.SMEM(dest.shape, jnp.int32),
            pltpu.VMEM(lengths.shape, lengths.dtype),
            pltpu.VMEM(adv.shape, adv.dtype),
            pltpu.SemaphoreType.DMA((3,)),
            pltpu.SemaphoreType.DMA((n_dp,)),
        ],
        compiler_params=params(16),
        name="pick",
    )(*[in_hbm(value) for value in (dest, lengths, adv, rows)])


def gate_notes(ids, gates):
    note = lax.broadcasted_iota(jnp.int32, (LANES, ids.shape[1]), 0) - GATES
    expert, part = note // PARTS, note % PARTS
    value = jnp.zeros(note.shape, F32)
    for k in range(ids.shape[0]):
        value = value + jnp.where(ids[k : k + 1] == expert, gates[k : k + 1], 0.0)
    value = jnp.where(note < 0, 0.0, value)
    high = value.astype(BF16).astype(F32)
    middle = (value - high).astype(BF16).astype(F32)
    low = value - high - middle
    return jnp.where(part == 0, high, jnp.where(part == 1, middle, low))


def assemble_kernel(n_dp, ids_ref, gates_ref, *refs):
    pieces, x_ref = refs[:n_dp], refs[-1]
    slot, wide = pieces[0].shape
    width = wide - LANES
    me = lax.axis_index("dp")
    for i, piece in enumerate(pieces):
        at = pl.multiple_of((me ^ i) * slot, slot)
        x_ref[pl.ds(at, slot), :] = piece[...]
    notes = gate_notes(ids_ref[...], gates_ref[...]).T
    x_ref[:, width:] = (x_ref[:, width:].astype(F32) + notes).astype(BF16)


def assemble(pieces, ids, gates, after):
    slot, wide = pieces[0].shape
    n_dp = len(pieces)
    return pl.pallas_call(
        functools.partial(assemble_kernel, n_dp),
        out_shape=jax.ShapeDtypeStruct((slot * n_dp, wide), BF16),
        in_specs=[vmem()] * (2 + n_dp) + [hbm()] * len(after),
        out_specs=vmem(),
        compiler_params=params(16),
        name="assemble",
    )(ids, gates, *pieces, *after)


def send_sequences(gen_rows, gen_lengths, gen_adv, destination, n_dp):
    seq_dev = destination.shape[2]
    slot = gen_rows.shape[0] // seq_dev
    pieces = pick(destination, gen_lengths, gen_adv, gen_rows.reshape(seq_dev, slot, gen_rows.shape[1]), n_dp)
    return [pieces[0]] + [
        lax.ppermute(pieces[i], "dp", [(d, d ^ i) for d in range(n_dp)]) for i in range(1, n_dp)
    ]


def place_sequences(got, seq_dev, ids, gates, after):
    n_dp = len(got)
    if n_dp == seq_dev:
        return assemble(got, ids.T, gates.T, after)
    slot, wide = got[0].shape
    width = wide - LANES
    g = lax.axis_index("dp")
    stack = jnp.stack(got)[jnp.arange(n_dp, dtype=jnp.int32) ^ g]
    arrived = stack[:, 0, width + LENGTH] > 0
    arrival = jnp.cumsum(arrived.astype(jnp.int32)) - 1
    chosen = arrived[None, :] & (arrival[None, :] == jnp.arange(seq_dev, dtype=jnp.int32)[:, None])
    from_peer = jnp.sum(jnp.where(chosen, jnp.arange(n_dp, dtype=jnp.int32)[None, :], 0), axis=1)
    x = stack[from_peer].reshape(seq_dev * slot, wide)
    notes = (x[:, width:].astype(F32) + gate_notes(ids.T, gates.T).T).astype(BF16)
    return jnp.concatenate([x[:, :width], notes], axis=1)


def swap(value, i, n_ex):
    return lax.ppermute(value, "expert", [(d, d ^ i) for d in range(n_ex)])


def gather_rows(rows, n_ex, between=None):
    if n_ex != 4:
        return [rows] + [swap(rows, i, n_ex) for i in range(1, n_ex)]
    half = rows.shape[0] // 2
    first = swap(rows, 1, n_ex)
    second = swap(rows, 2, n_ex)
    low, high = first[:half], second[half:]
    if between:
        low, high, *_ = lax.optimization_barrier((low, high, *between))
    return [rows, first, second, swap(low, 2, n_ex), swap(high, 1, n_ex)]


def with_last(pieces, size):
    at, cut = 0, sum(p.shape[0] for p in pieces) - size
    for i, piece in enumerate(pieces):
        if at == cut:
            return pieces[:i], pieces[i:]
        at += piece.shape[0]


def tie(value, *others):
    return lax.optimization_barrier((value,) + others)[0]


def load_pieces(pieces, whole, sems):
    at, copies = 0, []
    for i, piece in enumerate(pieces):
        size = piece.shape[0]
        copies.append(pltpu.make_async_copy(piece, whole.at[pl.ds(at, size)], sems.at[i]))
        at += size
    for copy in copies:
        copy.start()
    for copy in copies:
        copy.wait()


def hidden_grad_kernel(count, w_ref, *refs):
    pieces, (out, whole_out, whole, sems, out_sem) = refs[:count], refs[count:]
    step = pl.program_id(0)

    @pl.when(step == 0)
    def _():
        load_pieces(pieces, whole, sems)
        pltpu.make_async_copy(whole, whole_out, out_sem).start()

    out[...] = contract(whole[...], w_ref[...], 1, 1)

    @pl.when(step == pl.num_programs(0) - 1)
    def _():
        pltpu.make_async_copy(whole, whole_out, out_sem).wait()


def hidden_grad(pieces, w_down):
    rows = sum(p.shape[0] for p in pieces)
    units, width = w_down.shape
    tile = 256
    return pl.pallas_call(
        functools.partial(hidden_grad_kernel, len(pieces)),
        grid=(units // tile,),
        out_shape=[jax.ShapeDtypeStruct((rows, units), F32), jax.ShapeDtypeStruct((rows, width), BF16)],
        in_specs=[pl.BlockSpec((tile, width), lambda j: (j, 0))] + [hbm()] * len(pieces),
        out_specs=[pl.BlockSpec((rows, tile), lambda j: (0, j)), hbm()],
        scratch_shapes=[
            pltpu.VMEM((rows, width), BF16),
            pltpu.SemaphoreType.DMA((len(pieces),)),
            pltpu.SemaphoreType.DMA,
        ],
        compiler_params=params(BIG),
        cost_estimate=cost(2 * rows * units * width, 2 * units * width + 4 * rows * width),
        name="hidden_grad",
    )(w_down, *pieces)


def shard_place(shard, n_dp):
    me = lax.axis_index("dp")
    n_z = n_dp // CORES
    chip, core = shard // CORES, shard % CORES
    at = jnp.where(me // CORES >= n_z // 2, chip, n_z - 1 - chip)
    return jnp.where(core == me % CORES, n_z, 0) + at


def units_kernel(count, slot, first, n_dp, wg_ref, wu_ref, hg_ref, *refs):
    if not first:
        refs = refs[6:]
    pieces, refs = refs[:count], refs[count:]
    gate_out, up_out, hid_out, turned_hs, turned_x, gates_out, whole, gs_ref, sems = refs
    step = pl.program_id(0)
    rows, wide = whole.shape
    width = wide - LANES

    @pl.when(step == 0)
    def _():
        load_pieces(pieces, whole, sems)
        notes = whole[:, width:].astype(F32)
        lane = lax.broadcasted_iota(jnp.int32, notes.shape, 1) - GATES - PARTS * lax.axis_index("expert")
        gates = jnp.sum(jnp.where((lane >= 0) & (lane < PARTS), notes, 0.0), axis=1, keepdims=True)
        length, adv = notes[:, LENGTH : LENGTH + 1], notes[:, ADV : ADV + 1]
        position = lax.broadcasted_iota(jnp.int32, (rows, 1), 0) % slot
        gates_out[...] = gates
        gs_ref[...] = jnp.where(position.astype(F32) < length, gates * (adv / length), 0.0)
        strip = width // n_dp
        for i in range(n_dp):
            at = pl.multiple_of(shard_place(i, n_dp) * strip, strip)
            turned_x[pl.ds(at, strip), :] = whole[:, i * strip : (i + 1) * strip].T

    x = whole[:, :width]
    gate = jnp.dot(x, wg_ref[...], preferred_element_type=F32)
    up = jnp.dot(x, wu_ref[...], preferred_element_type=F32)
    gs = gs_ref[...]
    sig = jax.nn.sigmoid(gate)
    act = gate * sig
    hid = (act * up).astype(BF16)
    hid_out[...] = hid
    turned = (hid.astype(F32) * gs).astype(BF16).T
    tile, shard = turned.shape[0], turned_hs.shape[0] // n_dp
    chunk = math.gcd(tile, shard)
    for i in range(tile // chunk):
        row = step * tile + i * chunk
        at = shard_place(row // shard, n_dp) * shard + row % shard
        turned_hs[pl.ds(pl.multiple_of(at, chunk), chunk), :] = turned[i * chunk : (i + 1) * chunk]
    hg = hg_ref[...] * gs
    gate_out[...] = (hg * up * sig * (1.0 + gate * (1.0 - sig))).astype(BF16)
    up_out[...] = (hg * act).astype(BF16)


def hidden_units(pieces, w_gate, w_up, hg, slot, n_dp, before=None):
    total, units = hg.shape
    width = w_gate.shape[0]
    rows = sum(p.shape[0] for p in pieces)
    tile = 256
    at = 0 if before is None else total // rows - 1
    columns = pl.BlockSpec((rows, tile), lambda j: (at, j))
    weights = pl.BlockSpec((width, tile), lambda j: (0, j))
    before = before or []
    return pl.pallas_call(
        functools.partial(units_kernel, len(pieces), slot, not before, n_dp),
        grid=(units // tile,),
        out_shape=[jax.ShapeDtypeStruct((total, units), BF16)] * 3
        + [
            jax.ShapeDtypeStruct((units, total), BF16),
            jax.ShapeDtypeStruct((width, total), BF16),
            jax.ShapeDtypeStruct((total, 1), F32),
        ],
        in_specs=[weights, weights, columns] + [hbm()] * (len(before) + len(pieces)),
        out_specs=[columns] * 3
        + [
            pl.BlockSpec((units, rows), lambda j: (0, at)),
            pl.BlockSpec((width, rows), lambda j: (0, at)),
            pl.BlockSpec((rows, 1), lambda j: (at, 0)),
        ],
        scratch_shapes=[
            pltpu.VMEM((rows, width + LANES), BF16),
            pltpu.VMEM((rows, 1), F32),
            pltpu.SemaphoreType.DMA((len(pieces),)),
        ],
        input_output_aliases={3 + i: i for i in range(len(before))},
        compiler_params=params(room(rows, width)),
        cost_estimate=cost(4 * rows * units * width, 4 * units * width + 4 * rows * width),
        name="hidden_units",
    )(w_gate, w_up, hg, *before, *pieces)


def far_grads_kernel(x_ref, gate_ref, up_ref, other, mine):
    gate = jnp.dot(x_ref[...], gate_ref[...], preferred_element_type=F32).astype(BF16)
    up = jnp.dot(x_ref[...], up_ref[...], preferred_element_type=F32).astype(BF16)

    @pl.when(pl.program_id(0) == 0)
    def _():
        other[0] = gate
        other[1] = up

    @pl.when(pl.program_id(0) == 1)
    def _():
        mine[0] = gate
        mine[1] = up


def far_grads(turned_x, gate_grad, up_grad, n_dp):
    rows, units = gate_grad.shape
    width = turned_x.shape[0]
    n_z, shard = n_dp // CORES, width // n_dp
    out = pl.BlockSpec((2, shard, units), lambda k: (0, 0, 0))
    whole = pl.BlockSpec((rows, units), lambda k: (0, 0))
    return pl.pallas_call(
        far_grads_kernel,
        grid=(CORES,),
        in_specs=[pl.BlockSpec((shard, rows), lambda k: (k * n_z, 0)), whole, whole],
        out_specs=[out, out],
        out_shape=[pltpu.HBM((2, shard, units), BF16)] * 2,
        compiler_params=params(BIG),
        cost_estimate=cost(8 * rows * units * shard, 16 * units * shard + 4 * rows * units),
        name="far_grads",
    )(turned_x, gate_grad, up_grad)


def rest_grads_kernel(shard, x_ref, gate_ref, up_ref, other, mine):
    count = other.shape[0]
    for k, out in enumerate((other, mine)):
        x = x_ref[pl.ds((k * (count + 1) + 1) * shard, count * shard), :]
        for p, grad in enumerate((gate_ref, up_ref)):
            value = jnp.dot(x, grad[...], preferred_element_type=F32).astype(BF16)
            for b in range(count):
                out[b, p] = value[b * shard : (b + 1) * shard]


def rest_grads(turned_x, gate_grad, up_grad, n_dp):
    rows, units = gate_grad.shape
    width = turned_x.shape[0]
    n_z, shard = n_dp // CORES, width // n_dp
    tile = 256
    columns = pl.BlockSpec((rows, tile), lambda j: (0, j))
    out = pl.BlockSpec((n_z - 1, 2, shard, tile), lambda j: (0, 0, 0, j))
    return pl.pallas_call(
        functools.partial(rest_grads_kernel, shard),
        grid=(units // tile,),
        in_specs=[pl.BlockSpec((width, rows), lambda j: (0, 0)), columns, columns],
        out_specs=[out, out],
        out_shape=[pltpu.HBM((n_z - 1, 2, shard, units), BF16)] * 2,
        compiler_params=params(room(rows, width)),
        cost_estimate=cost(4 * rows * units * width, 4 * units * width + 4 * rows * units),
        name="rest_grads",
    )(turned_x, gate_grad, up_grad)


def row_grad_kernel(hid_ref, dy_ref, other, mine):
    n_z, shard, tile = mine.shape
    value = jnp.dot(hid_ref[...], dy_ref[...], preferred_element_type=F32).astype(BF16)
    for k, out in enumerate((other, mine)):
        for b in range(n_z):
            at = (k * n_z + b) * shard
            out[b] = value[at : at + shard]


def row_grad(turned_hid, dy, n_dp):
    units, rows = turned_hid.shape
    width = dy.shape[1]
    n_z, shard = n_dp // CORES, units // n_dp
    tile = 512
    block = pl.BlockSpec((n_z, shard, tile), lambda j: (0, 0, j))
    return pl.pallas_call(
        row_grad_kernel,
        grid=(width // tile,),
        in_specs=[pl.BlockSpec((units, rows), lambda j: (0, 0)), pl.BlockSpec((rows, tile), lambda j: (0, j))],
        out_specs=[block, block],
        out_shape=[pltpu.HBM((n_z, shard, width), BF16)] * 2,
        compiler_params=params(BIG),
        cost_estimate=cost(2 * rows * units * width, 2 * units * width + 2 * rows * width),
        name="row_grad",
    )(turned_hid, dy)


def outputs_kernel(layer_groups, grad_groups, hid_ref, gates_ref, gate_ref, up_ref, wd_ref, wg_ref, wu_ref, *outs):
    layer = jnp.dot(hid_ref[...], wd_ref[...], preferred_element_type=F32) * gates_ref[...]
    value = contract(gate_ref[...], wg_ref[...], 1, 1) + contract(up_ref[...], wu_ref[...], 1, 1)
    size = outs[0].shape[1]
    for result, groups, refs in (
        (layer.astype(BF16), layer_groups, outs[: len(layer_groups)]),
        (value.astype(BF16), grad_groups, outs[len(layer_groups) :]),
    ):
        for group, out in zip(groups, refs):
            for n, i in enumerate(group):
                out[n] = result[i * size : (i + 1) * size]


def outputs(hid, gates, gate_grad, up_grad, w_down, w_gate, w_up, n_ex, layer_groups, grad_groups):
    rows, units = hid.shape
    width = w_down.shape[1]
    tile = 512
    size = rows // n_ex
    whole = pl.BlockSpec((rows, units), lambda j: (0, 0))
    columns = pl.BlockSpec((units, tile), lambda j: (0, j))
    weights = pl.BlockSpec((tile, units), lambda j: (j, 0))
    counts = [len(group) for group in layer_groups + grad_groups]
    return pl.pallas_call(
        functools.partial(outputs_kernel, layer_groups, grad_groups),
        grid=(width // tile,),
        out_shape=[jax.ShapeDtypeStruct((n, size, width), BF16) for n in counts],
        in_specs=[whole, pl.BlockSpec((rows, 1), lambda j: (0, 0)), whole, whole, columns, weights, weights],
        out_specs=[pl.BlockSpec((n, size, tile), lambda j: (0, 0, j)) for n in counts],
        compiler_params=params(room(rows, width)),
        cost_estimate=cost(6 * rows * units * width, 6 * units * width + 4 * rows * width),
        name="outputs",
    )(hid, gates, gate_grad, up_grad, w_down, w_gate, w_up)


def add(*parts):
    return sum(part.astype(F32) for part in parts).astype(BF16)


def outputs_home(hid, gates, gate_grad, up_grad, w_down, w_gate, w_up, n_ex):
    weights = (hid, gates, gate_grad, up_grad, w_down, w_gate, w_up, n_ex)
    if n_ex != 4:
        single = [[i] for i in range(n_ex)]
        parts = outputs(*weights, single, single)
        layer, grad = [], []
        for i in range(n_ex):
            layer.append(swap(parts[i][0], i, n_ex) if i else parts[i][0])
            grad.append(swap(parts[n_ex + i][0], i, n_ex) if i else parts[n_ex + i][0])
        return add(*layer), add(*grad)
    layer0, layer2, layer13, grad0, grad1, grad23 = outputs(*weights, [[0], [2], [1, 3]], [[0], [1], [2, 3]])
    layer_got = swap(layer13, 1, n_ex)
    grad_got = swap(grad23, 2, n_ex)
    layer_last = swap(add(layer2[0], layer_got[1]), 2, n_ex)
    grad_last = swap(add(grad1[0], grad_got[1]), 1, n_ex)
    return add(layer0[0], layer_got[0], layer_last), add(grad0[0], grad_got[0], grad_last)


def line_permute(value, links, n_dp):
    n_z = n_dp // CORES
    pairs = [pair for k in links for pair in ((k, k + 1), (n_z - 1 - k, n_z - 2 - k))]
    return lax.ppermute(value, "dp", [(CORES * a + c, CORES * b + c) for a, b in pairs for c in range(CORES)])


def on_device(
    gen_rows, gen_lengths, gen_adv, destination, expert_ids, gate_values, cotangent, w_gate, w_up, w_down
):
    n_dp = lax.axis_size("dp")
    n_ex = lax.axis_size("expert")
    n_z = n_dp // CORES
    size = cotangent.shape[0]
    slot = gen_rows.shape[0] // destination.shape[2]
    weight_gate, weight_up, weight_down = w_gate[0], w_up[0], w_down[0]
    g = lax.axis_index("dp")
    z = g // CORES
    near = jnp.minimum(z, n_z - 1 - z)
    other_core = [(d, d ^ 1) for d in range(n_dp)]

    def swap_core(value):
        return lax.ppermute(value, "dp", other_core)

    got = send_sequences(gen_rows, gen_lengths, gen_adv, destination, n_dp)
    cot_pieces = gather_rows(cotangent, n_ex, [got[i] for i in EARLY if i < n_dp])
    x = place_sequences(got, destination.shape[2], expert_ids, gate_values, cot_pieces[3:5])
    hg, dy_all = hidden_grad(cot_pieces, weight_down)
    x_pieces = gather_rows(x, n_ex, [hg])
    early, late = with_last(x_pieces, size)
    before = hidden_units(early, weight_gate, weight_up, hg, slot, n_dp)
    gate_grad, up_grad, hid, turned_hs, turned_x, gates = hidden_units(
        late, weight_gate, weight_up, hg, slot, n_dp, before
    )

    far = n_z - 1
    rest = list(range(far - 1, -1, -1))
    far_other, far_mine = far_grads(turned_x, gate_grad, up_grad, n_dp)
    row_other, row_mine = row_grad(tie(turned_hs, far_other), dy_all, n_dp)
    rest_other, rest_mine = rest_grads(tie(turned_x, row_other), gate_grad, up_grad, n_dp)
    far_got, row_got, rest_got = swap_core(far_other), swap_core(row_other), swap_core(rest_other)
    sums = [[None, None] for _ in range(n_z)]
    sums[far][0] = add(tie(far_mine, rest_other), far_got)
    for k in range(n_z):
        sums[k][1] = add(row_mine[far - k], row_got[far - k])
    for i, k in enumerate(rest):
        sums[k][0] = add(rest_mine[i], rest_got[i])

    passed = {}
    ends = [[], []]
    joined = n_z > 3
    at_end = near == 0

    def own(link, d, p):
        return sums[d if link < n_z // 2 else far - d][p]

    for link in range(n_z - 1 - joined):
        issued = []
        for d in range(far, link + (joined and link == 0), -1):
            for p in range(2):
                value = own(link, d, p)
                if link > 0:
                    value = add(value, passed[link - 1, d, p])
                ahead = 2 if link == 0 else 1
                if len(issued) >= ahead:
                    value = tie(value, issued[-ahead])
                got = line_permute(value, [link], n_dp)
                issued.append(got)
                passed[link, d, p] = got
                if d == link + 1:
                    ends[p].append(got)
        if link == 0:
            firsts = issued
    if joined:
        for p in range(2):
            value = jnp.where(at_end, own(0, 1, p), add(own(n_z - 2, far, p), passed[n_z - 3, far, p]))
            got = line_permute(tie(value, firsts[-2]), [0, n_z - 2], n_dp)
            firsts.append(got)
            ends[p].append(got)
    totals = []
    for p in range(2):
        mine = sum(jnp.where(near == k, sums[k][p].astype(F32), 0.0) for k in range((n_z + 1) // 2))
        mine = lax.optimization_barrier(add(mine, *ends[p][:-1]))
        totals.append(add(mine, ends[p][-1]))

    hid, gate_grad, up_grad, _ = lax.optimization_barrier((hid, gate_grad, up_grad, firsts[0]))
    layer_out, input_grad = outputs_home(
        hid, gates, gate_grad, up_grad, weight_down, weight_gate, weight_up, n_ex
    )
    return layer_out, input_grad, totals[0][0:1], totals[0][1:2], totals[1][None]


def solution(mesh):
    rows = P(("dp", "expert"), None)
    seqs = P("dp", "expert", None)
    weights = P("expert", None, None)
    shards = P("expert", "dp", None)
    return jax.shard_map(
        on_device,
        mesh=mesh,
        in_specs=(rows, seqs, seqs, seqs, rows, rows, rows, weights, weights, weights),
        out_specs=(rows, rows, shards, shards, shards),
        check_vma=False,
    )
```

```python
import functools
import math

import jax
import jax.numpy as jnp
from jax import lax
from jax.experimental import pallas as pl
from jax.experimental.pallas import tpu as pltpu
from jax.sharding import PartitionSpec as P

CORES = 2
LANES = 128
F32 = jnp.float32
BF16 = jnp.bfloat16
MIB = 1 << 20
PIECES = 1
BIG = 24


def contract(left, right, left_dim, right_dim):
    return lax.dot_general(left, right, (((left_dim,), (right_dim,)), ((), ())), preferred_element_type=F32)


def params(mib, **more):
    return pltpu.CompilerParams(vmem_limit_bytes=mib * MIB, **more)


def room(rows, width):
    return 16 + rows * width * 10 // MIB


def cost(flops, bytes_accessed):
    return pl.CostEstimate(flops=flops, bytes_accessed=bytes_accessed, transcendentals=0)


def vmem():
    return pl.BlockSpec(memory_space=pltpu.VMEM)


def in_hbm(value):
    return pltpu.with_memory_space_constraint(value, pltpu.HBM)


def hbm():
    return pl.BlockSpec(memory_space=pl.ANY)


LENGTH, ADV, GATES = 0, 1, 2
PARTS = 3


def pick_kernel(n_dp, dest_hbm, len_hbm, adv_hbm, rows_hbm, *refs):
    outs, (dest_ref, len_ref, adv_ref, sems, row_sems) = refs[:-5], refs[-5:]
    small = [
        pltpu.make_async_copy(source, target, sems.at[i])
        for i, (source, target) in enumerate(((dest_hbm, dest_ref), (len_hbm, len_ref), (adv_hbm, adv_ref)))
    ]
    for copy in small:
        copy.start()
    seqs, slot, width = rows_hbm.shape
    lane = lax.broadcasted_iota(jnp.int32, (slot, LANES), 1)
    which = lax.broadcasted_iota(jnp.int32, (1, seqs), 1)
    me = lax.axis_index("dp")
    small[0].wait()
    found, copies = [], []
    for i in range(n_dp):
        out = outs[i // CORES]
        here = pl.ds(i % CORES * slot, slot)
        seq = jnp.int32(0)
        live = jnp.int32(0)
        for s in range(seqs):
            hit = dest_ref[0, 0, s] == (me ^ i)
            seq = jnp.where(hit, s, seq)
            live = jnp.where(hit, 1, live)
        found.append((seq, live))
        copies.append(pltpu.make_async_copy(rows_hbm.at[seq], out.at[here, pl.ds(0, width)], row_sems.at[i]))
        copies[-1].start()
    small[1].wait()
    small[2].wait()
    lengths = len_ref[0].astype(F32)
    advs = adv_ref[0].astype(F32)
    for i, (seq, live) in enumerate(found):
        mine = (which == seq) & (live == 1)
        length = jnp.sum(jnp.where(mine, lengths, 0.0), axis=1, keepdims=True)
        adv = jnp.sum(jnp.where(mine, advs, 0.0), axis=1, keepdims=True)
        value = jnp.where(lane == LENGTH, length, jnp.where(lane == ADV, adv, 0.0)).astype(BF16)
        outs[i // CORES][i % CORES * slot : (i % CORES + 1) * slot, width:] = value
    for copy in copies:
        copy.wait()


def pick(dest, lengths, adv, rows, n_dp):
    seqs, slot, width = rows.shape
    return pl.pallas_call(
        functools.partial(pick_kernel, n_dp),
        out_shape=[jax.ShapeDtypeStruct((CORES * slot, width + LANES), BF16)] * (n_dp // CORES),
        in_specs=[hbm()] * 4,
        out_specs=[vmem()] * (n_dp // CORES),
        scratch_shapes=[
            pltpu.SMEM(dest.shape, jnp.int32),
            pltpu.VMEM(lengths.shape, lengths.dtype),
            pltpu.VMEM(adv.shape, adv.dtype),
            pltpu.SemaphoreType.DMA((3,)),
            pltpu.SemaphoreType.DMA((n_dp,)),
        ],
        compiler_params=params(16),
        name="pick",
    )(*[in_hbm(value) for value in (dest, lengths, adv, rows)])


def gate_notes(ids, gates):
    note = lax.broadcasted_iota(jnp.int32, (LANES, ids.shape[1]), 0) - GATES
    expert, part = note // PARTS, note % PARTS
    value = jnp.zeros(note.shape, F32)
    for k in range(ids.shape[0]):
        value = value + jnp.where(ids[k : k + 1] == expert, gates[k : k + 1], 0.0)
    value = jnp.where(note < 0, 0.0, value)
    high = value.astype(BF16).astype(F32)
    middle = (value - high).astype(BF16).astype(F32)
    low = value - high - middle
    return jnp.where(part == 0, high, jnp.where(part == 1, middle, low))


def regroup_kernel(count, *refs):
    pieces, (mine, other) = refs[:count], refs[-2:]
    slot = pieces[0].shape[0] // CORES
    for i, piece in enumerate(pieces):
        mine[i * slot : (i + 1) * slot, :] = piece[:slot]
        other[i * slot : (i + 1) * slot, :] = piece[slot:]


def regroup(pieces, after):
    rows, wide = pieces[0].shape
    count = len(pieces)
    out = jax.ShapeDtypeStruct((count * rows // CORES, wide), BF16)
    return pl.pallas_call(
        functools.partial(regroup_kernel, count),
        out_shape=[out, out],
        in_specs=[vmem()] * count + [hbm()] * len(after),
        out_specs=[vmem()] * 2,
        compiler_params=params(16),
        name="regroup",
    )(*pieces, *after)


def assemble_kernel(slot, ids_ref, gates_ref, mine, other, *halves):
    rows, wide = halves[0].shape
    width = wide - LANES
    per_half = rows // slot
    me = lax.axis_index("dp")
    notes = gate_notes(ids_ref[...], gates_ref[...]).T
    for i in range(CORES * per_half):
        piece = (mine, other)[i % CORES][i // CORES * slot : (i // CORES + 1) * slot, :]
        place = me ^ i
        at = pl.multiple_of((place % per_half) * slot, slot)
        for h, half in enumerate(halves):

            @pl.when(place // per_half == h)
            def _(piece=piece, half=half, at=at):
                half[pl.ds(at, slot), :] = piece

    for h, half in enumerate(halves):
        own = notes[h * rows : (h + 1) * rows]
        half[:, width:] = (half[:, width:].astype(F32) + own).astype(BF16)


def assemble(mine, other, slot, ids, gates):
    return pl.pallas_call(
        functools.partial(assemble_kernel, slot),
        out_shape=[jax.ShapeDtypeStruct(mine.shape, BF16)] * 2,
        in_specs=[vmem()] * 4,
        out_specs=[vmem()] * 2,
        compiler_params=params(16),
        name="assemble",
    )(ids, gates, mine, other)


def send_sequences(gen_rows, gen_lengths, gen_adv, destination, n_dp, after):
    seq_dev = destination.shape[2]
    slot = gen_rows.shape[0] // seq_dev
    pieces = list(pick(destination, gen_lengths, gen_adv, gen_rows.reshape(seq_dev, slot, gen_rows.shape[1]), n_dp))
    for i in range(1, len(pieces)):
        pieces[i] = lax.ppermute(pieces[i], "dp", [(d, d ^ (CORES * i)) for d in range(n_dp)])
    mine, other = regroup(pieces, after)
    return mine, lax.ppermute(other, "dp", [(d, d ^ 1) for d in range(n_dp)])


def place_sequences(mine, other, n_dp, seq_dev, ids, gates):
    slot = CORES * mine.shape[0] // n_dp
    if n_dp == seq_dev:
        return assemble(mine, other, slot, ids.T, gates.T)
    wide = mine.shape[1]
    width = wide - LANES
    g = lax.axis_index("dp")
    stack = jnp.stack([mine.reshape(-1, slot, wide), other.reshape(-1, slot, wide)], axis=1)
    stack = stack.reshape(n_dp, slot, wide)[jnp.arange(n_dp, dtype=jnp.int32) ^ g]
    arrived = stack[:, 0, width + LENGTH] > 0
    arrival = jnp.cumsum(arrived.astype(jnp.int32)) - 1
    chosen = arrived[None, :] & (arrival[None, :] == jnp.arange(seq_dev, dtype=jnp.int32)[:, None])
    from_peer = jnp.sum(jnp.where(chosen, jnp.arange(n_dp, dtype=jnp.int32)[None, :], 0), axis=1)
    x = stack[from_peer].reshape(seq_dev * slot, wide)
    notes = (x[:, width:].astype(F32) + gate_notes(ids.T, gates.T).T).astype(BF16)
    x = jnp.concatenate([x[:, :width], notes], axis=1)
    half = x.shape[0] // 2
    return x[:half], x[half:]


def swap(value, i, n_ex):
    return lax.ppermute(value, "expert", [(d, d ^ i) for d in range(n_ex)])


def gather_rows(rows, n_ex):
    if n_ex != 4:
        return [rows] + [swap(rows, i, n_ex) for i in range(1, n_ex)]
    half = rows.shape[0] // 2
    first = swap(rows, 1, n_ex)
    second = swap(rows, 2, n_ex)
    return [rows, first, second, swap(first[:half], 2, n_ex), swap(second[half:], 1, n_ex)]


def gather_halves(low, high, n_ex, between):
    if n_ex != 4:
        pieces = [low, high]
        for i in range(1, n_ex):
            pieces += [swap(low, i, n_ex), swap(high, i, n_ex)]
        return pieces
    first_low, second_high = swap(low, 1, n_ex), swap(high, 2, n_ex)
    first_high, second_low = swap(high, 1, n_ex), swap(low, 2, n_ex)
    on_low, on_high, _ = lax.optimization_barrier((first_low, second_high, between))
    return [low, high, first_low, first_high, second_low, second_high, swap(on_low, 2, n_ex), swap(on_high, 1, n_ex)]


def with_last(pieces, size):
    at, cut = 0, sum(p.shape[0] for p in pieces) - size
    for i, piece in enumerate(pieces):
        if at == cut:
            return pieces[:i], pieces[i:]
        at += piece.shape[0]


def tie(value, *others):
    return lax.optimization_barrier((value,) + others)[0]


def load_pieces(pieces, whole, sems):
    at, copies = 0, []
    for i, piece in enumerate(pieces):
        size = piece.shape[0]
        copies.append(pltpu.make_async_copy(piece, whole.at[pl.ds(at, size)], sems.at[i]))
        at += size
    for copy in copies:
        copy.start()
    for copy in copies:
        copy.wait()


def hidden_grad_kernel(count, w_ref, *refs):
    pieces, (out, whole_out, whole, sems, out_sem) = refs[:count], refs[count:]
    step = pl.program_id(0)

    @pl.when(step == 0)
    def _():
        load_pieces(pieces, whole, sems)
        pltpu.make_async_copy(whole, whole_out, out_sem).start()

    out[...] = contract(whole[...], w_ref[...], 1, 1)

    @pl.when(step == pl.num_programs(0) - 1)
    def _():
        pltpu.make_async_copy(whole, whole_out, out_sem).wait()


def hidden_grad(pieces, w_down):
    rows = sum(p.shape[0] for p in pieces)
    units, width = w_down.shape
    tile = 256
    return pl.pallas_call(
        functools.partial(hidden_grad_kernel, len(pieces)),
        grid=(units // tile,),
        out_shape=[jax.ShapeDtypeStruct((rows, units), F32), jax.ShapeDtypeStruct((rows, width), BF16)],
        in_specs=[pl.BlockSpec((tile, width), lambda j: (j, 0))] + [hbm()] * len(pieces),
        out_specs=[pl.BlockSpec((rows, tile), lambda j: (0, j)), hbm()],
        scratch_shapes=[
            pltpu.VMEM((rows, width), BF16),
            pltpu.SemaphoreType.DMA((len(pieces),)),
            pltpu.SemaphoreType.DMA,
        ],
        compiler_params=params(BIG),
        cost_estimate=cost(2 * rows * units * width, 2 * units * width + 4 * rows * width),
        name="hidden_grad",
    )(w_down, *pieces)


def shard_place(shard, n_dp):
    me = lax.axis_index("dp")
    n_z = n_dp // CORES
    chip, core = shard // CORES, shard % CORES
    at = jnp.where(me // CORES >= n_z // 2, chip, n_z - 1 - chip)
    return jnp.where(core == me % CORES, n_z, 0) + at


def units_kernel(count, slot, first, n_dp, wg_ref, wu_ref, hg_ref, *refs):
    if not first:
        refs = refs[6:]
    pieces, refs = refs[:count], refs[count:]
    gate_out, up_out, hid_out, turned_hs, turned_x, gates_out, whole, gs_ref, sems = refs
    step = pl.program_id(0)
    rows, wide = whole.shape
    width = wide - LANES

    @pl.when(step == 0)
    def _():
        load_pieces(pieces, whole, sems)
        notes = whole[:, width:].astype(F32)
        lane = lax.broadcasted_iota(jnp.int32, notes.shape, 1) - GATES - PARTS * lax.axis_index("expert")
        gates = jnp.sum(jnp.where((lane >= 0) & (lane < PARTS), notes, 0.0), axis=1, keepdims=True)
        length, adv = notes[:, LENGTH : LENGTH + 1], notes[:, ADV : ADV + 1]
        position = lax.broadcasted_iota(jnp.int32, (rows, 1), 0) % slot
        gates_out[...] = gates
        gs_ref[...] = jnp.where(position.astype(F32) < length, gates * (adv / length), 0.0)
        strip = width // n_dp
        for i in range(n_dp):
            at = pl.multiple_of(shard_place(i, n_dp) * strip, strip)
            turned_x[pl.ds(at, strip), :] = whole[:, i * strip : (i + 1) * strip].T

    x = whole[:, :width]
    gate = jnp.dot(x, wg_ref[...], preferred_element_type=F32)
    up = jnp.dot(x, wu_ref[...], preferred_element_type=F32)
    gs = gs_ref[...]
    sig = jax.nn.sigmoid(gate)
    act = gate * sig
    hid = (act * up).astype(BF16)
    hid_out[...] = hid
    turned = (hid.astype(F32) * gs).astype(BF16).T
    tile, shard = turned.shape[0], turned_hs.shape[0] // n_dp
    chunk = math.gcd(tile, shard)
    for i in range(tile // chunk):
        row = step * tile + i * chunk
        at = shard_place(row // shard, n_dp) * shard + row % shard
        turned_hs[pl.ds(pl.multiple_of(at, chunk), chunk), :] = turned[i * chunk : (i + 1) * chunk]
    hg = hg_ref[...] * gs
    gate_out[...] = (hg * up * sig * (1.0 + gate * (1.0 - sig))).astype(BF16)
    up_out[...] = (hg * act).astype(BF16)


def hidden_units(pieces, w_gate, w_up, hg, slot, n_dp, before=None):
    total, units = hg.shape
    width = w_gate.shape[0]
    rows = sum(p.shape[0] for p in pieces)
    tile = 256
    at = 0 if before is None else total // rows - 1
    columns = pl.BlockSpec((rows, tile), lambda j: (at, j))
    weights = pl.BlockSpec((width, tile), lambda j: (0, j))
    before = before or []
    return pl.pallas_call(
        functools.partial(units_kernel, len(pieces), slot, not before, n_dp),
        grid=(units // tile,),
        out_shape=[jax.ShapeDtypeStruct((total, units), BF16)] * 3
        + [
            jax.ShapeDtypeStruct((units, total), BF16),
            jax.ShapeDtypeStruct((width, total), BF16),
            jax.ShapeDtypeStruct((total, 1), F32),
        ],
        in_specs=[weights, weights, columns] + [hbm()] * (len(before) + len(pieces)),
        out_specs=[columns] * 3
        + [
            pl.BlockSpec((units, rows), lambda j: (0, at)),
            pl.BlockSpec((width, rows), lambda j: (0, at)),
            pl.BlockSpec((rows, 1), lambda j: (at, 0)),
        ],
        scratch_shapes=[
            pltpu.VMEM((rows, width + LANES), BF16),
            pltpu.VMEM((rows, 1), F32),
            pltpu.SemaphoreType.DMA((len(pieces),)),
        ],
        input_output_aliases={3 + i: i for i in range(len(before))},
        compiler_params=params(room(rows, width)),
        cost_estimate=cost(4 * rows * units * width, 4 * units * width + 4 * rows * width),
        name="hidden_units",
    )(w_gate, w_up, hg, *before, *pieces)


def far_grads_kernel(x_ref, gate_ref, up_ref, other, mine):
    gate = jnp.dot(x_ref[...], gate_ref[...], preferred_element_type=F32).astype(BF16)
    up = jnp.dot(x_ref[...], up_ref[...], preferred_element_type=F32).astype(BF16)

    @pl.when(pl.program_id(0) == 0)
    def _():
        other[0] = gate
        other[1] = up

    @pl.when(pl.program_id(0) == 1)
    def _():
        mine[0] = gate
        mine[1] = up


def far_grads(turned_x, gate_grad, up_grad, n_dp):
    rows, units = gate_grad.shape
    width = turned_x.shape[0]
    n_z, shard = n_dp // CORES, width // n_dp
    out = pl.BlockSpec((2, shard, units), lambda k: (0, 0, 0))
    whole = pl.BlockSpec((rows, units), lambda k: (0, 0))
    return pl.pallas_call(
        far_grads_kernel,
        grid=(CORES,),
        in_specs=[pl.BlockSpec((shard, rows), lambda k: (k * n_z, 0)), whole, whole],
        out_specs=[out, out],
        out_shape=[pltpu.HBM((2, shard, units), BF16)] * 2,
        compiler_params=params(BIG),
        cost_estimate=cost(8 * rows * units * shard, 16 * units * shard + 4 * rows * units),
        name="far_grads",
    )(turned_x, gate_grad, up_grad)


def rest_grads_kernel(shard, x_ref, gate_ref, up_ref, _, other, mine):
    count = other.shape[0]
    for k, out in enumerate((other, mine)):
        x = x_ref[pl.ds((k * (count + 1) + 1) * shard, count * shard), :]
        for p, grad in enumerate((gate_ref, up_ref)):
            value = jnp.dot(x, grad[...], preferred_element_type=F32).astype(BF16)
            for b in range(count):
                out[b, p] = value[b * shard : (b + 1) * shard]


def rest_grads(turned_x, gate_grad, up_grad, after, n_dp):
    rows, units = gate_grad.shape
    width = turned_x.shape[0]
    n_z, shard = n_dp // CORES, width // n_dp
    tile = 256
    columns = pl.BlockSpec((rows, tile), lambda j: (0, j))
    out = pl.BlockSpec((n_z - 1, 2, shard, tile), lambda j: (0, 0, 0, j))
    return pl.pallas_call(
        functools.partial(rest_grads_kernel, shard),
        grid=(units // tile,),
        in_specs=[pl.BlockSpec((width, rows), lambda j: (0, 0)), columns, columns, hbm()],
        out_specs=[out, out],
        out_shape=[pltpu.HBM((n_z - 1, 2, shard, units), BF16)] * 2,
        compiler_params=params(room(rows, width)),
        cost_estimate=cost(4 * rows * units * width, 4 * units * width + 4 * rows * units),
        name="rest_grads",
    )(turned_x, gate_grad, up_grad, after)


def row_grad_kernel(hid_ref, dy_ref, other, mine):
    n_z, shard, tile = mine.shape
    value = jnp.dot(hid_ref[...], dy_ref[...], preferred_element_type=F32).astype(BF16)
    for k, out in enumerate((other, mine)):
        for b in range(n_z):
            at = (k * n_z + b) * shard
            out[b] = value[at : at + shard]


def row_grad(turned_hid, dy, n_dp):
    units, rows = turned_hid.shape
    width = dy.shape[1]
    n_z, shard = n_dp // CORES, units // n_dp
    tile = 512
    block = pl.BlockSpec((n_z, shard, tile), lambda j: (0, 0, j))
    return pl.pallas_call(
        row_grad_kernel,
        grid=(width // tile,),
        in_specs=[pl.BlockSpec((units, rows), lambda j: (0, 0)), pl.BlockSpec((rows, tile), lambda j: (0, j))],
        out_specs=[block, block],
        out_shape=[pltpu.HBM((n_z, shard, width), BF16)] * 2,
        compiler_params=params(BIG),
        cost_estimate=cost(2 * rows * units * width, 2 * units * width + 2 * rows * width),
        name="row_grad",
    )(turned_hid, dy)


def outputs_kernel(layer_groups, grad_groups, hid_ref, gates_ref, gate_ref, up_ref, wd_ref, wg_ref, wu_ref, _, *outs):
    layer = jnp.dot(hid_ref[...], wd_ref[...], preferred_element_type=F32) * gates_ref[...]
    value = contract(gate_ref[...], wg_ref[...], 1, 1) + contract(up_ref[...], wu_ref[...], 1, 1)
    size = outs[0].shape[1]
    for result, groups, refs in (
        (layer.astype(BF16), layer_groups, outs[: len(layer_groups)]),
        (value.astype(BF16), grad_groups, outs[len(layer_groups) :]),
    ):
        for group, out in zip(groups, refs):
            for n, i in enumerate(group):
                out[n] = result[i * size : (i + 1) * size]


def outputs(hid, gates, gate_grad, up_grad, w_down, w_gate, w_up, after, n_ex, layer_groups, grad_groups):
    rows, units = hid.shape
    width = w_down.shape[1]
    tile = 512
    size = rows // n_ex
    whole = pl.BlockSpec((rows, units), lambda j: (0, 0))
    columns = pl.BlockSpec((units, tile), lambda j: (0, j))
    weights = pl.BlockSpec((tile, units), lambda j: (j, 0))
    counts = [len(group) for group in layer_groups + grad_groups]
    return pl.pallas_call(
        functools.partial(outputs_kernel, layer_groups, grad_groups),
        grid=(width // tile,),
        out_shape=[jax.ShapeDtypeStruct((n, size, width), BF16) for n in counts],
        in_specs=[whole, pl.BlockSpec((rows, 1), lambda j: (0, 0)), whole, whole, columns, weights, weights, hbm()],
        out_specs=[pl.BlockSpec((n, size, tile), lambda j: (0, 0, j)) for n in counts],
        compiler_params=params(room(rows, width)),
        cost_estimate=cost(6 * rows * units * width, 6 * units * width + 4 * rows * width),
        name="outputs",
    )(hid, gates, gate_grad, up_grad, w_down, w_gate, w_up, after)


def add(*parts):
    return sum(part.astype(F32) for part in parts).astype(BF16)


def outputs_home(hid, gates, gate_grad, up_grad, w_down, w_gate, w_up, after, n_ex):
    weights = (hid, gates, gate_grad, up_grad, w_down, w_gate, w_up, after, n_ex)
    if n_ex != 4:
        single = [[i] for i in range(n_ex)]
        parts = outputs(*weights, single, single)
        layer, grad = [], []
        for i in range(n_ex):
            layer.append(swap(parts[i][0], i, n_ex) if i else parts[i][0])
            grad.append(swap(parts[n_ex + i][0], i, n_ex) if i else parts[n_ex + i][0])
        return add(*layer), add(*grad), []
    layer0, layer2, layer13, grad0, grad1, grad23 = outputs(*weights, [[0], [2], [1, 3]], [[0], [1], [2, 3]])
    layer_got = swap(layer13, 1, n_ex)
    grad_got = swap(grad23, 2, n_ex)
    layer_last = swap(add(layer2[0], layer_got[1]), 2, n_ex)
    grad_last = swap(add(grad1[0], grad_got[1]), 1, n_ex)
    layer, grad = add(layer0[0], layer_got[0], layer_last), add(grad0[0], grad_got[0], grad_last)
    return layer, grad, [layer_last, grad_last]


def fold_kernel(gu_mine, gu_got, row_mine, row_got, *refs):
    out = refs[-1]
    step = pl.program_id(0)

    def put(mine, got):
        value = (mine.astype(F32) + got.astype(F32)).astype(BF16)
        rows, columns = value.shape
        for i in range(columns // LANES):
            out[0, i * rows : (i + 1) * rows, :] = value[:, i * LANES : (i + 1) * LANES]

    @pl.when(step < 2)
    def _():
        put(gu_mine[0, 0], gu_got[0, 0])

    @pl.when(step == 2)
    def _():
        put(row_mine[0], row_got[0])


def fold(gu_mine, gu_got, row_mine, row_got, gu_at, row_at, piece, pieces, after):
    _, _, shard, units = gu_mine.shape
    _, row_shard, width = row_mine.shape
    per = shard * units // LANES // pieces
    gu = pl.BlockSpec((1, 1, shard, units // pieces), lambda j: (gu_at, jnp.minimum(j, 1), 0, piece))
    row = pl.BlockSpec((1, row_shard, width // pieces), lambda j: (row_at, 0, piece))
    return pl.pallas_call(
        fold_kernel,
        grid=(3,),
        in_specs=[gu, gu, row, row] + [hbm()] * len(after),
        out_specs=pl.BlockSpec((1, per, LANES), lambda j: (j, 0, 0)),
        out_shape=jax.ShapeDtypeStruct((3, per, LANES), BF16),
        compiler_params=params(16),
        cost_estimate=cost(6 * per * LANES, 18 * per * LANES),
        name="fold",
    )(gu_mine, gu_got, row_mine, row_got, *after)


def pass_on_kernel(own, got, *refs):
    refs[-1][...] = (own[...].astype(F32) + got[...].astype(F32)).astype(BF16)


def pass_on(own, at, got, after):
    block = pl.BlockSpec((1,) + got.shape[1:], lambda j: (j, 0, 0))
    return pl.pallas_call(
        pass_on_kernel,
        grid=(got.shape[0],),
        in_specs=[pl.BlockSpec((1,) + got.shape[1:], lambda j: (j, at, 0)), block] + [hbm()] * len(after),
        out_specs=block,
        out_shape=jax.ShapeDtypeStruct(got.shape, BF16),
        compiler_params=params(16),
        cost_estimate=cost(2 * got.size, 6 * got.size),
        name="pass_on",
    )(own, got, *after)


def unfold_kernel(count, *refs):
    parts, outs = refs[:count], refs[count:]
    per = max(part.shape[1] for part in parts)
    total = sum(part[0].astype(F32) for part in parts if part.shape[1] == per)
    pieces = [part[0].astype(F32) for part in parts if part.shape[1] < per]
    if pieces:
        total = total + jnp.concatenate(pieces, axis=0)
    total = total.astype(BF16)
    for j, out in enumerate(outs):

        @pl.when(pl.program_id(0) == j)
        def _(out=out):
            rows, columns = out.shape[1:]
            for i in range(columns // LANES):
                out[0, :, i * LANES : (i + 1) * LANES] = total[i * rows : (i + 1) * rows]


def unfold(parts, shapes):
    return pl.pallas_call(
        functools.partial(unfold_kernel, len(parts)),
        grid=(3,),
        in_specs=[pl.BlockSpec((1,) + part.shape[1:], lambda j: (j, 0, 0)) for part in parts],
        out_specs=[pl.BlockSpec(shape, lambda j: (0, 0, 0)) for shape in shapes],
        out_shape=[jax.ShapeDtypeStruct(shape, BF16) for shape in shapes],
        compiler_params=params(24),
        cost_estimate=cost(4 * parts[0].size, 10 * parts[0].size),
        name="unfold",
    )(*parts)


def line_permute(value, link, n_dp):
    n_z = n_dp // CORES
    pairs = [(link, link + 1), (n_z - 1 - link, n_z - 2 - link)]
    return lax.ppermute(value, "dp", [(CORES * a + c, CORES * b + c) for a, b in pairs for c in range(CORES)])


def on_device(
    gen_rows, gen_lengths, gen_adv, destination, expert_ids, gate_values, cotangent, w_gate, w_up, w_down
):
    n_dp = lax.axis_size("dp")
    n_ex = lax.axis_size("expert")
    n_z = n_dp // CORES
    size = cotangent.shape[0]
    slot = gen_rows.shape[0] // destination.shape[2]
    weight_gate, weight_up, weight_down = w_gate[0], w_up[0], w_down[0]
    g = lax.axis_index("dp")
    z = g // CORES
    near = jnp.minimum(z, n_z - 1 - z)
    other_core = [(d, d ^ 1) for d in range(n_dp)]

    def swap_core(value):
        return lax.ppermute(value, "dp", other_core)

    cot_pieces = gather_rows(cotangent, n_ex)
    mine, other = send_sequences(gen_rows, gen_lengths, gen_adv, destination, n_dp, cot_pieces[1:3])
    low, high = place_sequences(mine, other, n_dp, destination.shape[2], expert_ids, gate_values)
    hg, dy_all = hidden_grad(cot_pieces, weight_down)
    x_pieces = gather_halves(low, high, n_ex, hg)
    early, late = with_last(x_pieces, size)
    before = hidden_units(early, weight_gate, weight_up, hg, slot, n_dp)
    gate_grad, up_grad, hid, turned_hs, turned_x, gates = hidden_units(
        late, weight_gate, weight_up, hg, slot, n_dp, before
    )

    far = n_z - 1
    rest = list(range(far - 1, -1, -1))
    far_other, far_mine = far_grads(turned_x, gate_grad, up_grad, n_dp)
    far_got = swap_core(far_other)
    row_other, row_mine = row_grad(tie(turned_hs, far_other), dy_all, n_dp)
    row_got = swap_core(row_other)
    rest_other, rest_mine = rest_grads(tie(turned_x, row_other), gate_grad, up_grad, far_got, n_dp)
    rest_got = swap_core(rest_other)
    far_mine, far_got = far_mine[None], far_got[None]

    def pieces(k):
        return PIECES if k == far else 1

    sums = []
    for k in range(n_z):
        gu = (far_mine, far_got) if k == far else (rest_mine, rest_got)
        at = max(far - 1 - k, 0)
        sums.append([fold(*gu, row_mine, row_got, at, far - k, p, pieces(k), []) for p in range(pieces(k))])
    passed, ends = {}, []
    for link in range(n_z - 1):
        for d in range(far, link, -1):
            for p in range(pieces(d)):
                here = sums[d if link < n_z // 2 else far - d]
                if link == 0:
                    value = here[p]
                else:
                    own, at = (here[p], 0) if len(here) == pieces(d) else (here[0], p)
                    value = pass_on(own, at, passed[link - 1, d, p], [])
                passed[link, d, p] = line_permute(value, link, n_dp)
                if d == link + 1:
                    ends.append(passed[link, d, p])
    own = sums[0][0]
    for k in range(1, (n_z + 1) // 2):
        own = jnp.where(near == k, sums[k][0], own)
    shapes = [(1, w_gate.shape[1] // n_dp, w_gate.shape[2])] * 2 + [(1, w_down.shape[1] // n_dp, w_down.shape[2])]
    totals = unfold([own] + ends, shapes)

    layer_out, input_grad, _ = outputs_home(
        hid, gates, gate_grad, up_grad, weight_down, weight_gate, weight_up, far_got, n_ex
    )
    return layer_out, input_grad, *totals


def solution(mesh):
    rows = P(("dp", "expert"), None)
    seqs = P("dp", "expert", None)
    weights = P("expert", None, None)
    shards = P("expert", "dp", None)
    return jax.shard_map(
        on_device,
        mesh=mesh,
        in_specs=(rows, seqs, seqs, seqs, rows, rows, rows, weights, weights, weights),
        out_specs=(rows, rows, shards, shards, shards),
        check_vma=False,
    )
```

```python
import functools
import math

import jax
import jax.numpy as jnp
from jax import lax
from jax.experimental import pallas as pl
from jax.experimental.pallas import tpu as pltpu
from jax.sharding import PartitionSpec as P

CORES = 2
LANES = 128
F32 = jnp.float32
BF16 = jnp.bfloat16
MIB = 1 << 20
PIECES = 1
BIG = 24


def contract(left, right, left_dim, right_dim):
    return lax.dot_general(left, right, (((left_dim,), (right_dim,)), ((), ())), preferred_element_type=F32)


def params(mib, **more):
    return pltpu.CompilerParams(vmem_limit_bytes=mib * MIB, **more)


def room(rows, width):
    return 16 + rows * width * 10 // MIB


def cost(flops, bytes_accessed):
    return pl.CostEstimate(flops=flops, bytes_accessed=bytes_accessed, transcendentals=0)


def vmem():
    return pl.BlockSpec(memory_space=pltpu.VMEM)


def in_hbm(value):
    return pltpu.with_memory_space_constraint(value, pltpu.HBM)


def hbm():
    return pl.BlockSpec(memory_space=pl.ANY)


LENGTH, ADV, GATES = 0, 1, 2
PARTS = 3


def pick_kernel(n_dp, dest_hbm, len_hbm, adv_hbm, rows_hbm, *refs):
    outs, (dest_ref, len_ref, adv_ref, sems, row_sems) = refs[:-5], refs[-5:]
    small = [
        pltpu.make_async_copy(source, target, sems.at[i])
        for i, (source, target) in enumerate(((dest_hbm, dest_ref), (len_hbm, len_ref), (adv_hbm, adv_ref)))
    ]
    for copy in small:
        copy.start()
    seqs, slot, width = rows_hbm.shape
    lane = lax.broadcasted_iota(jnp.int32, (slot, LANES), 1)
    which = lax.broadcasted_iota(jnp.int32, (1, seqs), 1)
    me = lax.axis_index("dp")
    small[0].wait()
    found, copies = [], []
    for i in range(n_dp):
        out = outs[i // CORES]
        here = pl.ds(i % CORES * slot, slot)
        seq = jnp.int32(0)
        live = jnp.int32(0)
        for s in range(seqs):
            hit = dest_ref[0, 0, s] == (me ^ i)
            seq = jnp.where(hit, s, seq)
            live = jnp.where(hit, 1, live)
        found.append((seq, live))
        copies.append(pltpu.make_async_copy(rows_hbm.at[seq], out.at[here, pl.ds(0, width)], row_sems.at[i]))
        copies[-1].start()
    small[1].wait()
    small[2].wait()
    lengths = len_ref[0].astype(F32)
    advs = adv_ref[0].astype(F32)
    for i, (seq, live) in enumerate(found):
        mine = (which == seq) & (live == 1)
        length = jnp.sum(jnp.where(mine, lengths, 0.0), axis=1, keepdims=True)
        adv = jnp.sum(jnp.where(mine, advs, 0.0), axis=1, keepdims=True)
        value = jnp.where(lane == LENGTH, length, jnp.where(lane == ADV, adv, 0.0)).astype(BF16)
        outs[i // CORES][i % CORES * slot : (i % CORES + 1) * slot, width:] = value
    for copy in copies:
        copy.wait()


def pick(dest, lengths, adv, rows, n_dp):
    seqs, slot, width = rows.shape
    return pl.pallas_call(
        functools.partial(pick_kernel, n_dp),
        out_shape=[jax.ShapeDtypeStruct((CORES * slot, width + LANES), BF16)] * (n_dp // CORES),
        in_specs=[hbm()] * 4,
        out_specs=[vmem()] * (n_dp // CORES),
        scratch_shapes=[
            pltpu.SMEM(dest.shape, jnp.int32),
            pltpu.VMEM(lengths.shape, lengths.dtype),
            pltpu.VMEM(adv.shape, adv.dtype),
            pltpu.SemaphoreType.DMA((3,)),
            pltpu.SemaphoreType.DMA((n_dp,)),
        ],
        compiler_params=params(16),
        name="pick",
    )(*[in_hbm(value) for value in (dest, lengths, adv, rows)])


def gate_notes(ids, gates):
    note = lax.broadcasted_iota(jnp.int32, (LANES, ids.shape[1]), 0) - GATES
    expert, part = note // PARTS, note % PARTS
    value = jnp.zeros(note.shape, F32)
    for k in range(ids.shape[0]):
        value = value + jnp.where(ids[k : k + 1] == expert, gates[k : k + 1], 0.0)
    value = jnp.where(note < 0, 0.0, value)
    high = value.astype(BF16).astype(F32)
    middle = (value - high).astype(BF16).astype(F32)
    low = value - high - middle
    return jnp.where(part == 0, high, jnp.where(part == 1, middle, low))


def regroup_kernel(count, *refs):
    pieces, (mine, other) = refs[:count], refs[-2:]
    slot = pieces[0].shape[0] // CORES
    for i, piece in enumerate(pieces):
        mine[i * slot : (i + 1) * slot, :] = piece[:slot]
        other[i * slot : (i + 1) * slot, :] = piece[slot:]


def regroup(pieces, after):
    rows, wide = pieces[0].shape
    count = len(pieces)
    out = jax.ShapeDtypeStruct((count * rows // CORES, wide), BF16)
    return pl.pallas_call(
        functools.partial(regroup_kernel, count),
        out_shape=[out, out],
        in_specs=[vmem()] * count + [hbm()] * len(after),
        out_specs=[vmem()] * 2,
        compiler_params=params(16),
        name="regroup",
    )(*pieces, *after)


def assemble_kernel(slot, ids_ref, gates_ref, mine, other, *halves):
    rows, wide = halves[0].shape
    width = wide - LANES
    per_half = rows // slot
    me = lax.axis_index("dp")
    notes = gate_notes(ids_ref[...], gates_ref[...]).T
    for i in range(CORES * per_half):
        piece = (mine, other)[i % CORES][i // CORES * slot : (i // CORES + 1) * slot, :]
        place = me ^ i
        at = pl.multiple_of((place % per_half) * slot, slot)
        for h, half in enumerate(halves):

            @pl.when(place // per_half == h)
            def _(piece=piece, half=half, at=at):
                half[pl.ds(at, slot), :] = piece

    for h, half in enumerate(halves):
        own = notes[h * rows : (h + 1) * rows]
        half[:, width:] = (half[:, width:].astype(F32) + own).astype(BF16)


def assemble(mine, other, slot, ids, gates):
    return pl.pallas_call(
        functools.partial(assemble_kernel, slot),
        out_shape=[jax.ShapeDtypeStruct(mine.shape, BF16)] * 2,
        in_specs=[vmem()] * 4,
        out_specs=[vmem()] * 2,
        compiler_params=params(16),
        name="assemble",
    )(ids, gates, mine, other)


def send_sequences(gen_rows, gen_lengths, gen_adv, destination, n_dp, after):
    seq_dev = destination.shape[2]
    slot = gen_rows.shape[0] // seq_dev
    pieces = list(pick(destination, gen_lengths, gen_adv, gen_rows.reshape(seq_dev, slot, gen_rows.shape[1]), n_dp))
    for i in range(1, len(pieces)):
        pieces[i] = lax.ppermute(pieces[i], "dp", [(d, d ^ (CORES * i)) for d in range(n_dp)])
    mine, other = regroup(pieces, after)
    return mine, lax.ppermute(other, "dp", [(d, d ^ 1) for d in range(n_dp)])


def place_sequences(mine, other, n_dp, seq_dev, ids, gates):
    slot = CORES * mine.shape[0] // n_dp
    if n_dp == seq_dev:
        return assemble(mine, other, slot, ids.T, gates.T)
    wide = mine.shape[1]
    width = wide - LANES
    g = lax.axis_index("dp")
    stack = jnp.stack([mine.reshape(-1, slot, wide), other.reshape(-1, slot, wide)], axis=1)
    stack = stack.reshape(n_dp, slot, wide)[jnp.arange(n_dp, dtype=jnp.int32) ^ g]
    arrived = stack[:, 0, width + LENGTH] > 0
    arrival = jnp.cumsum(arrived.astype(jnp.int32)) - 1
    chosen = arrived[None, :] & (arrival[None, :] == jnp.arange(seq_dev, dtype=jnp.int32)[:, None])
    from_peer = jnp.sum(jnp.where(chosen, jnp.arange(n_dp, dtype=jnp.int32)[None, :], 0), axis=1)
    x = stack[from_peer].reshape(seq_dev * slot, wide)
    notes = (x[:, width:].astype(F32) + gate_notes(ids.T, gates.T).T).astype(BF16)
    x = jnp.concatenate([x[:, :width], notes], axis=1)
    half = x.shape[0] // 2
    return x[:half], x[half:]


def swap(value, i, n_ex):
    return lax.ppermute(value, "expert", [(d, d ^ i) for d in range(n_ex)])


def gather_rows(rows, n_ex):
    if n_ex != 4:
        return [rows] + [swap(rows, i, n_ex) for i in range(1, n_ex)]
    half = rows.shape[0] // 2
    first = swap(rows, 1, n_ex)
    second = swap(rows, 2, n_ex)
    return [rows, first, second, swap(first[:half], 2, n_ex), swap(second[half:], 1, n_ex)]


def gather_halves(low, high, n_ex, between):
    if n_ex != 4:
        pieces = [low, high]
        for i in range(1, n_ex):
            pieces += [swap(low, i, n_ex), swap(high, i, n_ex)]
        return pieces
    first_low, second_high = swap(low, 1, n_ex), swap(high, 2, n_ex)
    first_high, second_low = swap(high, 1, n_ex), swap(low, 2, n_ex)
    on_low, on_high, _ = lax.optimization_barrier((first_low, second_high, between))
    return [low, high, first_low, first_high, second_low, second_high, swap(on_low, 2, n_ex), swap(on_high, 1, n_ex)]


def with_last(pieces, size):
    at, cut = 0, sum(p.shape[0] for p in pieces) - size
    for i, piece in enumerate(pieces):
        if at == cut:
            return pieces[:i], pieces[i:]
        at += piece.shape[0]


def tie(value, *others):
    return lax.optimization_barrier((value,) + others)[0]


def load_pieces(pieces, whole, sems):
    at, copies = 0, []
    for i, piece in enumerate(pieces):
        size = piece.shape[0]
        copies.append(pltpu.make_async_copy(piece, whole.at[pl.ds(at, size)], sems.at[i]))
        at += size
    for copy in copies:
        copy.start()
    for copy in copies:
        copy.wait()


def hidden_grad_kernel(count, w_ref, *refs):
    pieces, (out, whole_out, whole, sems, out_sem) = refs[:count], refs[count:]
    step = pl.program_id(0)

    @pl.when(step == 0)
    def _():
        load_pieces(pieces, whole, sems)
        pltpu.make_async_copy(whole, whole_out, out_sem).start()

    out[...] = contract(whole[...], w_ref[...], 1, 1)

    @pl.when(step == pl.num_programs(0) - 1)
    def _():
        pltpu.make_async_copy(whole, whole_out, out_sem).wait()


def hidden_grad(pieces, w_down):
    rows = sum(p.shape[0] for p in pieces)
    units, width = w_down.shape
    tile = 256
    return pl.pallas_call(
        functools.partial(hidden_grad_kernel, len(pieces)),
        grid=(units // tile,),
        out_shape=[jax.ShapeDtypeStruct((rows, units), F32), jax.ShapeDtypeStruct((rows, width), BF16)],
        in_specs=[pl.BlockSpec((tile, width), lambda j: (j, 0))] + [hbm()] * len(pieces),
        out_specs=[pl.BlockSpec((rows, tile), lambda j: (0, j)), hbm()],
        scratch_shapes=[
            pltpu.VMEM((rows, width), BF16),
            pltpu.SemaphoreType.DMA((len(pieces),)),
            pltpu.SemaphoreType.DMA,
        ],
        compiler_params=params(BIG),
        cost_estimate=cost(2 * rows * units * width, 2 * units * width + 4 * rows * width),
        name="hidden_grad",
    )(w_down, *pieces)


def shard_place(shard, n_dp):
    me = lax.axis_index("dp")
    n_z = n_dp // CORES
    chip, core = shard // CORES, shard % CORES
    at = jnp.where(me // CORES >= n_z // 2, chip, n_z - 1 - chip)
    return jnp.where(core == me % CORES, n_z, 0) + at


def units_kernel(count, slot, first, n_dp, wg_ref, wu_ref, hg_ref, *refs):
    if not first:
        refs = refs[6:]
    pieces, refs = refs[:count], refs[count:]
    gate_out, up_out, hid_out, turned_hs, turned_x, gates_out, whole, gs_ref, sems = refs
    step = pl.program_id(0)
    rows, wide = whole.shape
    width = wide - LANES

    @pl.when(step == 0)
    def _():
        load_pieces(pieces, whole, sems)
        notes = whole[:, width:].astype(F32)
        lane = lax.broadcasted_iota(jnp.int32, notes.shape, 1) - GATES - PARTS * lax.axis_index("expert")
        gates = jnp.sum(jnp.where((lane >= 0) & (lane < PARTS), notes, 0.0), axis=1, keepdims=True)
        length, adv = notes[:, LENGTH : LENGTH + 1], notes[:, ADV : ADV + 1]
        position = lax.broadcasted_iota(jnp.int32, (rows, 1), 0) % slot
        gates_out[...] = gates
        gs_ref[...] = jnp.where(position.astype(F32) < length, gates * (adv / length), 0.0)
        strip = width // n_dp
        for i in range(n_dp):
            at = pl.multiple_of(shard_place(i, n_dp) * strip, strip)
            turned_x[pl.ds(at, strip), :] = whole[:, i * strip : (i + 1) * strip].T

    x = whole[:, :width]
    gate = jnp.dot(x, wg_ref[...], preferred_element_type=F32)
    up = jnp.dot(x, wu_ref[...], preferred_element_type=F32)
    gs = gs_ref[...]
    sig = jax.nn.sigmoid(gate)
    act = gate * sig
    hid = (act * up).astype(BF16)
    hid_out[...] = hid
    turned = (hid.astype(F32) * gs).astype(BF16).T
    tile, shard = turned.shape[0], turned_hs.shape[0] // n_dp
    chunk = math.gcd(tile, shard)
    for i in range(tile // chunk):
        row = step * tile + i * chunk
        at = shard_place(row // shard, n_dp) * shard + row % shard
        turned_hs[pl.ds(pl.multiple_of(at, chunk), chunk), :] = turned[i * chunk : (i + 1) * chunk]
    hg = hg_ref[...] * gs
    gate_out[...] = (hg * up * sig * (1.0 + gate * (1.0 - sig))).astype(BF16)
    up_out[...] = (hg * act).astype(BF16)


def hidden_units(pieces, w_gate, w_up, hg, slot, n_dp, before=None):
    total, units = hg.shape
    width = w_gate.shape[0]
    rows = sum(p.shape[0] for p in pieces)
    tile = 256
    at = 0 if before is None else total // rows - 1
    columns = pl.BlockSpec((rows, tile), lambda j: (at, j))
    weights = pl.BlockSpec((width, tile), lambda j: (0, j))
    before = before or []
    return pl.pallas_call(
        functools.partial(units_kernel, len(pieces), slot, not before, n_dp),
        grid=(units // tile,),
        out_shape=[jax.ShapeDtypeStruct((total, units), BF16)] * 3
        + [
            jax.ShapeDtypeStruct((units, total), BF16),
            jax.ShapeDtypeStruct((width, total), BF16),
            jax.ShapeDtypeStruct((total, 1), F32),
        ],
        in_specs=[weights, weights, columns] + [hbm()] * (len(before) + len(pieces)),
        out_specs=[columns] * 3
        + [
            pl.BlockSpec((units, rows), lambda j: (0, at)),
            pl.BlockSpec((width, rows), lambda j: (0, at)),
            pl.BlockSpec((rows, 1), lambda j: (at, 0)),
        ],
        scratch_shapes=[
            pltpu.VMEM((rows, width + LANES), BF16),
            pltpu.VMEM((rows, 1), F32),
            pltpu.SemaphoreType.DMA((len(pieces),)),
        ],
        input_output_aliases={3 + i: i for i in range(len(before))},
        compiler_params=params(room(rows, width)),
        cost_estimate=cost(4 * rows * units * width, 4 * units * width + 4 * rows * width),
        name="hidden_units",
    )(w_gate, w_up, hg, *before, *pieces)


def far_grads_kernel(x_ref, gate_ref, up_ref, other, mine):
    gate = jnp.dot(x_ref[...], gate_ref[...], preferred_element_type=F32).astype(BF16)
    up = jnp.dot(x_ref[...], up_ref[...], preferred_element_type=F32).astype(BF16)

    @pl.when(pl.program_id(0) == 0)
    def _():
        other[0] = gate
        other[1] = up

    @pl.when(pl.program_id(0) == 1)
    def _():
        mine[0] = gate
        mine[1] = up


def far_grads(turned_x, gate_grad, up_grad, n_dp):
    rows, units = gate_grad.shape
    width = turned_x.shape[0]
    n_z, shard = n_dp // CORES, width // n_dp
    out = pl.BlockSpec((2, shard, units), lambda k: (0, 0, 0))
    whole = pl.BlockSpec((rows, units), lambda k: (0, 0))
    return pl.pallas_call(
        far_grads_kernel,
        grid=(CORES,),
        in_specs=[pl.BlockSpec((shard, rows), lambda k: (k * n_z, 0)), whole, whole],
        out_specs=[out, out],
        out_shape=[pltpu.HBM((2, shard, units), BF16)] * 2,
        compiler_params=params(BIG),
        cost_estimate=cost(8 * rows * units * shard, 16 * units * shard + 4 * rows * units),
        name="far_grads",
    )(turned_x, gate_grad, up_grad)


def rest_grads_kernel(shard, x_ref, gate_ref, up_ref, _, other, mine):
    count = other.shape[0]
    for k, out in enumerate((other, mine)):
        x = x_ref[pl.ds((k * (count + 1) + 1) * shard, count * shard), :]
        for p, grad in enumerate((gate_ref, up_ref)):
            value = jnp.dot(x, grad[...], preferred_element_type=F32).astype(BF16)
            for b in range(count):
                out[b, p] = value[b * shard : (b + 1) * shard]


def rest_grads(turned_x, gate_grad, up_grad, after, n_dp):
    rows, units = gate_grad.shape
    width = turned_x.shape[0]
    n_z, shard = n_dp // CORES, width // n_dp
    tile = 256
    columns = pl.BlockSpec((rows, tile), lambda j: (0, j))
    out = pl.BlockSpec((n_z - 1, 2, shard, tile), lambda j: (0, 0, 0, j))
    return pl.pallas_call(
        functools.partial(rest_grads_kernel, shard),
        grid=(units // tile,),
        in_specs=[pl.BlockSpec((width, rows), lambda j: (0, 0)), columns, columns, hbm()],
        out_specs=[out, out],
        out_shape=[pltpu.HBM((n_z - 1, 2, shard, units), BF16)] * 2,
        compiler_params=params(room(rows, width)),
        cost_estimate=cost(4 * rows * units * width, 4 * units * width + 4 * rows * units),
        name="rest_grads",
    )(turned_x, gate_grad, up_grad, after)


def row_grad_kernel(hid_ref, dy_ref, other, mine):
    n_z, shard, tile = mine.shape
    value = jnp.dot(hid_ref[...], dy_ref[...], preferred_element_type=F32).astype(BF16)
    for k, out in enumerate((other, mine)):
        for b in range(n_z):
            at = (k * n_z + b) * shard
            out[b] = value[at : at + shard]


def row_grad(turned_hid, dy, n_dp):
    units, rows = turned_hid.shape
    width = dy.shape[1]
    n_z, shard = n_dp // CORES, units // n_dp
    tile = 512
    block = pl.BlockSpec((n_z, shard, tile), lambda j: (0, 0, j))
    return pl.pallas_call(
        row_grad_kernel,
        grid=(width // tile,),
        in_specs=[pl.BlockSpec((units, rows), lambda j: (0, 0)), pl.BlockSpec((rows, tile), lambda j: (0, j))],
        out_specs=[block, block],
        out_shape=[pltpu.HBM((n_z, shard, width), BF16)] * 2,
        compiler_params=params(BIG),
        cost_estimate=cost(2 * rows * units * width, 2 * units * width + 2 * rows * width),
        name="row_grad",
    )(turned_hid, dy)


def outputs_kernel(layer_groups, grad_groups, hid_ref, gates_ref, gate_ref, up_ref, wd_ref, wg_ref, wu_ref, _, *outs):
    layer = jnp.dot(hid_ref[...], wd_ref[...], preferred_element_type=F32) * gates_ref[...]
    value = contract(gate_ref[...], wg_ref[...], 1, 1) + contract(up_ref[...], wu_ref[...], 1, 1)
    size = outs[0].shape[1]
    for result, groups, refs in (
        (layer.astype(BF16), layer_groups, outs[: len(layer_groups)]),
        (value.astype(BF16), grad_groups, outs[len(layer_groups) :]),
    ):
        for group, out in zip(groups, refs):
            for n, i in enumerate(group):
                out[n] = result[i * size : (i + 1) * size]


def outputs(hid, gates, gate_grad, up_grad, w_down, w_gate, w_up, after, n_ex, layer_groups, grad_groups):
    rows, units = hid.shape
    width = w_down.shape[1]
    tile = 512
    size = rows // n_ex
    whole = pl.BlockSpec((rows, units), lambda j: (0, 0))
    columns = pl.BlockSpec((units, tile), lambda j: (0, j))
    weights = pl.BlockSpec((tile, units), lambda j: (j, 0))
    counts = [len(group) for group in layer_groups + grad_groups]
    return pl.pallas_call(
        functools.partial(outputs_kernel, layer_groups, grad_groups),
        grid=(width // tile,),
        out_shape=[jax.ShapeDtypeStruct((n, size, width), BF16) for n in counts],
        in_specs=[whole, pl.BlockSpec((rows, 1), lambda j: (0, 0)), whole, whole, columns, weights, weights, hbm()],
        out_specs=[pl.BlockSpec((n, size, tile), lambda j: (0, 0, j)) for n in counts],
        compiler_params=params(room(rows, width)),
        cost_estimate=cost(6 * rows * units * width, 6 * units * width + 4 * rows * width),
        name="outputs",
    )(hid, gates, gate_grad, up_grad, w_down, w_gate, w_up, after)


def add(*parts):
    return sum(part.astype(F32) for part in parts).astype(BF16)


def outputs_home(hid, gates, gate_grad, up_grad, w_down, w_gate, w_up, after, n_ex):
    weights = (hid, gates, gate_grad, up_grad, w_down, w_gate, w_up, after, n_ex)
    if n_ex != 4:
        single = [[i] for i in range(n_ex)]
        parts = outputs(*weights, single, single)
        layer, grad = [], []
        for i in range(n_ex):
            layer.append(swap(parts[i][0], i, n_ex) if i else parts[i][0])
            grad.append(swap(parts[n_ex + i][0], i, n_ex) if i else parts[n_ex + i][0])
        return add(*layer), add(*grad), []
    layer0, layer2, layer13, grad0, grad1, grad23 = outputs(*weights, [[0], [2], [1, 3]], [[0], [1], [2, 3]])
    layer_got = swap(layer13, 1, n_ex)
    grad_got = swap(grad23, 2, n_ex)
    layer_last = swap(add(layer2[0], layer_got[1]), 2, n_ex)
    grad_last = swap(add(grad1[0], grad_got[1]), 1, n_ex)
    layer, grad = add(layer0[0], layer_got[0], layer_last), add(grad0[0], grad_got[0], grad_last)
    return layer, grad, [layer_last, grad_last]


def fold_kernel(gu_mine, gu_got, row_mine, row_got, *refs):
    out = refs[-1]
    step = pl.program_id(0)

    def put(mine, got):
        value = (mine.astype(F32) + got.astype(F32)).astype(BF16)
        rows, columns = value.shape
        for i in range(columns // LANES):
            out[0, i * rows : (i + 1) * rows, :] = value[:, i * LANES : (i + 1) * LANES]

    @pl.when(step < 2)
    def _():
        put(gu_mine[0, 0], gu_got[0, 0])

    @pl.when(step == 2)
    def _():
        put(row_mine[0], row_got[0])


def fold(gu_mine, gu_got, row_mine, row_got, gu_at, row_at, piece, pieces, after):
    _, _, shard, units = gu_mine.shape
    _, row_shard, width = row_mine.shape
    per = shard * units // LANES // pieces
    gu = pl.BlockSpec((1, 1, shard, units // pieces), lambda j: (gu_at, jnp.minimum(j, 1), 0, piece))
    row = pl.BlockSpec((1, row_shard, width // pieces), lambda j: (row_at, 0, piece))
    return pl.pallas_call(
        fold_kernel,
        grid=(3,),
        in_specs=[gu, gu, row, row] + [hbm()] * len(after),
        out_specs=pl.BlockSpec((1, per, LANES), lambda j: (j, 0, 0)),
        out_shape=jax.ShapeDtypeStruct((3, per, LANES), BF16),
        compiler_params=params(16),
        cost_estimate=cost(6 * per * LANES, 18 * per * LANES),
        name="fold",
    )(gu_mine, gu_got, row_mine, row_got, *after)


def pass_on_kernel(own, got, *refs):
    refs[-1][...] = (own[...].astype(F32) + got[...].astype(F32)).astype(BF16)


def pass_on(own, got, piece, pieces, whole, after):
    per = whole // pieces

    def part(array):
        at = piece if array.shape[1] > per else 0
        return pl.BlockSpec((1, per, LANES), lambda j: (j, at, 0))

    return pl.pallas_call(
        pass_on_kernel,
        grid=(got.shape[0],),
        in_specs=[part(own), part(got)] + [hbm()] * len(after),
        out_specs=pl.BlockSpec((1, per, LANES), lambda j: (j, 0, 0)),
        out_shape=jax.ShapeDtypeStruct((got.shape[0], per, LANES), BF16),
        compiler_params=params(16),
        cost_estimate=cost(2 * got.size, 6 * got.size),
        name="pass_on",
    )(own, got, *after)


def choose_kernel(place_ref, one, other, *refs):
    refs[-1][...] = jnp.where(place_ref[0] > 0, one[...].astype(F32), other[...].astype(F32)).astype(BF16)


def choose(place, one, other, after):
    block = pl.BlockSpec((1,) + one.shape[1:], lambda j, place: (j, 0, 0))
    return pl.pallas_call(
        choose_kernel,
        grid_spec=pltpu.PrefetchScalarGridSpec(
            num_scalar_prefetch=1,
            grid=(one.shape[0],),
            in_specs=[block, block] + [hbm()] * len(after),
            out_specs=block,
        ),
        out_shape=jax.ShapeDtypeStruct(one.shape, BF16),
        compiler_params=params(16),
        cost_estimate=cost(one.size, 6 * one.size),
        name="choose",
    )(place.reshape(1).astype(jnp.int32), one, other, *after)


def unfold_kernel(counts, *refs):
    parts, outs = refs[: sum(counts)], refs[sum(counts) :]
    total, at = None, 0
    for count in counts:
        pieces = [part[0].astype(F32) for part in parts[at : at + count]]
        value = pieces[0] if count == 1 else jnp.concatenate(pieces, axis=0)
        total = value if total is None else total + value
        at += count
    total = total.astype(BF16)
    for j, out in enumerate(outs):

        @pl.when(pl.program_id(0) == j)
        def _(out=out):
            rows, columns = out.shape[1:]
            for i in range(columns // LANES):
                out[0, :, i * LANES : (i + 1) * LANES] = total[i * rows : (i + 1) * rows]


def unfold(groups, shapes):
    parts = [part for group in groups for part in group]
    return pl.pallas_call(
        functools.partial(unfold_kernel, [len(group) for group in groups]),
        grid=(3,),
        in_specs=[pl.BlockSpec((1,) + part.shape[1:], lambda j: (j, 0, 0)) for part in parts],
        out_specs=[pl.BlockSpec(shape, lambda j: (0, 0, 0)) for shape in shapes],
        out_shape=[jax.ShapeDtypeStruct(shape, BF16) for shape in shapes],
        compiler_params=params(24),
        cost_estimate=cost(4 * parts[0].size, 10 * parts[0].size),
        name="unfold",
    )(*parts)


def chips_permute(value, pairs, n_dp):
    return lax.ppermute(value, "dp", [(CORES * a + c, CORES * b + c) for a, b in pairs for c in range(CORES)])


def on_device(
    gen_rows, gen_lengths, gen_adv, destination, expert_ids, gate_values, cotangent, w_gate, w_up, w_down
):
    n_dp = lax.axis_size("dp")
    n_ex = lax.axis_size("expert")
    n_z = n_dp // CORES
    size = cotangent.shape[0]
    slot = gen_rows.shape[0] // destination.shape[2]
    weight_gate, weight_up, weight_down = w_gate[0], w_up[0], w_down[0]
    g = lax.axis_index("dp")
    z = g // CORES
    near = jnp.minimum(z, n_z - 1 - z)
    other_core = [(d, d ^ 1) for d in range(n_dp)]

    def swap_core(value):
        return lax.ppermute(value, "dp", other_core)

    cot_pieces = gather_rows(cotangent, n_ex)
    mine, other = send_sequences(gen_rows, gen_lengths, gen_adv, destination, n_dp, cot_pieces[1:3])
    low, high = place_sequences(mine, other, n_dp, destination.shape[2], expert_ids, gate_values)
    hg, dy_all = hidden_grad(cot_pieces, weight_down)
    x_pieces = gather_halves(low, high, n_ex, hg)
    early, late = with_last(x_pieces, size)
    before = hidden_units(early, weight_gate, weight_up, hg, slot, n_dp)
    gate_grad, up_grad, hid, turned_hs, turned_x, gates = hidden_units(
        late, weight_gate, weight_up, hg, slot, n_dp, before
    )

    far = n_z - 1
    rest = list(range(far - 1, -1, -1))
    far_other, far_mine = far_grads(turned_x, gate_grad, up_grad, n_dp)
    far_got = swap_core(far_other)
    row_other, row_mine = row_grad(tie(turned_hs, far_other), dy_all, n_dp)
    row_got = swap_core(row_other)
    whole = w_gate.shape[1] * w_gate.shape[2] // n_dp // LANES
    far_sum = fold(far_mine[None], far_got[None], row_mine, row_got, 0, 0, 0, 1, [])
    rest_other, rest_mine = rest_grads(turned_x, gate_grad, up_grad, far_got, n_dp)
    rest_got = swap_core(rest_other)

    def block(k, *after):
        return fold(rest_mine, rest_got, row_mine, row_got, far - 1 - k, far - k, 0, 1, after)

    if n_z == 4:
        outward, across = [(0, 1), (3, 2)], [(0, 1), (1, 0), (2, 3), (3, 2)]
        three = chips_permute(far_sum, outward, n_dp)
        sum_two = block(2)
        two = chips_permute(sum_two, outward, n_dp)
        sum_one, sum_none = block(1), block(0)
        three_sum = pass_on(far_sum, three, 0, 1, whole, [sum_two])
        three_on = chips_permute(three_sum, [(1, 3), (2, 0)], n_dp)
        two_sum = pass_on(sum_two, two, 0, 1, whole, [three_on])
        two_on = chips_permute(two_sum, [(1, 2), (2, 1)], n_dp)
        last = chips_permute(choose(near, sum_none, sum_one, [two]), across, n_dp)
        own = add(jnp.where(near > 0, sum_one, sum_none), three_on)
        ends = [[last], [two_on]]
    else:
        sums = [block(k) for k in range(far)] + [far_sum]
        passed, ends = {}, []
        for link in range(far):
            for d in range(far, link, -1):
                value = sums[d if link < n_z // 2 else far - d]
                if link > 0:
                    value = pass_on(value, passed[link - 1, d], 0, 1, whole, [])
                pairs = [(link, link + 1), (far - link, far - 1 - link)]
                passed[link, d] = chips_permute(value, pairs, n_dp)
                if d == link + 1:
                    ends.append([passed[link, d]])
        own = sums[0]
        for k in range(1, (n_z + 1) // 2):
            own = jnp.where(near == k, sums[k], own)
    shapes = [(1, w_gate.shape[1] // n_dp, w_gate.shape[2])] * 2 + [(1, w_down.shape[1] // n_dp, w_down.shape[2])]
    totals = unfold([[own]] + ends, shapes)

    layer_out, input_grad, _ = outputs_home(
        hid, gates, gate_grad, up_grad, weight_down, weight_gate, weight_up, far_sum, n_ex
    )
    return layer_out, input_grad, *totals


def solution(mesh):
    rows = P(("dp", "expert"), None)
    seqs = P("dp", "expert", None)
    weights = P("expert", None, None)
    shards = P("expert", "dp", None)
    return jax.shard_map(
        on_device,
        mesh=mesh,
        in_specs=(rows, seqs, seqs, seqs, rows, rows, rows, weights, weights, weights),
        out_specs=(rows, rows, shards, shards, shards),
        check_vma=False,
    )
```

```python
import functools
import math

import jax
import jax.numpy as jnp
from jax import lax
from jax.experimental import pallas as pl
from jax.experimental.pallas import tpu as pltpu
from jax.sharding import PartitionSpec as P

CORES = 2
LANES = 128
F32 = jnp.float32
BF16 = jnp.bfloat16
MIB = 1 << 20
PIECES = 1
BIG = 24


def contract(left, right, left_dim, right_dim):
    return lax.dot_general(left, right, (((left_dim,), (right_dim,)), ((), ())), preferred_element_type=F32)


def params(mib, **more):
    return pltpu.CompilerParams(vmem_limit_bytes=mib * MIB, **more)


def room(rows, width):
    return 16 + rows * width * 10 // MIB


def cost(flops, bytes_accessed):
    return pl.CostEstimate(flops=flops, bytes_accessed=bytes_accessed, transcendentals=0)


def vmem():
    return pl.BlockSpec(memory_space=pltpu.VMEM)


def in_hbm(value):
    return pltpu.with_memory_space_constraint(value, pltpu.HBM)


def hbm():
    return pl.BlockSpec(memory_space=pl.ANY)


LENGTH, ADV, GATES = 0, 1, 2
PARTS = 3


def pick_kernel(n_dp, dest_hbm, len_hbm, adv_hbm, rows_hbm, *refs):
    outs, (dest_ref, len_ref, adv_ref, sems, row_sems) = refs[:-5], refs[-5:]
    small = [
        pltpu.make_async_copy(source, target, sems.at[i])
        for i, (source, target) in enumerate(((dest_hbm, dest_ref), (len_hbm, len_ref), (adv_hbm, adv_ref)))
    ]
    for copy in small:
        copy.start()
    seqs, slot, width = rows_hbm.shape
    lane = lax.broadcasted_iota(jnp.int32, (slot, LANES), 1)
    which = lax.broadcasted_iota(jnp.int32, (1, seqs), 1)
    me = lax.axis_index("dp")
    small[0].wait()
    found, copies = [], []
    for i in range(n_dp):
        out = outs[i // CORES]
        here = pl.ds(i % CORES * slot, slot)
        seq = jnp.int32(0)
        live = jnp.int32(0)
        for s in range(seqs):
            hit = dest_ref[0, 0, s] == (me ^ i)
            seq = jnp.where(hit, s, seq)
            live = jnp.where(hit, 1, live)
        found.append((seq, live))
        copies.append(pltpu.make_async_copy(rows_hbm.at[seq], out.at[here, pl.ds(0, width)], row_sems.at[i]))
        copies[-1].start()
    small[1].wait()
    small[2].wait()
    lengths = len_ref[0].astype(F32)
    advs = adv_ref[0].astype(F32)
    for i, (seq, live) in enumerate(found):
        mine = (which == seq) & (live == 1)
        length = jnp.sum(jnp.where(mine, lengths, 0.0), axis=1, keepdims=True)
        adv = jnp.sum(jnp.where(mine, advs, 0.0), axis=1, keepdims=True)
        value = jnp.where(lane == LENGTH, length, jnp.where(lane == ADV, adv, 0.0)).astype(BF16)
        outs[i // CORES][i % CORES * slot : (i % CORES + 1) * slot, width:] = value
    for copy in copies:
        copy.wait()


def pick(dest, lengths, adv, rows, n_dp):
    seqs, slot, width = rows.shape
    return pl.pallas_call(
        functools.partial(pick_kernel, n_dp),
        out_shape=[jax.ShapeDtypeStruct((CORES * slot, width + LANES), BF16)] * (n_dp // CORES),
        in_specs=[hbm()] * 4,
        out_specs=[vmem()] * (n_dp // CORES),
        scratch_shapes=[
            pltpu.SMEM(dest.shape, jnp.int32),
            pltpu.VMEM(lengths.shape, lengths.dtype),
            pltpu.VMEM(adv.shape, adv.dtype),
            pltpu.SemaphoreType.DMA((3,)),
            pltpu.SemaphoreType.DMA((n_dp,)),
        ],
        compiler_params=params(16),
        name="pick",
    )(*[in_hbm(value) for value in (dest, lengths, adv, rows)])


def gate_notes(ids, gates):
    note = lax.broadcasted_iota(jnp.int32, (LANES, ids.shape[1]), 0) - GATES
    expert, part = note // PARTS, note % PARTS
    value = jnp.zeros(note.shape, F32)
    for k in range(ids.shape[0]):
        value = value + jnp.where(ids[k : k + 1] == expert, gates[k : k + 1], 0.0)
    value = jnp.where(note < 0, 0.0, value)
    high = value.astype(BF16).astype(F32)
    middle = (value - high).astype(BF16).astype(F32)
    low = value - high - middle
    return jnp.where(part == 0, high, jnp.where(part == 1, middle, low))


def regroup_kernel(count, *refs):
    pieces, (mine, other) = refs[:count], refs[-2:]
    slot = pieces[0].shape[0] // CORES
    for i, piece in enumerate(pieces):
        mine[i * slot : (i + 1) * slot, :] = piece[:slot]
        other[i * slot : (i + 1) * slot, :] = piece[slot:]


def regroup(pieces, after):
    rows, wide = pieces[0].shape
    count = len(pieces)
    out = jax.ShapeDtypeStruct((count * rows // CORES, wide), BF16)
    return pl.pallas_call(
        functools.partial(regroup_kernel, count),
        out_shape=[out, out],
        in_specs=[vmem()] * count + [hbm()] * len(after),
        out_specs=[vmem()] * 2,
        compiler_params=params(16),
        name="regroup",
    )(*pieces, *after)


def assemble_kernel(slot, ids_ref, gates_ref, mine, other, *halves):
    rows, wide = halves[0].shape
    width = wide - LANES
    per_half = rows // slot
    me = lax.axis_index("dp")
    notes = gate_notes(ids_ref[...], gates_ref[...]).T
    for i in range(CORES * per_half):
        piece = (mine, other)[i % CORES][i // CORES * slot : (i // CORES + 1) * slot, :]
        place = me ^ i
        at = pl.multiple_of((place % per_half) * slot, slot)
        for h, half in enumerate(halves):

            @pl.when(place // per_half == h)
            def _(piece=piece, half=half, at=at):
                half[pl.ds(at, slot), :] = piece

    for h, half in enumerate(halves):
        own = notes[h * rows : (h + 1) * rows]
        half[:, width:] = (half[:, width:].astype(F32) + own).astype(BF16)


def assemble(mine, other, slot, ids, gates):
    return pl.pallas_call(
        functools.partial(assemble_kernel, slot),
        out_shape=[jax.ShapeDtypeStruct(mine.shape, BF16)] * 2,
        in_specs=[vmem()] * 4,
        out_specs=[vmem()] * 2,
        compiler_params=params(16),
        name="assemble",
    )(ids, gates, mine, other)


def send_sequences(gen_rows, gen_lengths, gen_adv, destination, n_dp):
    seq_dev = destination.shape[2]
    slot = gen_rows.shape[0] // seq_dev
    pieces = list(pick(destination, gen_lengths, gen_adv, gen_rows.reshape(seq_dev, slot, gen_rows.shape[1]), n_dp))
    for i in range(1, len(pieces)):
        pieces[i] = lax.ppermute(pieces[i], "dp", [(d, d ^ (CORES * i)) for d in range(n_dp)])
    return pieces


def place_sequences(mine, other, n_dp, seq_dev, ids, gates):
    slot = CORES * mine.shape[0] // n_dp
    if n_dp == seq_dev:
        return assemble(mine, other, slot, ids.T, gates.T)
    wide = mine.shape[1]
    width = wide - LANES
    g = lax.axis_index("dp")
    stack = jnp.stack([mine.reshape(-1, slot, wide), other.reshape(-1, slot, wide)], axis=1)
    stack = stack.reshape(n_dp, slot, wide)[jnp.arange(n_dp, dtype=jnp.int32) ^ g]
    arrived = stack[:, 0, width + LENGTH] > 0
    arrival = jnp.cumsum(arrived.astype(jnp.int32)) - 1
    chosen = arrived[None, :] & (arrival[None, :] == jnp.arange(seq_dev, dtype=jnp.int32)[:, None])
    from_peer = jnp.sum(jnp.where(chosen, jnp.arange(n_dp, dtype=jnp.int32)[None, :], 0), axis=1)
    x = stack[from_peer].reshape(seq_dev * slot, wide)
    notes = (x[:, width:].astype(F32) + gate_notes(ids.T, gates.T).T).astype(BF16)
    x = jnp.concatenate([x[:, :width], notes], axis=1)
    half = x.shape[0] // 2
    return x[:half], x[half:]


def swap(value, i, n_ex):
    return lax.ppermute(value, "expert", [(d, d ^ i) for d in range(n_ex)])


def gather_rows(rows, n_ex):
    if n_ex != 4:
        return [rows] + [swap(rows, i, n_ex) for i in range(1, n_ex)]
    half = rows.shape[0] // 2
    first = swap(rows, 1, n_ex)
    second = swap(rows, 2, n_ex)
    return [rows, first, second, swap(first[:half], 2, n_ex), swap(second[half:], 1, n_ex)]


def gather_halves(low, high, n_ex, between):
    if n_ex != 4:
        pieces = [low, high]
        for i in range(1, n_ex):
            pieces += [swap(low, i, n_ex), swap(high, i, n_ex)]
        return pieces
    first_low, second_high = swap(low, 1, n_ex), swap(high, 2, n_ex)
    first_high, second_low = swap(high, 1, n_ex), swap(low, 2, n_ex)
    on_low, on_high, _ = lax.optimization_barrier((first_low, second_high, between))
    return [low, high, first_low, first_high, second_low, second_high, swap(on_low, 2, n_ex), swap(on_high, 1, n_ex)]


def with_last(pieces, size):
    at, cut = 0, sum(p.shape[0] for p in pieces) - size
    for i, piece in enumerate(pieces):
        if at == cut:
            return pieces[:i], pieces[i:]
        at += piece.shape[0]


def tie(value, *others):
    return lax.optimization_barrier((value,) + others)[0]


def load_pieces(pieces, whole, sems):
    at, copies = 0, []
    for i, piece in enumerate(pieces):
        size = piece.shape[0]
        copies.append(pltpu.make_async_copy(piece, whole.at[pl.ds(at, size)], sems.at[i]))
        at += size
    for copy in copies:
        copy.start()
    for copy in copies:
        copy.wait()


def hidden_grad_kernel(count, w_ref, *refs):
    pieces, (out, whole_out, whole, sems, out_sem) = refs[:count], refs[count:]
    step = pl.program_id(0)

    @pl.when(step == 0)
    def _():
        load_pieces(pieces, whole, sems)
        pltpu.make_async_copy(whole, whole_out, out_sem).start()

    out[...] = contract(whole[...], w_ref[...], 1, 1)

    @pl.when(step == pl.num_programs(0) - 1)
    def _():
        pltpu.make_async_copy(whole, whole_out, out_sem).wait()


def hidden_grad(pieces, w_down):
    rows = sum(p.shape[0] for p in pieces)
    units, width = w_down.shape
    tile = 256
    return pl.pallas_call(
        functools.partial(hidden_grad_kernel, len(pieces)),
        grid=(units // tile,),
        out_shape=[jax.ShapeDtypeStruct((rows, units), F32), jax.ShapeDtypeStruct((rows, width), BF16)],
        in_specs=[pl.BlockSpec((tile, width), lambda j: (j, 0))] + [hbm()] * len(pieces),
        out_specs=[pl.BlockSpec((rows, tile), lambda j: (0, j)), hbm()],
        scratch_shapes=[
            pltpu.VMEM((rows, width), BF16),
            pltpu.SemaphoreType.DMA((len(pieces),)),
            pltpu.SemaphoreType.DMA,
        ],
        compiler_params=params(BIG),
        cost_estimate=cost(2 * rows * units * width, 2 * units * width + 4 * rows * width),
        name="hidden_grad",
    )(w_down, *pieces)


def shard_place(shard, n_dp):
    me = lax.axis_index("dp")
    n_z = n_dp // CORES
    chip, core = shard // CORES, shard % CORES
    at = jnp.where(me // CORES >= n_z // 2, chip, n_z - 1 - chip)
    return jnp.where(core == me % CORES, n_z, 0) + at


def units_kernel(count, slot, first, n_dp, wg_ref, wu_ref, hg_ref, *refs):
    if not first:
        refs = refs[6:]
    pieces, refs = refs[:count], refs[count:]
    gate_out, up_out, hid_out, turned_hs, turned_x, gates_out, whole, gs_ref, sems = refs
    step = pl.program_id(0)
    rows, wide = whole.shape
    width = wide - LANES

    @pl.when(step == 0)
    def _():
        load_pieces(pieces, whole, sems)
        notes = whole[:, width:].astype(F32)
        lane = lax.broadcasted_iota(jnp.int32, notes.shape, 1) - GATES - PARTS * lax.axis_index("expert")
        gates = jnp.sum(jnp.where((lane >= 0) & (lane < PARTS), notes, 0.0), axis=1, keepdims=True)
        length, adv = notes[:, LENGTH : LENGTH + 1], notes[:, ADV : ADV + 1]
        position = lax.broadcasted_iota(jnp.int32, (rows, 1), 0) % slot
        gates_out[...] = gates
        gs_ref[...] = jnp.where(position.astype(F32) < length, gates * (adv / length), 0.0)
        strip = width // n_dp
        for i in range(n_dp):
            at = pl.multiple_of(shard_place(i, n_dp) * strip, strip)
            turned_x[pl.ds(at, strip), :] = whole[:, i * strip : (i + 1) * strip].T

    x = whole[:, :width]
    gate = jnp.dot(x, wg_ref[...], preferred_element_type=F32)
    up = jnp.dot(x, wu_ref[...], preferred_element_type=F32)
    gs = gs_ref[...]
    sig = jax.nn.sigmoid(gate)
    act = gate * sig
    hid = (act * up).astype(BF16)
    hid_out[...] = hid
    turned = (hid.astype(F32) * gs).astype(BF16).T
    tile, shard = turned.shape[0], turned_hs.shape[0] // n_dp
    chunk = math.gcd(tile, shard)
    for i in range(tile // chunk):
        row = step * tile + i * chunk
        at = shard_place(row // shard, n_dp) * shard + row % shard
        turned_hs[pl.ds(pl.multiple_of(at, chunk), chunk), :] = turned[i * chunk : (i + 1) * chunk]
    hg = hg_ref[...] * gs
    gate_out[...] = (hg * up * sig * (1.0 + gate * (1.0 - sig))).astype(BF16)
    up_out[...] = (hg * act).astype(BF16)


def hidden_units(pieces, w_gate, w_up, hg, slot, n_dp, before=None):
    total, units = hg.shape
    width = w_gate.shape[0]
    rows = sum(p.shape[0] for p in pieces)
    tile = 256
    at = 0 if before is None else total // rows - 1
    columns = pl.BlockSpec((rows, tile), lambda j: (at, j))
    weights = pl.BlockSpec((width, tile), lambda j: (0, j))
    before = before or []
    return pl.pallas_call(
        functools.partial(units_kernel, len(pieces), slot, not before, n_dp),
        grid=(units // tile,),
        out_shape=[jax.ShapeDtypeStruct((total, units), BF16)] * 3
        + [
            jax.ShapeDtypeStruct((units, total), BF16),
            jax.ShapeDtypeStruct((width, total), BF16),
            jax.ShapeDtypeStruct((total, 1), F32),
        ],
        in_specs=[weights, weights, columns] + [hbm()] * (len(before) + len(pieces)),
        out_specs=[columns] * 3
        + [
            pl.BlockSpec((units, rows), lambda j: (0, at)),
            pl.BlockSpec((width, rows), lambda j: (0, at)),
            pl.BlockSpec((rows, 1), lambda j: (at, 0)),
        ],
        scratch_shapes=[
            pltpu.VMEM((rows, width + LANES), BF16),
            pltpu.VMEM((rows, 1), F32),
            pltpu.SemaphoreType.DMA((len(pieces),)),
        ],
        input_output_aliases={3 + i: i for i in range(len(before))},
        compiler_params=params(room(rows, width)),
        cost_estimate=cost(4 * rows * units * width, 4 * units * width + 4 * rows * width),
        name="hidden_units",
    )(w_gate, w_up, hg, *before, *pieces)


def far_grads_kernel(x_ref, gate_ref, up_ref, other, mine):
    gate = jnp.dot(x_ref[...], gate_ref[...], preferred_element_type=F32).astype(BF16)
    up = jnp.dot(x_ref[...], up_ref[...], preferred_element_type=F32).astype(BF16)

    @pl.when(pl.program_id(0) == 0)
    def _():
        other[0] = gate
        other[1] = up

    @pl.when(pl.program_id(0) == 1)
    def _():
        mine[0] = gate
        mine[1] = up


def far_grads(turned_x, gate_grad, up_grad, n_dp):
    rows, units = gate_grad.shape
    width = turned_x.shape[0]
    n_z, shard = n_dp // CORES, width // n_dp
    out = pl.BlockSpec((2, shard, units), lambda k: (0, 0, 0))
    whole = pl.BlockSpec((rows, units), lambda k: (0, 0))
    return pl.pallas_call(
        far_grads_kernel,
        grid=(CORES,),
        in_specs=[pl.BlockSpec((shard, rows), lambda k: (k * n_z, 0)), whole, whole],
        out_specs=[out, out],
        out_shape=[pltpu.HBM((2, shard, units), BF16)] * 2,
        compiler_params=params(BIG),
        cost_estimate=cost(8 * rows * units * shard, 16 * units * shard + 4 * rows * units),
        name="far_grads",
    )(turned_x, gate_grad, up_grad)


def rest_grads_kernel(shard, x_ref, gate_ref, up_ref, _, other, mine):
    count = other.shape[0]
    for k, out in enumerate((other, mine)):
        x = x_ref[pl.ds((k * (count + 1) + 1) * shard, count * shard), :]
        for p, grad in enumerate((gate_ref, up_ref)):
            value = jnp.dot(x, grad[...], preferred_element_type=F32).astype(BF16)
            for b in range(count):
                out[b, p] = value[b * shard : (b + 1) * shard]


def rest_grads(turned_x, gate_grad, up_grad, after, n_dp):
    rows, units = gate_grad.shape
    width = turned_x.shape[0]
    n_z, shard = n_dp // CORES, width // n_dp
    tile = 256
    columns = pl.BlockSpec((rows, tile), lambda j: (0, j))
    out = pl.BlockSpec((n_z - 1, 2, shard, tile), lambda j: (0, 0, 0, j))
    return pl.pallas_call(
        functools.partial(rest_grads_kernel, shard),
        grid=(units // tile,),
        in_specs=[pl.BlockSpec((width, rows), lambda j: (0, 0)), columns, columns, hbm()],
        out_specs=[out, out],
        out_shape=[pltpu.HBM((n_z - 1, 2, shard, units), BF16)] * 2,
        compiler_params=params(room(rows, width)),
        cost_estimate=cost(4 * rows * units * width, 4 * units * width + 4 * rows * units),
        name="rest_grads",
    )(turned_x, gate_grad, up_grad, after)


def row_grad_kernel(hid_ref, dy_ref, other, mine):
    n_z, shard, tile = mine.shape
    value = jnp.dot(hid_ref[...], dy_ref[...], preferred_element_type=F32).astype(BF16)
    for k, out in enumerate((other, mine)):
        for b in range(n_z):
            at = (k * n_z + b) * shard
            out[b] = value[at : at + shard]


def row_grad(turned_hid, dy, n_dp):
    units, rows = turned_hid.shape
    width = dy.shape[1]
    n_z, shard = n_dp // CORES, units // n_dp
    tile = 512
    block = pl.BlockSpec((n_z, shard, tile), lambda j: (0, 0, j))
    return pl.pallas_call(
        row_grad_kernel,
        grid=(width // tile,),
        in_specs=[pl.BlockSpec((units, rows), lambda j: (0, 0)), pl.BlockSpec((rows, tile), lambda j: (0, j))],
        out_specs=[block, block],
        out_shape=[pltpu.HBM((n_z, shard, width), BF16)] * 2,
        compiler_params=params(BIG),
        cost_estimate=cost(2 * rows * units * width, 2 * units * width + 2 * rows * width),
        name="row_grad",
    )(turned_hid, dy)


def outputs_kernel(layer_groups, grad_groups, hid_ref, gates_ref, gate_ref, up_ref, wd_ref, wg_ref, wu_ref, _, *outs):
    layer = jnp.dot(hid_ref[...], wd_ref[...], preferred_element_type=F32) * gates_ref[...]
    value = contract(gate_ref[...], wg_ref[...], 1, 1) + contract(up_ref[...], wu_ref[...], 1, 1)
    size = outs[0].shape[1]
    for result, groups, refs in (
        (layer.astype(BF16), layer_groups, outs[: len(layer_groups)]),
        (value.astype(BF16), grad_groups, outs[len(layer_groups) :]),
    ):
        for group, out in zip(groups, refs):
            for n, i in enumerate(group):
                out[n] = result[i * size : (i + 1) * size]


def outputs(hid, gates, gate_grad, up_grad, w_down, w_gate, w_up, after, n_ex, layer_groups, grad_groups):
    rows, units = hid.shape
    width = w_down.shape[1]
    tile = 512
    size = rows // n_ex
    whole = pl.BlockSpec((rows, units), lambda j: (0, 0))
    columns = pl.BlockSpec((units, tile), lambda j: (0, j))
    weights = pl.BlockSpec((tile, units), lambda j: (j, 0))
    counts = [len(group) for group in layer_groups + grad_groups]
    return pl.pallas_call(
        functools.partial(outputs_kernel, layer_groups, grad_groups),
        grid=(width // tile,),
        out_shape=[jax.ShapeDtypeStruct((n, size, width), BF16) for n in counts],
        in_specs=[whole, pl.BlockSpec((rows, 1), lambda j: (0, 0)), whole, whole, columns, weights, weights, hbm()],
        out_specs=[pl.BlockSpec((n, size, tile), lambda j: (0, 0, j)) for n in counts],
        compiler_params=params(room(rows, width)),
        cost_estimate=cost(6 * rows * units * width, 6 * units * width + 4 * rows * width),
        name="outputs",
    )(hid, gates, gate_grad, up_grad, w_down, w_gate, w_up, after)


def add(*parts):
    return sum(part.astype(F32) for part in parts).astype(BF16)


def outputs_home(hid, gates, gate_grad, up_grad, w_down, w_gate, w_up, after, n_ex):
    weights = (hid, gates, gate_grad, up_grad, w_down, w_gate, w_up, after, n_ex)
    if n_ex != 4:
        single = [[i] for i in range(n_ex)]
        parts = outputs(*weights, single, single)
        layer, grad = [], []
        for i in range(n_ex):
            layer.append(swap(parts[i][0], i, n_ex) if i else parts[i][0])
            grad.append(swap(parts[n_ex + i][0], i, n_ex) if i else parts[n_ex + i][0])
        return add(*layer), add(*grad), []
    layer0, layer2, layer13, grad0, grad1, grad23 = outputs(*weights, [[0], [2], [1, 3]], [[0], [1], [2, 3]])
    layer_got = swap(layer13, 1, n_ex)
    grad_got = swap(grad23, 2, n_ex)
    layer_last = swap(add(layer2[0], layer_got[1]), 2, n_ex)
    grad_last = swap(add(grad1[0], grad_got[1]), 1, n_ex)
    layer, grad = add(layer0[0], layer_got[0], layer_last), add(grad0[0], grad_got[0], grad_last)
    return layer, grad, [layer_last, grad_last]


def fold_kernel(gu_mine, gu_got, row_mine, row_got, *refs):
    out = refs[-1]
    step = pl.program_id(0)

    def put(mine, got):
        value = (mine.astype(F32) + got.astype(F32)).astype(BF16)
        rows, columns = value.shape
        for i in range(columns // LANES):
            out[0, i * rows : (i + 1) * rows, :] = value[:, i * LANES : (i + 1) * LANES]

    @pl.when(step < 2)
    def _():
        put(gu_mine[0, 0], gu_got[0, 0])

    @pl.when(step == 2)
    def _():
        put(row_mine[0], row_got[0])


def fold(gu_mine, gu_got, row_mine, row_got, gu_at, row_at, piece, pieces, after):
    _, _, shard, units = gu_mine.shape
    _, row_shard, width = row_mine.shape
    per = shard * units // LANES // pieces
    gu = pl.BlockSpec((1, 1, shard, units // pieces), lambda j: (gu_at, jnp.minimum(j, 1), 0, piece))
    row = pl.BlockSpec((1, row_shard, width // pieces), lambda j: (row_at, 0, piece))
    return pl.pallas_call(
        fold_kernel,
        grid=(3,),
        in_specs=[gu, gu, row, row] + [hbm()] * len(after),
        out_specs=pl.BlockSpec((1, per, LANES), lambda j: (j, 0, 0)),
        out_shape=jax.ShapeDtypeStruct((3, per, LANES), BF16),
        compiler_params=params(16),
        cost_estimate=cost(6 * per * LANES, 18 * per * LANES),
        name="fold",
    )(gu_mine, gu_got, row_mine, row_got, *after)


def pass_on_kernel(own, got, *refs):
    refs[-1][...] = (own[...].astype(F32) + got[...].astype(F32)).astype(BF16)


def pass_on(own, got, piece, pieces, whole, after, weight=1):
    per = whole // pieces

    def part(array):
        at = piece if array.shape[1] > per else 0
        return pl.BlockSpec((1, per, LANES), lambda j: (j, at, 0))

    return pl.pallas_call(
        pass_on_kernel,
        grid=(got.shape[0],),
        in_specs=[part(own), part(got)] + [hbm()] * len(after),
        out_specs=pl.BlockSpec((1, per, LANES), lambda j: (j, 0, 0)),
        out_shape=jax.ShapeDtypeStruct((got.shape[0], per, LANES), BF16),
        compiler_params=params(16),
        cost_estimate=cost(2 * weight * got.size, 6 * weight * got.size),
        name="pass_on",
    )(own, got, *after)


def choose_kernel(place_ref, one, other, *refs):
    refs[-1][...] = jnp.where(place_ref[0] > 0, one[...].astype(F32), other[...].astype(F32)).astype(BF16)


def choose(place, one, other, after):
    block = pl.BlockSpec((1,) + one.shape[1:], lambda j, place: (j, 0, 0))
    return pl.pallas_call(
        choose_kernel,
        grid_spec=pltpu.PrefetchScalarGridSpec(
            num_scalar_prefetch=1,
            grid=(one.shape[0],),
            in_specs=[block, block] + [hbm()] * len(after),
            out_specs=block,
        ),
        out_shape=jax.ShapeDtypeStruct(one.shape, BF16),
        compiler_params=params(16),
        cost_estimate=cost(one.size, 6 * one.size),
        name="choose",
    )(place.reshape(1).astype(jnp.int32), one, other, *after)


def unfold_kernel(counts, *refs):
    parts, outs = refs[: sum(counts)], refs[sum(counts) :]
    total, at = None, 0
    for count in counts:
        pieces = [part[0].astype(F32) for part in parts[at : at + count]]
        value = pieces[0] if count == 1 else jnp.concatenate(pieces, axis=0)
        total = value if total is None else total + value
        at += count
    total = total.astype(BF16)
    for j, out in enumerate(outs):

        @pl.when(pl.program_id(0) == j)
        def _(out=out):
            rows, columns = out.shape[1:]
            for i in range(columns // LANES):
                out[0, :, i * LANES : (i + 1) * LANES] = total[i * rows : (i + 1) * rows]


def unfold(groups, shapes):
    parts = [part for group in groups for part in group]
    return pl.pallas_call(
        functools.partial(unfold_kernel, [len(group) for group in groups]),
        grid=(3,),
        in_specs=[pl.BlockSpec((1,) + part.shape[1:], lambda j: (j, 0, 0)) for part in parts],
        out_specs=[pl.BlockSpec(shape, lambda j: (0, 0, 0)) for shape in shapes],
        out_shape=[jax.ShapeDtypeStruct(shape, BF16) for shape in shapes],
        compiler_params=params(24),
        cost_estimate=cost(4 * parts[0].size, 10 * parts[0].size),
        name="unfold",
    )(*parts)


def chips_permute(value, pairs, n_dp):
    return lax.ppermute(value, "dp", [(CORES * a + c, CORES * b + c) for a, b in pairs for c in range(CORES)])


def on_device(
    gen_rows, gen_lengths, gen_adv, destination, expert_ids, gate_values, cotangent, w_gate, w_up, w_down
):
    n_dp = lax.axis_size("dp")
    n_ex = lax.axis_size("expert")
    n_z = n_dp // CORES
    size = cotangent.shape[0]
    slot = gen_rows.shape[0] // destination.shape[2]
    weight_gate, weight_up, weight_down = w_gate[0], w_up[0], w_down[0]
    g = lax.axis_index("dp")
    z = g // CORES
    near = jnp.minimum(z, n_z - 1 - z)
    other_core = [(d, d ^ 1) for d in range(n_dp)]

    def swap_core(value):
        return lax.ppermute(value, "dp", other_core)

    pieces = send_sequences(gen_rows, gen_lengths, gen_adv, destination, n_dp)
    cot_pieces = gather_rows(tie(cotangent, pieces[0]), n_ex)
    mine, other = regroup(pieces, cot_pieces[1:3])
    other = swap_core(other)
    low, high = place_sequences(mine, other, n_dp, destination.shape[2], expert_ids, gate_values)
    hg, dy_all = hidden_grad(cot_pieces, weight_down)
    x_pieces = gather_halves(low, high, n_ex, hg)
    early, late = with_last(x_pieces, size)
    before = hidden_units(early, weight_gate, weight_up, hg, slot, n_dp)
    gate_grad, up_grad, hid, turned_hs, turned_x, gates = hidden_units(
        late, weight_gate, weight_up, hg, slot, n_dp, before
    )

    far = n_z - 1
    rest = list(range(far - 1, -1, -1))
    far_other, far_mine = far_grads(turned_x, gate_grad, up_grad, n_dp)
    far_got = swap_core(far_other)
    row_other, row_mine = row_grad(tie(turned_hs, far_other), dy_all, n_dp)
    row_got = swap_core(row_other)
    whole = w_gate.shape[1] * w_gate.shape[2] // n_dp // LANES
    far_sum = fold(far_mine[None], far_got[None], row_mine, row_got, 0, 0, 0, 1, [])
    rest_other, rest_mine = rest_grads(turned_x, gate_grad, up_grad, far_got, n_dp)
    rest_got = swap_core(rest_other)

    def block(k, *after):
        return fold(rest_mine, rest_got, row_mine, row_got, far - 1 - k, far - k, 0, 1, after)

    if n_z == 4:
        outward, across = [(0, 1), (3, 2)], [(0, 1), (1, 0), (2, 3), (3, 2)]
        three = chips_permute(far_sum, outward, n_dp)
        sum_two = block(2)
        two = chips_permute(sum_two, outward, n_dp)
        sum_one, sum_none = block(1), block(0)
        three_sum = pass_on(far_sum, three, 0, 1, whole, [sum_two])
        three_on = chips_permute(three_sum, [(1, 3), (2, 0)], n_dp)
        two_sum = pass_on(sum_two, two, 0, 1, whole, [])
        two_on = chips_permute(tie(two_sum, three_on), [(1, 2), (2, 1)], n_dp)
        last = chips_permute(choose(near, sum_none, sum_one, [two]), across, n_dp)
        own = add(jnp.where(near > 0, sum_one, sum_none), three_on)
        ends = [[last], [two_on]]
    else:
        sums = [block(k) for k in range(far)] + [far_sum]
        passed, ends = {}, []
        for link in range(far):
            for d in range(far, link, -1):
                value = sums[d if link < n_z // 2 else far - d]
                if link > 0:
                    value = pass_on(value, passed[link - 1, d], 0, 1, whole, [])
                pairs = [(link, link + 1), (far - link, far - 1 - link)]
                passed[link, d] = chips_permute(value, pairs, n_dp)
                if d == link + 1:
                    ends.append([passed[link, d]])
        own = sums[0]
        for k in range(1, (n_z + 1) // 2):
            own = jnp.where(near == k, sums[k], own)
    shapes = [(1, w_gate.shape[1] // n_dp, w_gate.shape[2])] * 2 + [(1, w_down.shape[1] // n_dp, w_down.shape[2])]
    totals = unfold([[own]] + ends, shapes)

    layer_out, input_grad, _ = outputs_home(
        hid, gates, gate_grad, up_grad, weight_down, weight_gate, weight_up, far_sum, n_ex
    )
    return layer_out, input_grad, *totals


def solution(mesh):
    rows = P(("dp", "expert"), None)
    seqs = P("dp", "expert", None)
    weights = P("expert", None, None)
    shards = P("expert", "dp", None)
    return jax.shard_map(
        on_device,
        mesh=mesh,
        in_specs=(rows, seqs, seqs, seqs, rows, rows, rows, weights, weights, weights),
        out_specs=(rows, rows, shards, shards, shards),
        check_vma=False,
    )
```

```python
import functools
import math

import jax
import jax.numpy as jnp
from jax import lax
from jax.experimental import pallas as pl
from jax.experimental.pallas import tpu as pltpu
from jax.sharding import PartitionSpec as P

CORES = 2
LANES = 128
F32 = jnp.float32
BF16 = jnp.bfloat16
MIB = 1 << 20
PIECES = 1
BIG = 24


def contract(left, right, left_dim, right_dim):
    return lax.dot_general(left, right, (((left_dim,), (right_dim,)), ((), ())), preferred_element_type=F32)


def params(mib, **more):
    return pltpu.CompilerParams(vmem_limit_bytes=mib * MIB, **more)


def room(rows, width):
    return 16 + rows * width * 10 // MIB


def cost(flops, bytes_accessed):
    return pl.CostEstimate(flops=flops, bytes_accessed=bytes_accessed, transcendentals=0)


def vmem():
    return pl.BlockSpec(memory_space=pltpu.VMEM)


def in_hbm(value):
    return pltpu.with_memory_space_constraint(value, pltpu.HBM)


def hbm():
    return pl.BlockSpec(memory_space=pl.ANY)


LENGTH, ADV, GATES = 0, 1, 2
PARTS = 3


def pick_kernel(n_dp, dest_hbm, len_hbm, adv_hbm, rows_hbm, *refs):
    outs, (dest_ref, len_ref, adv_ref, sems, row_sems) = refs[:-5], refs[-5:]
    small = [
        pltpu.make_async_copy(source, target, sems.at[i])
        for i, (source, target) in enumerate(((dest_hbm, dest_ref), (len_hbm, len_ref), (adv_hbm, adv_ref)))
    ]
    for copy in small:
        copy.start()
    seqs, slot, width = rows_hbm.shape
    lane = lax.broadcasted_iota(jnp.int32, (slot, LANES), 1)
    which = lax.broadcasted_iota(jnp.int32, (1, seqs), 1)
    me = lax.axis_index("dp")
    small[0].wait()
    found, copies = [], []
    for i in range(n_dp):
        out = outs[i // CORES]
        here = pl.ds(i % CORES * slot, slot)
        seq = jnp.int32(0)
        live = jnp.int32(0)
        for s in range(seqs):
            hit = dest_ref[0, 0, s] == (me ^ i)
            seq = jnp.where(hit, s, seq)
            live = jnp.where(hit, 1, live)
        found.append((seq, live))
        copies.append(pltpu.make_async_copy(rows_hbm.at[seq], out.at[here, pl.ds(0, width)], row_sems.at[i]))
        copies[-1].start()
    small[1].wait()
    small[2].wait()
    lengths = len_ref[0].astype(F32)
    advs = adv_ref[0].astype(F32)
    for i, (seq, live) in enumerate(found):
        mine = (which == seq) & (live == 1)
        length = jnp.sum(jnp.where(mine, lengths, 0.0), axis=1, keepdims=True)
        adv = jnp.sum(jnp.where(mine, advs, 0.0), axis=1, keepdims=True)
        value = jnp.where(lane == LENGTH, length, jnp.where(lane == ADV, adv, 0.0)).astype(BF16)
        outs[i // CORES][i % CORES * slot : (i % CORES + 1) * slot, width:] = value
    for copy in copies:
        copy.wait()


def pick(dest, lengths, adv, rows, n_dp):
    seqs, slot, width = rows.shape
    return pl.pallas_call(
        functools.partial(pick_kernel, n_dp),
        out_shape=[jax.ShapeDtypeStruct((CORES * slot, width + LANES), BF16)] * (n_dp // CORES),
        in_specs=[hbm()] * 4,
        out_specs=[vmem()] * (n_dp // CORES),
        scratch_shapes=[
            pltpu.SMEM(dest.shape, jnp.int32),
            pltpu.VMEM(lengths.shape, lengths.dtype),
            pltpu.VMEM(adv.shape, adv.dtype),
            pltpu.SemaphoreType.DMA((3,)),
            pltpu.SemaphoreType.DMA((n_dp,)),
        ],
        compiler_params=params(16),
        name="pick",
    )(*[in_hbm(value) for value in (dest, lengths, adv, rows)])


def gate_notes(ids, gates):
    note = lax.broadcasted_iota(jnp.int32, (LANES, ids.shape[1]), 0) - GATES
    expert, part = note // PARTS, note % PARTS
    value = jnp.zeros(note.shape, F32)
    for k in range(ids.shape[0]):
        value = value + jnp.where(ids[k : k + 1] == expert, gates[k : k + 1], 0.0)
    value = jnp.where(note < 0, 0.0, value)
    high = value.astype(BF16).astype(F32)
    middle = (value - high).astype(BF16).astype(F32)
    low = value - high - middle
    return jnp.where(part == 0, high, jnp.where(part == 1, middle, low))


def regroup_kernel(count, *refs):
    pieces, (mine, other) = refs[:count], refs[-2:]
    slot = pieces[0].shape[0] // CORES
    for i, piece in enumerate(pieces):
        mine[i * slot : (i + 1) * slot, :] = piece[:slot]
        other[i * slot : (i + 1) * slot, :] = piece[slot:]


def regroup(pieces, after):
    rows, wide = pieces[0].shape
    count = len(pieces)
    out = jax.ShapeDtypeStruct((count * rows // CORES, wide), BF16)
    return pl.pallas_call(
        functools.partial(regroup_kernel, count),
        out_shape=[out, out],
        in_specs=[vmem()] * count + [hbm()] * len(after),
        out_specs=[vmem()] * 2,
        compiler_params=params(16),
        name="regroup",
    )(*pieces, *after)


def assemble_kernel(slot, ids_ref, gates_ref, mine, other, *halves):
    rows, wide = halves[0].shape
    width = wide - LANES
    per_half = rows // slot
    me = lax.axis_index("dp")
    notes = gate_notes(ids_ref[...], gates_ref[...]).T
    for i in range(CORES * per_half):
        piece = (mine, other)[i % CORES][i // CORES * slot : (i // CORES + 1) * slot, :]
        place = me ^ i
        at = pl.multiple_of((place % per_half) * slot, slot)
        for h, half in enumerate(halves):

            @pl.when(place // per_half == h)
            def _(piece=piece, half=half, at=at):
                half[pl.ds(at, slot), :] = piece

    for h, half in enumerate(halves):
        own = notes[h * rows : (h + 1) * rows]
        half[:, width:] = (half[:, width:].astype(F32) + own).astype(BF16)


def assemble(mine, other, slot, ids, gates):
    return pl.pallas_call(
        functools.partial(assemble_kernel, slot),
        out_shape=[jax.ShapeDtypeStruct(mine.shape, BF16)] * 2,
        in_specs=[vmem()] * 4,
        out_specs=[vmem()] * 2,
        compiler_params=params(16),
        name="assemble",
    )(ids, gates, mine, other)


def send_sequences(gen_rows, gen_lengths, gen_adv, destination, n_dp):
    seq_dev = destination.shape[2]
    slot = gen_rows.shape[0] // seq_dev
    pieces = list(pick(destination, gen_lengths, gen_adv, gen_rows.reshape(seq_dev, slot, gen_rows.shape[1]), n_dp))
    for i in range(1, len(pieces)):
        pieces[i] = lax.ppermute(pieces[i], "dp", [(d, d ^ (CORES * i)) for d in range(n_dp)])
    return pieces


def place_sequences(mine, other, n_dp, seq_dev, ids, gates):
    slot = CORES * mine.shape[0] // n_dp
    if n_dp == seq_dev:
        return assemble(mine, other, slot, ids.T, gates.T)
    wide = mine.shape[1]
    width = wide - LANES
    g = lax.axis_index("dp")
    stack = jnp.stack([mine.reshape(-1, slot, wide), other.reshape(-1, slot, wide)], axis=1)
    stack = stack.reshape(n_dp, slot, wide)[jnp.arange(n_dp, dtype=jnp.int32) ^ g]
    arrived = stack[:, 0, width + LENGTH] > 0
    arrival = jnp.cumsum(arrived.astype(jnp.int32)) - 1
    chosen = arrived[None, :] & (arrival[None, :] == jnp.arange(seq_dev, dtype=jnp.int32)[:, None])
    from_peer = jnp.sum(jnp.where(chosen, jnp.arange(n_dp, dtype=jnp.int32)[None, :], 0), axis=1)
    x = stack[from_peer].reshape(seq_dev * slot, wide)
    notes = (x[:, width:].astype(F32) + gate_notes(ids.T, gates.T).T).astype(BF16)
    x = jnp.concatenate([x[:, :width], notes], axis=1)
    half = x.shape[0] // 2
    return x[:half], x[half:]


def swap(value, i, n_ex):
    return lax.ppermute(value, "expert", [(d, d ^ i) for d in range(n_ex)])


def gather_rows(rows, n_ex):
    if n_ex != 4:
        return [rows] + [swap(rows, i, n_ex) for i in range(1, n_ex)]
    half = rows.shape[0] // 2
    first = swap(rows, 1, n_ex)
    second = swap(rows, 2, n_ex)
    return [rows, first, second, swap(first[:half], 2, n_ex), swap(second[half:], 1, n_ex)]


def gather_halves(low, high, n_ex, between):
    if n_ex != 4:
        pieces = [low, high]
        for i in range(1, n_ex):
            pieces += [swap(low, i, n_ex), swap(high, i, n_ex)]
        return pieces
    first_low, second_high = swap(low, 1, n_ex), swap(high, 2, n_ex)
    first_high, second_low = swap(high, 1, n_ex), swap(low, 2, n_ex)
    on_low, on_high, _ = lax.optimization_barrier((first_low, second_high, between))
    return [low, high, first_low, first_high, second_low, second_high, swap(on_low, 2, n_ex), swap(on_high, 1, n_ex)]


def with_last(pieces, size):
    at, cut = 0, sum(p.shape[0] for p in pieces) - size
    for i, piece in enumerate(pieces):
        if at == cut:
            return pieces[:i], pieces[i:]
        at += piece.shape[0]


def tie(value, *others):
    return lax.optimization_barrier((value,) + others)[0]


def load_pieces(pieces, whole, sems):
    at, copies = 0, []
    for i, piece in enumerate(pieces):
        size = piece.shape[0]
        copies.append(pltpu.make_async_copy(piece, whole.at[pl.ds(at, size)], sems.at[i]))
        at += size
    for copy in copies:
        copy.start()
    for copy in copies:
        copy.wait()


def hidden_grad_kernel(count, w_ref, *refs):
    pieces, (out, whole_out, whole, sems, out_sem) = refs[:count], refs[count:]
    step = pl.program_id(0)

    @pl.when(step == 0)
    def _():
        load_pieces(pieces, whole, sems)
        pltpu.make_async_copy(whole, whole_out, out_sem).start()

    out[...] = contract(whole[...], w_ref[...], 1, 1)

    @pl.when(step == pl.num_programs(0) - 1)
    def _():
        pltpu.make_async_copy(whole, whole_out, out_sem).wait()


def hidden_grad(pieces, w_down):
    rows = sum(p.shape[0] for p in pieces)
    units, width = w_down.shape
    tile = 256
    return pl.pallas_call(
        functools.partial(hidden_grad_kernel, len(pieces)),
        grid=(units // tile,),
        out_shape=[jax.ShapeDtypeStruct((rows, units), F32), jax.ShapeDtypeStruct((rows, width), BF16)],
        in_specs=[pl.BlockSpec((tile, width), lambda j: (j, 0))] + [hbm()] * len(pieces),
        out_specs=[pl.BlockSpec((rows, tile), lambda j: (0, j)), hbm()],
        scratch_shapes=[
            pltpu.VMEM((rows, width), BF16),
            pltpu.SemaphoreType.DMA((len(pieces),)),
            pltpu.SemaphoreType.DMA,
        ],
        compiler_params=params(BIG),
        cost_estimate=cost(2 * rows * units * width, 2 * units * width + 4 * rows * width),
        name="hidden_grad",
    )(w_down, *pieces)


def shard_place(shard, n_dp):
    me = lax.axis_index("dp")
    n_z = n_dp // CORES
    chip, core = shard // CORES, shard % CORES
    at = jnp.where(me // CORES >= n_z // 2, chip, n_z - 1 - chip)
    return jnp.where(core == me % CORES, n_z, 0) + at


def units_kernel(count, slot, first, n_dp, wg_ref, wu_ref, hg_ref, *refs):
    if not first:
        refs = refs[6:]
    pieces, refs = refs[:count], refs[count:]
    gate_out, up_out, hid_out, turned_hs, turned_x, gates_out, whole, gs_ref, sems = refs
    step = pl.program_id(0)
    rows, wide = whole.shape
    width = wide - LANES

    @pl.when(step == 0)
    def _():
        load_pieces(pieces, whole, sems)
        notes = whole[:, width:].astype(F32)
        lane = lax.broadcasted_iota(jnp.int32, notes.shape, 1) - GATES - PARTS * lax.axis_index("expert")
        gates = jnp.sum(jnp.where((lane >= 0) & (lane < PARTS), notes, 0.0), axis=1, keepdims=True)
        length, adv = notes[:, LENGTH : LENGTH + 1], notes[:, ADV : ADV + 1]
        position = lax.broadcasted_iota(jnp.int32, (rows, 1), 0) % slot
        gates_out[...] = gates
        gs_ref[...] = jnp.where(position.astype(F32) < length, gates * (adv / length), 0.0)
        strip = width // n_dp
        for i in range(n_dp):
            at = pl.multiple_of(shard_place(i, n_dp) * strip, strip)
            turned_x[pl.ds(at, strip), :] = whole[:, i * strip : (i + 1) * strip].T

    x = whole[:, :width]
    here = pl.ds(pl.multiple_of(step * gate_out.shape[1], LANES), gate_out.shape[1])
    gate = jnp.dot(x, wg_ref[:, here], preferred_element_type=F32)
    up = jnp.dot(x, wu_ref[:, here], preferred_element_type=F32)
    gs = gs_ref[...]
    sig = jax.nn.sigmoid(gate)
    act = gate * sig
    hid = (act * up).astype(BF16)
    hid_out[...] = hid
    turned = (hid.astype(F32) * gs).astype(BF16).T
    tile, shard = turned.shape[0], turned_hs.shape[0] // n_dp
    chunk = math.gcd(tile, shard)
    for i in range(tile // chunk):
        row = step * tile + i * chunk
        at = shard_place(row // shard, n_dp) * shard + row % shard
        turned_hs[pl.ds(pl.multiple_of(at, chunk), chunk), :] = turned[i * chunk : (i + 1) * chunk]
    hg = hg_ref[...] * gs
    gate_out[...] = (hg * up * sig * (1.0 + gate * (1.0 - sig))).astype(BF16)
    up_out[...] = (hg * act).astype(BF16)


def hidden_units(pieces, w_gate, w_up, hg, slot, n_dp, before=None):
    total, units = hg.shape
    width = w_gate.shape[0]
    rows = sum(p.shape[0] for p in pieces)
    tile = 256
    at = 0 if before is None else total // rows - 1
    columns = pl.BlockSpec((rows, tile), lambda j: (at, j))
    weights = vmem()
    before = before or []
    return pl.pallas_call(
        functools.partial(units_kernel, len(pieces), slot, not before, n_dp),
        grid=(units // tile,),
        out_shape=[jax.ShapeDtypeStruct((total, units), BF16)] * 3
        + [
            jax.ShapeDtypeStruct((units, total), BF16),
            jax.ShapeDtypeStruct((width, total), BF16),
            jax.ShapeDtypeStruct((total, 1), F32),
        ],
        in_specs=[weights, weights, columns] + [hbm()] * (len(before) + len(pieces)),
        out_specs=[columns] * 3
        + [
            pl.BlockSpec((units, rows), lambda j: (0, at)),
            pl.BlockSpec((width, rows), lambda j: (0, at)),
            pl.BlockSpec((rows, 1), lambda j: (at, 0)),
        ],
        scratch_shapes=[
            pltpu.VMEM((rows, width + LANES), BF16),
            pltpu.VMEM((rows, 1), F32),
            pltpu.SemaphoreType.DMA((len(pieces),)),
        ],
        input_output_aliases={3 + i: i for i in range(len(before))},
        compiler_params=params(room(rows, width)),
        cost_estimate=cost(4 * rows * units * width, 4 * units * width + 4 * rows * width),
        name="hidden_units",
    )(w_gate, w_up, hg, *before, *pieces)


def far_grads_kernel(x_ref, gate_ref, up_ref, other, mine):
    gate = jnp.dot(x_ref[...], gate_ref[...], preferred_element_type=F32).astype(BF16)
    up = jnp.dot(x_ref[...], up_ref[...], preferred_element_type=F32).astype(BF16)

    @pl.when(pl.program_id(0) == 0)
    def _():
        other[0] = gate
        other[1] = up

    @pl.when(pl.program_id(0) == 1)
    def _():
        mine[0] = gate
        mine[1] = up


def far_grads(turned_x, gate_grad, up_grad, n_dp):
    rows, units = gate_grad.shape
    width = turned_x.shape[0]
    n_z, shard = n_dp // CORES, width // n_dp
    out = pl.BlockSpec((2, shard, units), lambda k: (0, 0, 0))
    whole = pl.BlockSpec((rows, units), lambda k: (0, 0))
    return pl.pallas_call(
        far_grads_kernel,
        grid=(CORES,),
        in_specs=[pl.BlockSpec((shard, rows), lambda k: (k * n_z, 0)), whole, whole],
        out_specs=[out, out],
        out_shape=[pltpu.HBM((2, shard, units), BF16)] * 2,
        compiler_params=params(BIG),
        cost_estimate=cost(8 * rows * units * shard, 16 * units * shard + 4 * rows * units),
        name="far_grads",
    )(turned_x, gate_grad, up_grad)


def rest_grads_kernel(shard, x_ref, gate_ref, up_ref, _, other, mine):
    count = other.shape[0]
    for k, out in enumerate((other, mine)):
        x = x_ref[pl.ds((k * (count + 1) + 1) * shard, count * shard), :]
        for p, grad in enumerate((gate_ref, up_ref)):
            value = jnp.dot(x, grad[...], preferred_element_type=F32).astype(BF16)
            for b in range(count):
                out[b, p] = value[b * shard : (b + 1) * shard]


def rest_grads(turned_x, gate_grad, up_grad, after, n_dp):
    rows, units = gate_grad.shape
    width = turned_x.shape[0]
    n_z, shard = n_dp // CORES, width // n_dp
    tile = 256
    columns = pl.BlockSpec((rows, tile), lambda j: (0, j))
    out = pl.BlockSpec((n_z - 1, 2, shard, tile), lambda j: (0, 0, 0, j))
    return pl.pallas_call(
        functools.partial(rest_grads_kernel, shard),
        grid=(units // tile,),
        in_specs=[pl.BlockSpec((width, rows), lambda j: (0, 0)), columns, columns, hbm()],
        out_specs=[out, out],
        out_shape=[pltpu.HBM((n_z - 1, 2, shard, units), BF16)] * 2,
        compiler_params=params(room(rows, width)),
        cost_estimate=cost(4 * rows * units * width, 4 * units * width + 4 * rows * units),
        name="rest_grads",
    )(turned_x, gate_grad, up_grad, after)


def row_grad_kernel(hid_ref, dy_ref, other, mine):
    n_z, shard, tile = mine.shape
    value = jnp.dot(hid_ref[...], dy_ref[...], preferred_element_type=F32).astype(BF16)
    for k, out in enumerate((other, mine)):
        for b in range(n_z):
            at = (k * n_z + b) * shard
            out[b] = value[at : at + shard]


def row_grad(turned_hid, dy, n_dp):
    units, rows = turned_hid.shape
    width = dy.shape[1]
    n_z, shard = n_dp // CORES, units // n_dp
    tile = 512
    block = pl.BlockSpec((n_z, shard, tile), lambda j: (0, 0, j))
    return pl.pallas_call(
        row_grad_kernel,
        grid=(width // tile,),
        in_specs=[pl.BlockSpec((units, rows), lambda j: (0, 0)), pl.BlockSpec((rows, tile), lambda j: (0, j))],
        out_specs=[block, block],
        out_shape=[pltpu.HBM((n_z, shard, width), BF16)] * 2,
        compiler_params=params(BIG),
        cost_estimate=cost(2 * rows * units * width, 2 * units * width + 2 * rows * width),
        name="row_grad",
    )(turned_hid, dy)


def outputs_kernel(layer_groups, grad_groups, hid_ref, gates_ref, gate_ref, up_ref, wd_ref, wg_ref, wu_ref, _, *outs):
    layer = jnp.dot(hid_ref[...], wd_ref[...], preferred_element_type=F32) * gates_ref[...]
    value = contract(gate_ref[...], wg_ref[...], 1, 1) + contract(up_ref[...], wu_ref[...], 1, 1)
    size = outs[0].shape[1]
    for result, groups, refs in (
        (layer.astype(BF16), layer_groups, outs[: len(layer_groups)]),
        (value.astype(BF16), grad_groups, outs[len(layer_groups) :]),
    ):
        for group, out in zip(groups, refs):
            for n, i in enumerate(group):
                out[n] = result[i * size : (i + 1) * size]


def outputs(hid, gates, gate_grad, up_grad, w_down, w_gate, w_up, after, n_ex, layer_groups, grad_groups):
    rows, units = hid.shape
    width = w_down.shape[1]
    tile = 512
    size = rows // n_ex
    whole = pl.BlockSpec((rows, units), lambda j: (0, 0))
    columns = pl.BlockSpec((units, tile), lambda j: (0, j))
    weights = pl.BlockSpec((tile, units), lambda j: (j, 0))
    counts = [len(group) for group in layer_groups + grad_groups]
    return pl.pallas_call(
        functools.partial(outputs_kernel, layer_groups, grad_groups),
        grid=(width // tile,),
        out_shape=[jax.ShapeDtypeStruct((n, size, width), BF16) for n in counts],
        in_specs=[whole, pl.BlockSpec((rows, 1), lambda j: (0, 0)), whole, whole, columns, weights, weights, hbm()],
        out_specs=[pl.BlockSpec((n, size, tile), lambda j: (0, 0, j)) for n in counts],
        compiler_params=params(room(rows, width)),
        cost_estimate=cost(6 * rows * units * width, 6 * units * width + 4 * rows * width),
        name="outputs",
    )(hid, gates, gate_grad, up_grad, w_down, w_gate, w_up, after)


def add(*parts):
    return sum(part.astype(F32) for part in parts).astype(BF16)


def outputs_home(hid, gates, gate_grad, up_grad, w_down, w_gate, w_up, after, n_ex):
    weights = (hid, gates, gate_grad, up_grad, w_down, w_gate, w_up, after, n_ex)
    if n_ex != 4:
        single = [[i] for i in range(n_ex)]
        parts = outputs(*weights, single, single)
        layer, grad = [], []
        for i in range(n_ex):
            layer.append(swap(parts[i][0], i, n_ex) if i else parts[i][0])
            grad.append(swap(parts[n_ex + i][0], i, n_ex) if i else parts[n_ex + i][0])
        return add(*layer), add(*grad), []
    layer0, layer2, layer13, grad0, grad1, grad23 = outputs(*weights, [[0], [2], [1, 3]], [[0], [1], [2, 3]])
    layer_got = swap(layer13, 1, n_ex)
    grad_got = swap(grad23, 2, n_ex)
    layer_last = swap(add(layer2[0], layer_got[1]), 2, n_ex)
    grad_last = swap(add(grad1[0], grad_got[1]), 1, n_ex)
    layer, grad = add(layer0[0], layer_got[0], layer_last), add(grad0[0], grad_got[0], grad_last)
    return layer, grad, [layer_last, grad_last]


def fold_kernel(gu_mine, gu_got, row_mine, row_got, *refs):
    out = refs[-1]
    step = pl.program_id(0)

    def put(mine, got):
        value = (mine.astype(F32) + got.astype(F32)).astype(BF16)
        rows, columns = value.shape
        for i in range(columns // LANES):
            out[0, i * rows : (i + 1) * rows, :] = value[:, i * LANES : (i + 1) * LANES]

    @pl.when(step < 2)
    def _():
        put(gu_mine[0, 0], gu_got[0, 0])

    @pl.when(step == 2)
    def _():
        put(row_mine[0], row_got[0])


def fold(gu_mine, gu_got, row_mine, row_got, gu_at, row_at, piece, pieces, after):
    _, _, shard, units = gu_mine.shape
    _, row_shard, width = row_mine.shape
    per = shard * units // LANES // pieces
    gu = pl.BlockSpec((1, 1, shard, units // pieces), lambda j: (gu_at, jnp.minimum(j, 1), 0, piece))
    row = pl.BlockSpec((1, row_shard, width // pieces), lambda j: (row_at, 0, piece))
    return pl.pallas_call(
        fold_kernel,
        grid=(3,),
        in_specs=[gu, gu, row, row] + [hbm()] * len(after),
        out_specs=pl.BlockSpec((1, per, LANES), lambda j: (j, 0, 0)),
        out_shape=jax.ShapeDtypeStruct((3, per, LANES), BF16),
        compiler_params=params(16),
        cost_estimate=cost(6 * per * LANES, 18 * per * LANES),
        name="fold",
    )(gu_mine, gu_got, row_mine, row_got, *after)


def pass_on_kernel(own, got, *refs):
    refs[-1][...] = (own[...].astype(F32) + got[...].astype(F32)).astype(BF16)


def pass_on(own, got, piece, pieces, whole, after, weight=1):
    per = whole // pieces

    def part(array):
        at = piece if array.shape[1] > per else 0
        return pl.BlockSpec((1, per, LANES), lambda j: (j, at, 0))

    return pl.pallas_call(
        pass_on_kernel,
        grid=(got.shape[0],),
        in_specs=[part(own), part(got)] + [hbm()] * len(after),
        out_specs=pl.BlockSpec((1, per, LANES), lambda j: (j, 0, 0)),
        out_shape=jax.ShapeDtypeStruct((got.shape[0], per, LANES), BF16),
        compiler_params=params(16),
        cost_estimate=cost(2 * weight * got.size, 6 * weight * got.size),
        name="pass_on",
    )(own, got, *after)


def choose_kernel(place_ref, one, other, *refs):
    refs[-1][...] = jnp.where(place_ref[0] > 0, one[...].astype(F32), other[...].astype(F32)).astype(BF16)


def choose(place, one, other, after):
    block = pl.BlockSpec((1,) + one.shape[1:], lambda j, place: (j, 0, 0))
    return pl.pallas_call(
        choose_kernel,
        grid_spec=pltpu.PrefetchScalarGridSpec(
            num_scalar_prefetch=1,
            grid=(one.shape[0],),
            in_specs=[block, block] + [hbm()] * len(after),
            out_specs=block,
        ),
        out_shape=jax.ShapeDtypeStruct(one.shape, BF16),
        compiler_params=params(16),
        cost_estimate=cost(one.size, 6 * one.size),
        name="choose",
    )(place.reshape(1).astype(jnp.int32), one, other, *after)


def unfold_kernel(counts, *refs):
    parts, outs = refs[: sum(counts)], refs[sum(counts) :]
    total, at = None, 0
    for count in counts:
        pieces = [part[0].astype(F32) for part in parts[at : at + count]]
        value = pieces[0] if count == 1 else jnp.concatenate(pieces, axis=0)
        total = value if total is None else total + value
        at += count
    total = total.astype(BF16)
    for j, out in enumerate(outs):

        @pl.when(pl.program_id(0) == j)
        def _(out=out):
            rows, columns = out.shape[1:]
            for i in range(columns // LANES):
                out[0, :, i * LANES : (i + 1) * LANES] = total[i * rows : (i + 1) * rows]


def unfold(groups, shapes):
    parts = [part for group in groups for part in group]
    return pl.pallas_call(
        functools.partial(unfold_kernel, [len(group) for group in groups]),
        grid=(3,),
        in_specs=[pl.BlockSpec((1,) + part.shape[1:], lambda j: (j, 0, 0)) for part in parts],
        out_specs=[pl.BlockSpec(shape, lambda j: (0, 0, 0)) for shape in shapes],
        out_shape=[jax.ShapeDtypeStruct(shape, BF16) for shape in shapes],
        compiler_params=params(24),
        cost_estimate=cost(4 * parts[0].size, 10 * parts[0].size),
        name="unfold",
    )(*parts)


def chips_permute(value, pairs, n_dp):
    return lax.ppermute(value, "dp", [(CORES * a + c, CORES * b + c) for a, b in pairs for c in range(CORES)])


def on_device(
    gen_rows, gen_lengths, gen_adv, destination, expert_ids, gate_values, cotangent, w_gate, w_up, w_down
):
    n_dp = lax.axis_size("dp")
    n_ex = lax.axis_size("expert")
    n_z = n_dp // CORES
    size = cotangent.shape[0]
    slot = gen_rows.shape[0] // destination.shape[2]
    weight_gate, weight_up, weight_down = w_gate[0], w_up[0], w_down[0]
    g = lax.axis_index("dp")
    z = g // CORES
    near = jnp.minimum(z, n_z - 1 - z)
    other_core = [(d, d ^ 1) for d in range(n_dp)]

    def swap_core(value):
        return lax.ppermute(value, "dp", other_core)

    pieces = send_sequences(gen_rows, gen_lengths, gen_adv, destination, n_dp)
    cot_pieces = gather_rows(tie(cotangent, pieces[0]), n_ex)
    mine, other = regroup(pieces, cot_pieces[1:3])
    other = swap_core(other)
    low, high = place_sequences(mine, other, n_dp, destination.shape[2], expert_ids, gate_values)
    hg, dy_all = hidden_grad(cot_pieces, weight_down)
    x_pieces = gather_halves(low, high, n_ex, hg)
    early, late = with_last(x_pieces, size)
    before = hidden_units(early, weight_gate, weight_up, hg, slot, n_dp)
    gate_grad, up_grad, hid, turned_hs, turned_x, gates = hidden_units(
        late, weight_gate, weight_up, hg, slot, n_dp, before
    )

    far = n_z - 1
    rest = list(range(far - 1, -1, -1))
    far_other, far_mine = far_grads(turned_x, gate_grad, up_grad, n_dp)
    far_got = swap_core(far_other)
    row_other, row_mine = row_grad(tie(turned_hs, far_other), dy_all, n_dp)
    row_got = swap_core(row_other)
    whole = w_gate.shape[1] * w_gate.shape[2] // n_dp // LANES
    far_sum = fold(far_mine[None], far_got[None], row_mine, row_got, 0, 0, 0, 1, [])
    rest_other, rest_mine = rest_grads(turned_x, gate_grad, up_grad, far_got, n_dp)
    rest_got = swap_core(rest_other)

    def block(k, *after):
        return fold(rest_mine, rest_got, row_mine, row_got, far - 1 - k, far - k, 0, 1, after)

    if n_z == 4:
        outward, across = [(0, 1), (3, 2)], [(0, 1), (1, 0), (2, 3), (3, 2)]
        three = chips_permute(far_sum, outward, n_dp)
        sum_two = block(2)
        two = chips_permute(sum_two, outward, n_dp)
        sum_one, sum_none = block(1), block(0)
        three_sum = pass_on(far_sum, three, 0, 1, whole, [sum_two])
        three_on = chips_permute(three_sum, [(1, 3), (2, 0)], n_dp)
        two_sum = pass_on(sum_two, two, 0, 1, whole, [])
        two_on = chips_permute(tie(two_sum, three_on), [(1, 2), (2, 1)], n_dp)
        last = chips_permute(choose(near, sum_none, sum_one, [two]), across, n_dp)
        own = add(jnp.where(near > 0, sum_one, sum_none), three_on)
        ends = [[last], [two_on]]
    else:
        sums = [block(k) for k in range(far)] + [far_sum]
        passed, ends = {}, []
        for link in range(far):
            for d in range(far, link, -1):
                value = sums[d if link < n_z // 2 else far - d]
                if link > 0:
                    value = pass_on(value, passed[link - 1, d], 0, 1, whole, [])
                pairs = [(link, link + 1), (far - link, far - 1 - link)]
                passed[link, d] = chips_permute(value, pairs, n_dp)
                if d == link + 1:
                    ends.append([passed[link, d]])
        own = sums[0]
        for k in range(1, (n_z + 1) // 2):
            own = jnp.where(near == k, sums[k], own)
    shapes = [(1, w_gate.shape[1] // n_dp, w_gate.shape[2])] * 2 + [(1, w_down.shape[1] // n_dp, w_down.shape[2])]
    totals = unfold([[own]] + ends, shapes)

    layer_out, input_grad, _ = outputs_home(
        hid, gates, gate_grad, up_grad, weight_down, weight_gate, weight_up, far_sum, n_ex
    )
    return layer_out, input_grad, *totals


def solution(mesh):
    rows = P(("dp", "expert"), None)
    seqs = P("dp", "expert", None)
    weights = P("expert", None, None)
    shards = P("expert", "dp", None)
    return jax.shard_map(
        on_device,
        mesh=mesh,
        in_specs=(rows, seqs, seqs, seqs, rows, rows, rows, weights, weights, weights),
        out_specs=(rows, rows, shards, shards, shards),
        check_vma=False,
    )
```

```python
import functools
import math

import jax
import jax.numpy as jnp
from jax import lax
from jax.experimental import pallas as pl
from jax.experimental.pallas import tpu as pltpu
from jax.sharding import PartitionSpec as P

CORES = 2
LANES = 128
F32 = jnp.float32
BF16 = jnp.bfloat16
MIB = 1 << 20
PIECES = 1
BIG = 24


def contract(left, right, left_dim, right_dim):
    return lax.dot_general(left, right, (((left_dim,), (right_dim,)), ((), ())), preferred_element_type=F32)


def params(mib, **more):
    return pltpu.CompilerParams(vmem_limit_bytes=mib * MIB, **more)


def room(rows, width):
    return 16 + rows * width * 10 // MIB


def cost(flops, bytes_accessed):
    return pl.CostEstimate(flops=flops, bytes_accessed=bytes_accessed, transcendentals=0)


def vmem():
    return pl.BlockSpec(memory_space=pltpu.VMEM)


def in_hbm(value):
    return pltpu.with_memory_space_constraint(value, pltpu.HBM)


def hbm():
    return pl.BlockSpec(memory_space=pl.ANY)


LENGTH, ADV, GATES = 0, 1, 2
PARTS = 3


def pick_kernel(n_dp, dest_hbm, len_hbm, adv_hbm, rows_hbm, *refs):
    outs, (dest_ref, len_ref, adv_ref, sems, row_sems) = refs[:-5], refs[-5:]
    small = [
        pltpu.make_async_copy(source, target, sems.at[i])
        for i, (source, target) in enumerate(((dest_hbm, dest_ref), (len_hbm, len_ref), (adv_hbm, adv_ref)))
    ]
    for copy in small:
        copy.start()
    seqs, slot, width = rows_hbm.shape
    lane = lax.broadcasted_iota(jnp.int32, (slot, LANES), 1)
    which = lax.broadcasted_iota(jnp.int32, (1, seqs), 1)
    me = lax.axis_index("dp")
    small[0].wait()
    found, copies = [], []
    for i in range(n_dp):
        out = outs[i // CORES]
        here = pl.ds(i % CORES * slot, slot)
        seq = jnp.int32(0)
        live = jnp.int32(0)
        for s in range(seqs):
            hit = dest_ref[0, 0, s] == (me ^ i)
            seq = jnp.where(hit, s, seq)
            live = jnp.where(hit, 1, live)
        found.append((seq, live))
        copies.append(pltpu.make_async_copy(rows_hbm.at[seq], out.at[here, pl.ds(0, width)], row_sems.at[i]))
        copies[-1].start()
    small[1].wait()
    small[2].wait()
    lengths = len_ref[0].astype(F32)
    advs = adv_ref[0].astype(F32)
    for i, (seq, live) in enumerate(found):
        mine = (which == seq) & (live == 1)
        length = jnp.sum(jnp.where(mine, lengths, 0.0), axis=1, keepdims=True)
        adv = jnp.sum(jnp.where(mine, advs, 0.0), axis=1, keepdims=True)
        value = jnp.where(lane == LENGTH, length, jnp.where(lane == ADV, adv, 0.0)).astype(BF16)
        outs[i // CORES][i % CORES * slot : (i % CORES + 1) * slot, width:] = value
    for copy in copies:
        copy.wait()


def pick(dest, lengths, adv, rows, n_dp):
    seqs, slot, width = rows.shape
    return pl.pallas_call(
        functools.partial(pick_kernel, n_dp),
        out_shape=[jax.ShapeDtypeStruct((CORES * slot, width + LANES), BF16)] * (n_dp // CORES),
        in_specs=[hbm()] * 4,
        out_specs=[vmem()] * (n_dp // CORES),
        scratch_shapes=[
            pltpu.SMEM(dest.shape, jnp.int32),
            pltpu.VMEM(lengths.shape, lengths.dtype),
            pltpu.VMEM(adv.shape, adv.dtype),
            pltpu.SemaphoreType.DMA((3,)),
            pltpu.SemaphoreType.DMA((n_dp,)),
        ],
        compiler_params=params(16),
        name="pick",
    )(*[in_hbm(value) for value in (dest, lengths, adv, rows)])


def gate_notes(ids, gates):
    note = lax.broadcasted_iota(jnp.int32, (LANES, ids.shape[1]), 0) - GATES
    expert, part = note // PARTS, note % PARTS
    value = jnp.zeros(note.shape, F32)
    for k in range(ids.shape[0]):
        value = value + jnp.where(ids[k : k + 1] == expert, gates[k : k + 1], 0.0)
    value = jnp.where(note < 0, 0.0, value)
    high = value.astype(BF16).astype(F32)
    middle = (value - high).astype(BF16).astype(F32)
    low = value - high - middle
    return jnp.where(part == 0, high, jnp.where(part == 1, middle, low))


def regroup_kernel(count, *refs):
    pieces, (mine, other) = refs[:count], refs[-2:]
    slot = pieces[0].shape[0] // CORES
    for i, piece in enumerate(pieces):
        mine[i * slot : (i + 1) * slot, :] = piece[:slot]
        other[i * slot : (i + 1) * slot, :] = piece[slot:]


def regroup(pieces, after):
    rows, wide = pieces[0].shape
    count = len(pieces)
    out = jax.ShapeDtypeStruct((count * rows // CORES, wide), BF16)
    return pl.pallas_call(
        functools.partial(regroup_kernel, count),
        out_shape=[out, out],
        in_specs=[vmem()] * count + [hbm()] * len(after),
        out_specs=[vmem()] * 2,
        compiler_params=params(16),
        name="regroup",
    )(*pieces, *after)


def assemble_kernel(slot, ids_ref, gates_ref, mine, other, *halves):
    rows, wide = halves[0].shape
    width = wide - LANES
    per_half = rows // slot
    me = lax.axis_index("dp")
    notes = gate_notes(ids_ref[...], gates_ref[...]).T
    for i in range(CORES * per_half):
        piece = (mine, other)[i % CORES][i // CORES * slot : (i // CORES + 1) * slot, :]
        place = me ^ i
        at = pl.multiple_of((place % per_half) * slot, slot)
        for h, half in enumerate(halves):

            @pl.when(place // per_half == h)
            def _(piece=piece, half=half, at=at):
                half[pl.ds(at, slot), :] = piece

    for h, half in enumerate(halves):
        own = notes[h * rows : (h + 1) * rows]
        half[:, width:] = (half[:, width:].astype(F32) + own).astype(BF16)


def assemble(mine, other, slot, ids, gates):
    return pl.pallas_call(
        functools.partial(assemble_kernel, slot),
        out_shape=[jax.ShapeDtypeStruct(mine.shape, BF16)] * 2,
        in_specs=[vmem()] * 4,
        out_specs=[vmem()] * 2,
        compiler_params=params(16),
        name="assemble",
    )(ids, gates, mine, other)


def send_sequences(gen_rows, gen_lengths, gen_adv, destination, n_dp):
    seq_dev = destination.shape[2]
    slot = gen_rows.shape[0] // seq_dev
    pieces = list(pick(destination, gen_lengths, gen_adv, gen_rows.reshape(seq_dev, slot, gen_rows.shape[1]), n_dp))
    for i in range(1, len(pieces)):
        pieces[i] = lax.ppermute(pieces[i], "dp", [(d, d ^ (CORES * i)) for d in range(n_dp)])
    return pieces


def place_sequences(mine, other, n_dp, seq_dev, ids, gates):
    slot = CORES * mine.shape[0] // n_dp
    if n_dp == seq_dev:
        return assemble(mine, other, slot, ids.T, gates.T)
    wide = mine.shape[1]
    width = wide - LANES
    g = lax.axis_index("dp")
    stack = jnp.stack([mine.reshape(-1, slot, wide), other.reshape(-1, slot, wide)], axis=1)
    stack = stack.reshape(n_dp, slot, wide)[jnp.arange(n_dp, dtype=jnp.int32) ^ g]
    arrived = stack[:, 0, width + LENGTH] > 0
    arrival = jnp.cumsum(arrived.astype(jnp.int32)) - 1
    chosen = arrived[None, :] & (arrival[None, :] == jnp.arange(seq_dev, dtype=jnp.int32)[:, None])
    from_peer = jnp.sum(jnp.where(chosen, jnp.arange(n_dp, dtype=jnp.int32)[None, :], 0), axis=1)
    x = stack[from_peer].reshape(seq_dev * slot, wide)
    notes = (x[:, width:].astype(F32) + gate_notes(ids.T, gates.T).T).astype(BF16)
    x = jnp.concatenate([x[:, :width], notes], axis=1)
    half = x.shape[0] // 2
    return x[:half], x[half:]


def swap(value, i, n_ex):
    return lax.ppermute(value, "expert", [(d, d ^ i) for d in range(n_ex)])


def gather_rows(rows, n_ex):
    if n_ex != 4:
        return [rows] + [swap(rows, i, n_ex) for i in range(1, n_ex)]
    half = rows.shape[0] // 2
    first = swap(rows, 1, n_ex)
    second = swap(rows, 2, n_ex)
    return [rows, first, second, swap(first[:half], 2, n_ex), swap(second[half:], 1, n_ex)]


def gather_halves(low, high, n_ex, between):
    if n_ex != 4:
        pieces = [low, high]
        for i in range(1, n_ex):
            pieces += [swap(low, i, n_ex), swap(high, i, n_ex)]
        return pieces
    first_low, second_high = swap(low, 1, n_ex), swap(high, 2, n_ex)
    first_high, second_low = swap(high, 1, n_ex), swap(low, 2, n_ex)
    on_low, on_high, _ = lax.optimization_barrier((first_low, second_high, between))
    return [low, high, first_low, first_high, second_low, second_high, swap(on_low, 2, n_ex), swap(on_high, 1, n_ex)]


def with_last(pieces, size):
    at, cut = 0, sum(p.shape[0] for p in pieces) - size
    for i, piece in enumerate(pieces):
        if at == cut:
            return pieces[:i], pieces[i:]
        at += piece.shape[0]


def tie(value, *others):
    return lax.optimization_barrier((value,) + others)[0]


def load_pieces(pieces, whole, sems):
    at, copies = 0, []
    for i, piece in enumerate(pieces):
        size = piece.shape[0]
        copies.append(pltpu.make_async_copy(piece, whole.at[pl.ds(at, size)], sems.at[i]))
        at += size
    for copy in copies:
        copy.start()
    for copy in copies:
        copy.wait()


def hidden_grad_kernel(count, w_ref, *refs):
    pieces, (out, whole_out, whole, sems, out_sem) = refs[:count], refs[count:]
    step = pl.program_id(0)

    @pl.when(step == 0)
    def _():
        load_pieces(pieces, whole, sems)
        pltpu.make_async_copy(whole, whole_out, out_sem).start()

    out[...] = contract(whole[...], w_ref[...], 1, 1)

    @pl.when(step == pl.num_programs(0) - 1)
    def _():
        pltpu.make_async_copy(whole, whole_out, out_sem).wait()


def hidden_grad(pieces, w_down):
    rows = sum(p.shape[0] for p in pieces)
    units, width = w_down.shape
    tile = 256
    return pl.pallas_call(
        functools.partial(hidden_grad_kernel, len(pieces)),
        grid=(units // tile,),
        out_shape=[jax.ShapeDtypeStruct((rows, units), F32), jax.ShapeDtypeStruct((rows, width), BF16)],
        in_specs=[pl.BlockSpec((tile, width), lambda j: (j, 0))] + [hbm()] * len(pieces),
        out_specs=[pl.BlockSpec((rows, tile), lambda j: (0, j)), hbm()],
        scratch_shapes=[
            pltpu.VMEM((rows, width), BF16),
            pltpu.SemaphoreType.DMA((len(pieces),)),
            pltpu.SemaphoreType.DMA,
        ],
        compiler_params=params(BIG),
        cost_estimate=cost(2 * rows * units * width, 2 * units * width + 4 * rows * width),
        name="hidden_grad",
    )(w_down, *pieces)


def shard_place(shard, n_dp):
    me = lax.axis_index("dp")
    n_z = n_dp // CORES
    chip, core = shard // CORES, shard % CORES
    at = jnp.where(me // CORES >= n_z // 2, chip, n_z - 1 - chip)
    return jnp.where(core == me % CORES, n_z, 0) + at


def units_kernel(count, slot, first, n_dp, wg_ref, wu_ref, hg_ref, *refs):
    if not first:
        refs = refs[6:]
    pieces, refs = refs[:count], refs[count:]
    gate_out, up_out, hid_out, turned_hs, turned_x, gates_out, whole, gs_ref, sems = refs
    step = pl.program_id(0)
    rows, wide = whole.shape
    width = wide - LANES

    @pl.when(step == 0)
    def _():
        load_pieces(pieces, whole, sems)
        notes = whole[:, width:].astype(F32)
        lane = lax.broadcasted_iota(jnp.int32, notes.shape, 1) - GATES - PARTS * lax.axis_index("expert")
        gates = jnp.sum(jnp.where((lane >= 0) & (lane < PARTS), notes, 0.0), axis=1, keepdims=True)
        length, adv = notes[:, LENGTH : LENGTH + 1], notes[:, ADV : ADV + 1]
        position = lax.broadcasted_iota(jnp.int32, (rows, 1), 0) % slot
        gates_out[...] = gates
        gs_ref[...] = jnp.where(position.astype(F32) < length, gates * (adv / length), 0.0)
        strip = width // n_dp
        for i in range(n_dp):
            at = pl.multiple_of(shard_place(i, n_dp) * strip, strip)
            turned_x[pl.ds(at, strip), :] = whole[:, i * strip : (i + 1) * strip].T

    x = whole[:, :width]
    here = pl.ds(pl.multiple_of(step * gate_out.shape[1], LANES), gate_out.shape[1])
    gate = jnp.dot(x, wg_ref[:, here], preferred_element_type=F32)
    up = jnp.dot(x, wu_ref[:, here], preferred_element_type=F32)
    gs = gs_ref[...]
    sig = jax.nn.sigmoid(gate)
    act = gate * sig
    hid = (act * up).astype(BF16)
    hid_out[...] = hid
    turned = (hid.astype(F32) * gs).astype(BF16).T
    tile, shard = turned.shape[0], turned_hs.shape[0] // n_dp
    chunk = math.gcd(tile, shard)
    for i in range(tile // chunk):
        row = step * tile + i * chunk
        at = shard_place(row // shard, n_dp) * shard + row % shard
        turned_hs[pl.ds(pl.multiple_of(at, chunk), chunk), :] = turned[i * chunk : (i + 1) * chunk]
    hg = hg_ref[...] * gs
    gate_out[...] = (hg * up * sig * (1.0 + gate * (1.0 - sig))).astype(BF16)
    up_out[...] = (hg * act).astype(BF16)


def hidden_units(pieces, w_gate, w_up, hg, slot, n_dp, before=None):
    total, units = hg.shape
    width = w_gate.shape[0]
    rows = sum(p.shape[0] for p in pieces)
    tile = 256
    at = 0 if before is None else total // rows - 1
    columns = pl.BlockSpec((rows, tile), lambda j: (at, j))
    weights = vmem()
    before = before or []
    return pl.pallas_call(
        functools.partial(units_kernel, len(pieces), slot, not before, n_dp),
        grid=(units // tile,),
        out_shape=[jax.ShapeDtypeStruct((total, units), BF16)] * 3
        + [
            jax.ShapeDtypeStruct((units, total), BF16),
            jax.ShapeDtypeStruct((width, total), BF16),
            jax.ShapeDtypeStruct((total, 1), F32),
        ],
        in_specs=[weights, weights, columns] + [hbm()] * (len(before) + len(pieces)),
        out_specs=[columns] * 3
        + [
            pl.BlockSpec((units, rows), lambda j: (0, at)),
            pl.BlockSpec((width, rows), lambda j: (0, at)),
            pl.BlockSpec((rows, 1), lambda j: (at, 0)),
        ],
        scratch_shapes=[
            pltpu.VMEM((rows, width + LANES), BF16),
            pltpu.VMEM((rows, 1), F32),
            pltpu.SemaphoreType.DMA((len(pieces),)),
        ],
        input_output_aliases={3 + i: i for i in range(len(before))},
        compiler_params=params(room(rows, width)),
        cost_estimate=cost(4 * rows * units * width, 4 * units * width + 4 * rows * width),
        name="hidden_units",
    )(w_gate, w_up, hg, *before, *pieces)


def far_grads_kernel(x_ref, gate_ref, up_ref, other, mine):
    gate = jnp.dot(x_ref[...], gate_ref[...], preferred_element_type=F32).astype(BF16)
    up = jnp.dot(x_ref[...], up_ref[...], preferred_element_type=F32).astype(BF16)

    @pl.when(pl.program_id(0) == 0)
    def _():
        other[0] = gate
        other[1] = up

    @pl.when(pl.program_id(0) == 1)
    def _():
        mine[0] = gate
        mine[1] = up


def far_grads(turned_x, gate_grad, up_grad, n_dp):
    rows, units = gate_grad.shape
    width = turned_x.shape[0]
    n_z, shard = n_dp // CORES, width // n_dp
    out = pl.BlockSpec((2, shard, units), lambda k: (0, 0, 0))
    whole = pl.BlockSpec((rows, units), lambda k: (0, 0))
    return pl.pallas_call(
        far_grads_kernel,
        grid=(CORES,),
        in_specs=[pl.BlockSpec((shard, rows), lambda k: (k * n_z, 0)), whole, whole],
        out_specs=[out, out],
        out_shape=[pltpu.HBM((2, shard, units), BF16)] * 2,
        compiler_params=params(BIG),
        cost_estimate=cost(8 * rows * units * shard, 16 * units * shard + 4 * rows * units),
        name="far_grads",
    )(turned_x, gate_grad, up_grad)


def rest_grads_kernel(shard, x_ref, gate_ref, up_ref, _, other, mine):
    count = other.shape[0]
    for k, out in enumerate((other, mine)):
        x = x_ref[pl.ds((k * (count + 1) + 1) * shard, count * shard), :]
        for p, grad in enumerate((gate_ref, up_ref)):
            value = jnp.dot(x, grad[...], preferred_element_type=F32).astype(BF16)
            for b in range(count):
                out[b, p] = value[b * shard : (b + 1) * shard]


def rest_grads(turned_x, gate_grad, up_grad, after, n_dp):
    rows, units = gate_grad.shape
    width = turned_x.shape[0]
    n_z, shard = n_dp // CORES, width // n_dp
    tile = 256
    columns = pl.BlockSpec((rows, tile), lambda j: (0, j))
    out = pl.BlockSpec((n_z - 1, 2, shard, tile), lambda j: (0, 0, 0, j))
    return pl.pallas_call(
        functools.partial(rest_grads_kernel, shard),
        grid=(units // tile,),
        in_specs=[pl.BlockSpec((width, rows), lambda j: (0, 0)), columns, columns, hbm()],
        out_specs=[out, out],
        out_shape=[pltpu.HBM((n_z - 1, 2, shard, units), BF16)] * 2,
        compiler_params=params(room(rows, width)),
        cost_estimate=cost(4 * rows * units * width, 4 * units * width + 4 * rows * units),
        name="rest_grads",
    )(turned_x, gate_grad, up_grad, after)


def row_grad_kernel(hid_ref, dy_ref, other, mine):
    n_z, shard, tile = mine.shape
    value = jnp.dot(hid_ref[...], dy_ref[...], preferred_element_type=F32).astype(BF16)
    for k, out in enumerate((other, mine)):
        for b in range(n_z):
            at = (k * n_z + b) * shard
            out[b] = value[at : at + shard]


def row_grad(turned_hid, dy, n_dp):
    units, rows = turned_hid.shape
    width = dy.shape[1]
    n_z, shard = n_dp // CORES, units // n_dp
    tile = 512
    block = pl.BlockSpec((n_z, shard, tile), lambda j: (0, 0, j))
    return pl.pallas_call(
        row_grad_kernel,
        grid=(width // tile,),
        in_specs=[pl.BlockSpec((units, rows), lambda j: (0, 0)), pl.BlockSpec((rows, tile), lambda j: (0, j))],
        out_specs=[block, block],
        out_shape=[pltpu.HBM((n_z, shard, width), BF16)] * 2,
        compiler_params=params(BIG),
        cost_estimate=cost(2 * rows * units * width, 2 * units * width + 2 * rows * width),
        name="row_grad",
    )(turned_hid, dy)


def outputs_kernel(layer_groups, grad_groups, hid_ref, gates_ref, gate_ref, up_ref, wd_ref, wg_ref, wu_ref, _, *outs):
    layer = jnp.dot(hid_ref[...], wd_ref[...], preferred_element_type=F32) * gates_ref[...]
    value = contract(gate_ref[...], wg_ref[...], 1, 1) + contract(up_ref[...], wu_ref[...], 1, 1)
    size = outs[0].shape[1]
    for result, groups, refs in (
        (layer.astype(BF16), layer_groups, outs[: len(layer_groups)]),
        (value.astype(BF16), grad_groups, outs[len(layer_groups) :]),
    ):
        for group, out in zip(groups, refs):
            for n, i in enumerate(group):
                out[n] = result[i * size : (i + 1) * size]


def outputs(hid, gates, gate_grad, up_grad, w_down, w_gate, w_up, after, n_ex, layer_groups, grad_groups):
    rows, units = hid.shape
    width = w_down.shape[1]
    tile = 512
    size = rows // n_ex
    whole = pl.BlockSpec((rows, units), lambda j: (0, 0))
    columns = pl.BlockSpec((units, tile), lambda j: (0, j))
    weights = pl.BlockSpec((tile, units), lambda j: (j, 0))
    counts = [len(group) for group in layer_groups + grad_groups]
    return pl.pallas_call(
        functools.partial(outputs_kernel, layer_groups, grad_groups),
        grid=(width // tile,),
        out_shape=[jax.ShapeDtypeStruct((n, size, width), BF16) for n in counts],
        in_specs=[whole, pl.BlockSpec((rows, 1), lambda j: (0, 0)), whole, whole, columns, weights, weights, hbm()],
        out_specs=[pl.BlockSpec((n, size, tile), lambda j: (0, 0, j)) for n in counts],
        compiler_params=params(room(rows, width)),
        cost_estimate=cost(6 * rows * units * width, 6 * units * width + 4 * rows * width),
        name="outputs",
    )(hid, gates, gate_grad, up_grad, w_down, w_gate, w_up, after)


def add(*parts):
    return sum(part.astype(F32) for part in parts).astype(BF16)


def outputs_home(hid, gates, gate_grad, up_grad, w_down, w_gate, w_up, after, n_ex):
    weights = (hid, gates, gate_grad, up_grad, w_down, w_gate, w_up, after, n_ex)
    if n_ex != 4:
        single = [[i] for i in range(n_ex)]
        parts = outputs(*weights, single, single)
        layer, grad = [], []
        for i in range(n_ex):
            layer.append(swap(parts[i][0], i, n_ex) if i else parts[i][0])
            grad.append(swap(parts[n_ex + i][0], i, n_ex) if i else parts[n_ex + i][0])
        return add(*layer), add(*grad), []
    layer0, layer2, layer13, grad0, grad1, grad23 = outputs(*weights, [[0], [2], [1, 3]], [[0], [1], [2, 3]])
    layer_got = swap(layer13, 1, n_ex)
    grad_got = swap(grad23, 2, n_ex)
    layer_last = swap(add(layer2[0], layer_got[1]), 2, n_ex)
    grad_last = swap(add(grad1[0], grad_got[1]), 1, n_ex)
    layer, grad = add(layer0[0], layer_got[0], layer_last), add(grad0[0], grad_got[0], grad_last)
    return layer, grad, [layer_last, grad_last]


def fold_kernel(gu_mine, gu_got, row_mine, row_got, *refs):
    out = refs[-1]
    step = pl.program_id(0)

    def put(mine, got):
        value = (mine.astype(F32) + got.astype(F32)).astype(BF16)
        rows, columns = value.shape
        for i in range(columns // LANES):
            out[0, i * rows : (i + 1) * rows, :] = value[:, i * LANES : (i + 1) * LANES]

    @pl.when(step < 2)
    def _():
        put(gu_mine[0, 0], gu_got[0, 0])

    @pl.when(step == 2)
    def _():
        put(row_mine[0], row_got[0])


def fold(gu_mine, gu_got, row_mine, row_got, gu_at, row_at, piece, pieces, after):
    _, _, shard, units = gu_mine.shape
    _, row_shard, width = row_mine.shape
    per = shard * units // LANES // pieces
    gu = pl.BlockSpec((1, 1, shard, units // pieces), lambda j: (gu_at, jnp.minimum(j, 1), 0, piece))
    row = pl.BlockSpec((1, row_shard, width // pieces), lambda j: (row_at, 0, piece))
    return pl.pallas_call(
        fold_kernel,
        grid=(3,),
        in_specs=[gu, gu, row, row] + [hbm()] * len(after),
        out_specs=pl.BlockSpec((1, per, LANES), lambda j: (j, 0, 0)),
        out_shape=jax.ShapeDtypeStruct((3, per, LANES), BF16),
        compiler_params=params(16),
        cost_estimate=cost(6 * per * LANES, 18 * per * LANES),
        name="fold",
    )(gu_mine, gu_got, row_mine, row_got, *after)


def pass_on_kernel(own, got, *refs):
    refs[-1][...] = (own[...].astype(F32) + got[...].astype(F32)).astype(BF16)


def pass_on(own, got, piece, pieces, whole, after, weight=1):
    per, count = whole // pieces, got.shape[0]

    def part(array):
        at = piece if array.shape[1] > per else 0
        return pl.BlockSpec((count, per, LANES), lambda j: (0, at, 0))

    return pl.pallas_call(
        pass_on_kernel,
        grid=(1,),
        in_specs=[part(own), part(got)] + [hbm()] * len(after),
        out_specs=pl.BlockSpec((count, per, LANES), lambda j: (0, 0, 0)),
        out_shape=jax.ShapeDtypeStruct((count, per, LANES), BF16),
        compiler_params=params(16),
        cost_estimate=cost(2 * weight * got.size, 6 * weight * got.size),
        name="pass_on",
    )(own, got, *after)


def choose_kernel(place_ref, one, other, *refs):
    refs[-1][...] = jnp.where(place_ref[0] > 0, one[...].astype(F32), other[...].astype(F32)).astype(BF16)


def choose(place, one, other, after):
    block = pl.BlockSpec((1,) + one.shape[1:], lambda j, place: (j, 0, 0))
    return pl.pallas_call(
        choose_kernel,
        grid_spec=pltpu.PrefetchScalarGridSpec(
            num_scalar_prefetch=1,
            grid=(one.shape[0],),
            in_specs=[block, block] + [hbm()] * len(after),
            out_specs=block,
        ),
        out_shape=jax.ShapeDtypeStruct(one.shape, BF16),
        compiler_params=params(16),
        cost_estimate=cost(one.size, 6 * one.size),
        name="choose",
    )(place.reshape(1).astype(jnp.int32), one, other, *after)


def unfold_kernel(counts, *refs):
    parts, outs = refs[: sum(counts)], refs[sum(counts) :]
    for j, out in enumerate(outs):
        total, at = None, 0
        for count in counts:
            pieces = [part[j].astype(F32) for part in parts[at : at + count]]
            value = pieces[0] if count == 1 else jnp.concatenate(pieces, axis=0)
            total = value if total is None else total + value
            at += count
        total = total.astype(BF16)
        rows, columns = out.shape[1:]
        for i in range(columns // LANES):
            out[0, :, i * LANES : (i + 1) * LANES] = total[i * rows : (i + 1) * rows]


def unfold(groups, shapes):
    parts = [part for group in groups for part in group]
    return pl.pallas_call(
        functools.partial(unfold_kernel, [len(group) for group in groups]),
        grid=(1,),
        in_specs=[pl.BlockSpec(part.shape, lambda j: (0, 0, 0)) for part in parts],
        out_specs=[pl.BlockSpec(shape, lambda j: (0, 0, 0)) for shape in shapes],
        out_shape=[jax.ShapeDtypeStruct(shape, BF16) for shape in shapes],
        compiler_params=params(24),
        cost_estimate=cost(4 * parts[0].size, 10 * parts[0].size),
        name="unfold",
    )(*parts)


def chips_permute(value, pairs, n_dp):
    return lax.ppermute(value, "dp", [(CORES * a + c, CORES * b + c) for a, b in pairs for c in range(CORES)])


def on_device(
    gen_rows, gen_lengths, gen_adv, destination, expert_ids, gate_values, cotangent, w_gate, w_up, w_down
):
    n_dp = lax.axis_size("dp")
    n_ex = lax.axis_size("expert")
    n_z = n_dp // CORES
    size = cotangent.shape[0]
    slot = gen_rows.shape[0] // destination.shape[2]
    weight_gate, weight_up, weight_down = w_gate[0], w_up[0], w_down[0]
    g = lax.axis_index("dp")
    z = g // CORES
    near = jnp.minimum(z, n_z - 1 - z)
    other_core = [(d, d ^ 1) for d in range(n_dp)]

    def swap_core(value):
        return lax.ppermute(value, "dp", other_core)

    pieces = send_sequences(gen_rows, gen_lengths, gen_adv, destination, n_dp)
    cot_pieces = gather_rows(tie(cotangent, pieces[0]), n_ex)
    mine, other = regroup(pieces, cot_pieces[1:3])
    other = swap_core(other)
    low, high = place_sequences(mine, other, n_dp, destination.shape[2], expert_ids, gate_values)
    hg, dy_all = hidden_grad(cot_pieces, weight_down)
    x_pieces = gather_halves(low, high, n_ex, hg)
    early, late = with_last(x_pieces, size)
    before = hidden_units(early, weight_gate, weight_up, hg, slot, n_dp)
    gate_grad, up_grad, hid, turned_hs, turned_x, gates = hidden_units(
        late, weight_gate, weight_up, hg, slot, n_dp, before
    )

    far = n_z - 1
    rest = list(range(far - 1, -1, -1))
    far_other, far_mine = far_grads(turned_x, gate_grad, up_grad, n_dp)
    far_got = swap_core(far_other)
    row_other, row_mine = row_grad(tie(turned_hs, far_other), dy_all, n_dp)
    row_got = swap_core(row_other)
    whole = w_gate.shape[1] * w_gate.shape[2] // n_dp // LANES
    far_sum = fold(far_mine[None], far_got[None], row_mine, row_got, 0, 0, 0, 1, [])
    rest_other, rest_mine = rest_grads(turned_x, gate_grad, up_grad, far_got, n_dp)
    rest_got = swap_core(rest_other)

    def block(k, *after):
        return fold(rest_mine, rest_got, row_mine, row_got, far - 1 - k, far - k, 0, 1, after)

    if n_z == 4:
        outward, across = [(0, 1), (3, 2)], [(0, 1), (1, 0), (2, 3), (3, 2)]
        three = chips_permute(far_sum, outward, n_dp)
        sum_two = block(2)
        two = chips_permute(sum_two, outward, n_dp)
        sum_one, sum_none = block(1), block(0)
        three_sum = pass_on(far_sum, three, 0, 1, whole, [sum_two])
        three_on = chips_permute(three_sum, [(1, 3), (2, 0)], n_dp)
        two_sum = pass_on(sum_two, two, 0, 1, whole, [])
        two_on = chips_permute(tie(two_sum, three_on), [(1, 2), (2, 1)], n_dp)
        last = chips_permute(choose(near, sum_none, sum_one, [two]), across, n_dp)
        own = add(jnp.where(near > 0, sum_one, sum_none), three_on)
        ends = [[last], [two_on]]
    else:
        sums = [block(k) for k in range(far)] + [far_sum]
        passed, ends = {}, []
        for link in range(far):
            for d in range(far, link, -1):
                value = sums[d if link < n_z // 2 else far - d]
                if link > 0:
                    value = pass_on(value, passed[link - 1, d], 0, 1, whole, [])
                pairs = [(link, link + 1), (far - link, far - 1 - link)]
                passed[link, d] = chips_permute(value, pairs, n_dp)
                if d == link + 1:
                    ends.append([passed[link, d]])
        own = sums[0]
        for k in range(1, (n_z + 1) // 2):
            own = jnp.where(near == k, sums[k], own)
    shapes = [(1, w_gate.shape[1] // n_dp, w_gate.shape[2])] * 2 + [(1, w_down.shape[1] // n_dp, w_down.shape[2])]
    totals = unfold([[own]] + ends, shapes)

    layer_out, input_grad, _ = outputs_home(
        hid, gates, gate_grad, up_grad, weight_down, weight_gate, weight_up, far_sum, n_ex
    )
    return layer_out, input_grad, *totals


def solution(mesh):
    rows = P(("dp", "expert"), None)
    seqs = P("dp", "expert", None)
    weights = P("expert", None, None)
    shards = P("expert", "dp", None)
    return jax.shard_map(
        on_device,
        mesh=mesh,
        in_specs=(rows, seqs, seqs, seqs, rows, rows, rows, weights, weights, weights),
        out_specs=(rows, rows, shards, shards, shards),
        check_vma=False,
    )
```

```python
import functools
import math

import jax
import jax.numpy as jnp
from jax import lax
from jax.experimental import pallas as pl
from jax.experimental.pallas import tpu as pltpu
from jax.sharding import PartitionSpec as P

CORES = 2
LANES = 128
F32 = jnp.float32
BF16 = jnp.bfloat16
MIB = 1 << 20
PIECES = 1
BIG = 24


def contract(left, right, left_dim, right_dim):
    return lax.dot_general(left, right, (((left_dim,), (right_dim,)), ((), ())), preferred_element_type=F32)


def params(mib, **more):
    return pltpu.CompilerParams(vmem_limit_bytes=mib * MIB, **more)


def room(rows, width):
    return 16 + rows * width * 10 // MIB


def cost(flops, bytes_accessed):
    return pl.CostEstimate(flops=flops, bytes_accessed=bytes_accessed, transcendentals=0)


def vmem():
    return pl.BlockSpec(memory_space=pltpu.VMEM)


def in_hbm(value):
    return pltpu.with_memory_space_constraint(value, pltpu.HBM)


def hbm():
    return pl.BlockSpec(memory_space=pl.ANY)


LENGTH, ADV, GATES = 0, 1, 2
PARTS = 3


def pick_kernel(n_dp, dest_hbm, len_hbm, adv_hbm, rows_hbm, *refs):
    outs, (dest_ref, len_ref, adv_ref, sems, row_sems) = refs[:-5], refs[-5:]
    small = [
        pltpu.make_async_copy(source, target, sems.at[i])
        for i, (source, target) in enumerate(((dest_hbm, dest_ref), (len_hbm, len_ref), (adv_hbm, adv_ref)))
    ]
    for copy in small:
        copy.start()
    seqs, slot, width = rows_hbm.shape
    lane = lax.broadcasted_iota(jnp.int32, (slot, LANES), 1)
    which = lax.broadcasted_iota(jnp.int32, (1, seqs), 1)
    me = lax.axis_index("dp")
    small[0].wait()
    found, copies = [], []
    for i in range(n_dp):
        out = outs[i // CORES]
        here = pl.ds(i % CORES * slot, slot)
        seq = jnp.int32(0)
        live = jnp.int32(0)
        for s in range(seqs):
            hit = dest_ref[0, 0, s] == (me ^ i)
            seq = jnp.where(hit, s, seq)
            live = jnp.where(hit, 1, live)
        found.append((seq, live))
        copies.append(pltpu.make_async_copy(rows_hbm.at[seq], out.at[here, pl.ds(0, width)], row_sems.at[i]))
        copies[-1].start()
    small[1].wait()
    small[2].wait()
    lengths = len_ref[0].astype(F32)
    advs = adv_ref[0].astype(F32)
    for i, (seq, live) in enumerate(found):
        mine = (which == seq) & (live == 1)
        length = jnp.sum(jnp.where(mine, lengths, 0.0), axis=1, keepdims=True)
        adv = jnp.sum(jnp.where(mine, advs, 0.0), axis=1, keepdims=True)
        value = jnp.where(lane == LENGTH, length, jnp.where(lane == ADV, adv, 0.0)).astype(BF16)
        outs[i // CORES][i % CORES * slot : (i % CORES + 1) * slot, width:] = value
    for copy in copies:
        copy.wait()


def pick(dest, lengths, adv, rows, n_dp):
    seqs, slot, width = rows.shape
    return pl.pallas_call(
        functools.partial(pick_kernel, n_dp),
        out_shape=[jax.ShapeDtypeStruct((CORES * slot, width + LANES), BF16)] * (n_dp // CORES),
        in_specs=[hbm()] * 4,
        out_specs=[vmem()] * (n_dp // CORES),
        scratch_shapes=[
            pltpu.SMEM(dest.shape, jnp.int32),
            pltpu.VMEM(lengths.shape, lengths.dtype),
            pltpu.VMEM(adv.shape, adv.dtype),
            pltpu.SemaphoreType.DMA((3,)),
            pltpu.SemaphoreType.DMA((n_dp,)),
        ],
        compiler_params=params(16),
        name="pick",
    )(*[in_hbm(value) for value in (dest, lengths, adv, rows)])


def gate_notes(ids, gates):
    note = lax.broadcasted_iota(jnp.int32, (LANES, ids.shape[1]), 0) - GATES
    expert, part = note // PARTS, note % PARTS
    value = jnp.zeros(note.shape, F32)
    for k in range(ids.shape[0]):
        value = value + jnp.where(ids[k : k + 1] == expert, gates[k : k + 1], 0.0)
    value = jnp.where(note < 0, 0.0, value)
    high = value.astype(BF16).astype(F32)
    middle = (value - high).astype(BF16).astype(F32)
    low = value - high - middle
    return jnp.where(part == 0, high, jnp.where(part == 1, middle, low))


def regroup_kernel(count, *refs):
    pieces, (mine, other) = refs[:count], refs[-2:]
    slot = pieces[0].shape[0] // CORES
    for i, piece in enumerate(pieces):
        mine[i * slot : (i + 1) * slot, :] = piece[:slot]
        other[i * slot : (i + 1) * slot, :] = piece[slot:]


def regroup(pieces, after):
    rows, wide = pieces[0].shape
    count = len(pieces)
    out = jax.ShapeDtypeStruct((count * rows // CORES, wide), BF16)
    return pl.pallas_call(
        functools.partial(regroup_kernel, count),
        out_shape=[out, out],
        in_specs=[vmem()] * count + [hbm()] * len(after),
        out_specs=[vmem()] * 2,
        compiler_params=params(16),
        name="regroup",
    )(*pieces, *after)


def assemble_kernel(slot, ids_ref, gates_ref, mine, other, *halves):
    rows, wide = halves[0].shape
    width = wide - LANES
    per_half = rows // slot
    me = lax.axis_index("dp")
    notes = gate_notes(ids_ref[...], gates_ref[...]).T
    for i in range(CORES * per_half):
        piece = (mine, other)[i % CORES][i // CORES * slot : (i // CORES + 1) * slot, :]
        place = me ^ i
        at = pl.multiple_of((place % per_half) * slot, slot)
        for h, half in enumerate(halves):

            @pl.when(place // per_half == h)
            def _(piece=piece, half=half, at=at):
                half[pl.ds(at, slot), :] = piece

    for h, half in enumerate(halves):
        own = notes[h * rows : (h + 1) * rows]
        half[:, width:] = (half[:, width:].astype(F32) + own).astype(BF16)


def assemble(mine, other, slot, ids, gates):
    return pl.pallas_call(
        functools.partial(assemble_kernel, slot),
        out_shape=[jax.ShapeDtypeStruct(mine.shape, BF16)] * 2,
        in_specs=[vmem()] * 4,
        out_specs=[vmem()] * 2,
        compiler_params=params(16),
        name="assemble",
    )(ids, gates, mine, other)


def send_sequences(gen_rows, gen_lengths, gen_adv, destination, n_dp):
    seq_dev = destination.shape[2]
    slot = gen_rows.shape[0] // seq_dev
    pieces = list(pick(destination, gen_lengths, gen_adv, gen_rows.reshape(seq_dev, slot, gen_rows.shape[1]), n_dp))
    for i in range(1, len(pieces)):
        pieces[i] = lax.ppermute(pieces[i], "dp", [(d, d ^ (CORES * i)) for d in range(n_dp)])
    return pieces


def place_sequences(mine, other, n_dp, seq_dev, ids, gates):
    slot = CORES * mine.shape[0] // n_dp
    if n_dp == seq_dev:
        return assemble(mine, other, slot, ids.T, gates.T)
    wide = mine.shape[1]
    width = wide - LANES
    g = lax.axis_index("dp")
    stack = jnp.stack([mine.reshape(-1, slot, wide), other.reshape(-1, slot, wide)], axis=1)
    stack = stack.reshape(n_dp, slot, wide)[jnp.arange(n_dp, dtype=jnp.int32) ^ g]
    arrived = stack[:, 0, width + LENGTH] > 0
    arrival = jnp.cumsum(arrived.astype(jnp.int32)) - 1
    chosen = arrived[None, :] & (arrival[None, :] == jnp.arange(seq_dev, dtype=jnp.int32)[:, None])
    from_peer = jnp.sum(jnp.where(chosen, jnp.arange(n_dp, dtype=jnp.int32)[None, :], 0), axis=1)
    x = stack[from_peer].reshape(seq_dev * slot, wide)
    notes = (x[:, width:].astype(F32) + gate_notes(ids.T, gates.T).T).astype(BF16)
    x = jnp.concatenate([x[:, :width], notes], axis=1)
    half = x.shape[0] // 2
    return x[:half], x[half:]


def swap(value, i, n_ex):
    return lax.ppermute(value, "expert", [(d, d ^ i) for d in range(n_ex)])


def gather_rows(rows, n_ex):
    if n_ex != 4:
        return [rows] + [swap(rows, i, n_ex) for i in range(1, n_ex)]
    half = rows.shape[0] // 2
    first = swap(rows, 1, n_ex)
    second = swap(rows, 2, n_ex)
    return [rows, first, second, swap(first[:half], 2, n_ex), swap(second[half:], 1, n_ex)]


def gather_halves(low, high, n_ex, between):
    if n_ex != 4:
        pieces = [low, high]
        for i in range(1, n_ex):
            pieces += [swap(low, i, n_ex), swap(high, i, n_ex)]
        return pieces
    first_low, second_high = swap(low, 1, n_ex), swap(high, 2, n_ex)
    first_high, second_low = swap(high, 1, n_ex), swap(low, 2, n_ex)
    on_low, on_high, _ = lax.optimization_barrier((first_low, second_high, between))
    return [low, high, first_low, first_high, second_low, second_high, swap(on_low, 2, n_ex), swap(on_high, 1, n_ex)]


def with_last(pieces, size):
    at, cut = 0, sum(p.shape[0] for p in pieces) - size
    for i, piece in enumerate(pieces):
        if at == cut:
            return pieces[:i], pieces[i:]
        at += piece.shape[0]


def tie(value, *others):
    return lax.optimization_barrier((value,) + others)[0]


def load_pieces(pieces, whole, sems):
    at, copies = 0, []
    for i, piece in enumerate(pieces):
        size = piece.shape[0]
        copies.append(pltpu.make_async_copy(piece, whole.at[pl.ds(at, size)], sems.at[i]))
        at += size
    for copy in copies:
        copy.start()
    for copy in copies:
        copy.wait()


def hidden_grad_kernel(count, w_ref, *refs):
    pieces, (out, whole_out, whole, sems, out_sem) = refs[:count], refs[count:]
    step = pl.program_id(0)

    @pl.when(step == 0)
    def _():
        load_pieces(pieces, whole, sems)
        pltpu.make_async_copy(whole, whole_out, out_sem).start()

    out[...] = contract(whole[...], w_ref[...], 1, 1)

    @pl.when(step == pl.num_programs(0) - 1)
    def _():
        pltpu.make_async_copy(whole, whole_out, out_sem).wait()


def hidden_grad(pieces, w_down):
    rows = sum(p.shape[0] for p in pieces)
    units, width = w_down.shape
    tile = 256
    return pl.pallas_call(
        functools.partial(hidden_grad_kernel, len(pieces)),
        grid=(units // tile,),
        out_shape=[jax.ShapeDtypeStruct((rows, units), F32), jax.ShapeDtypeStruct((rows, width), BF16)],
        in_specs=[pl.BlockSpec((tile, width), lambda j: (j, 0))] + [hbm()] * len(pieces),
        out_specs=[pl.BlockSpec((rows, tile), lambda j: (0, j)), hbm()],
        scratch_shapes=[
            pltpu.VMEM((rows, width), BF16),
            pltpu.SemaphoreType.DMA((len(pieces),)),
            pltpu.SemaphoreType.DMA,
        ],
        compiler_params=params(BIG),
        cost_estimate=cost(2 * rows * units * width, 2 * units * width + 4 * rows * width),
        name="hidden_grad",
    )(w_down, *pieces)


def shard_place(shard, n_dp):
    me = lax.axis_index("dp")
    n_z = n_dp // CORES
    chip, core = shard // CORES, shard % CORES
    at = jnp.where(me // CORES >= n_z // 2, chip, n_z - 1 - chip)
    return jnp.where(core == me % CORES, n_z, 0) + at


def units_kernel(count, slot, first, n_dp, wg_ref, wu_ref, hg_ref, *refs):
    if not first:
        refs = refs[6:]
    pieces, refs = refs[:count], refs[count:]
    gate_out, up_out, hid_out, turned_hs, turned_x, gates_out, whole, gs_ref, sems = refs
    step = pl.program_id(0)
    rows, wide = whole.shape
    width = wide - LANES

    @pl.when(step == 0)
    def _():
        load_pieces(pieces, whole, sems)
        notes = whole[:, width:].astype(F32)
        lane = lax.broadcasted_iota(jnp.int32, notes.shape, 1) - GATES - PARTS * lax.axis_index("expert")
        gates = jnp.sum(jnp.where((lane >= 0) & (lane < PARTS), notes, 0.0), axis=1, keepdims=True)
        length, adv = notes[:, LENGTH : LENGTH + 1], notes[:, ADV : ADV + 1]
        position = lax.broadcasted_iota(jnp.int32, (rows, 1), 0) % slot
        gates_out[...] = gates
        gs_ref[...] = jnp.where(position.astype(F32) < length, gates * (adv / length), 0.0)
        strip = width // n_dp
        for i in range(n_dp):
            at = pl.multiple_of(shard_place(i, n_dp) * strip, strip)
            turned_x[pl.ds(at, strip), :] = whole[:, i * strip : (i + 1) * strip].T

    x = whole[:, :width]
    here = pl.ds(pl.multiple_of(step * gate_out.shape[1], LANES), gate_out.shape[1])
    gate = jnp.dot(x, wg_ref[:, here], preferred_element_type=F32)
    up = jnp.dot(x, wu_ref[:, here], preferred_element_type=F32)
    gs = gs_ref[...]
    sig = jax.nn.sigmoid(gate)
    act = gate * sig
    hid = (act * up).astype(BF16)
    hid_out[...] = hid
    turned = (hid.astype(F32) * gs).astype(BF16).T
    tile, shard = turned.shape[0], turned_hs.shape[0] // n_dp
    chunk = math.gcd(tile, shard)
    for i in range(tile // chunk):
        row = step * tile + i * chunk
        at = shard_place(row // shard, n_dp) * shard + row % shard
        turned_hs[pl.ds(pl.multiple_of(at, chunk), chunk), :] = turned[i * chunk : (i + 1) * chunk]
    hg = hg_ref[...] * gs
    gate_out[...] = (hg * up * sig * (1.0 + gate * (1.0 - sig))).astype(BF16)
    up_out[...] = (hg * act).astype(BF16)


def hidden_units(pieces, w_gate, w_up, hg, slot, n_dp, before=None):
    total, units = hg.shape
    width = w_gate.shape[0]
    rows = sum(p.shape[0] for p in pieces)
    tile = 256
    at = 0 if before is None else total // rows - 1
    columns = pl.BlockSpec((rows, tile), lambda j: (at, j))
    weights = vmem()
    before = before or []
    return pl.pallas_call(
        functools.partial(units_kernel, len(pieces), slot, not before, n_dp),
        grid=(units // tile,),
        out_shape=[jax.ShapeDtypeStruct((total, units), BF16)] * 3
        + [
            jax.ShapeDtypeStruct((units, total), BF16),
            jax.ShapeDtypeStruct((width, total), BF16),
            jax.ShapeDtypeStruct((total, 1), F32),
        ],
        in_specs=[weights, weights, columns] + [hbm()] * (len(before) + len(pieces)),
        out_specs=[columns] * 3
        + [
            pl.BlockSpec((units, rows), lambda j: (0, at)),
            pl.BlockSpec((width, rows), lambda j: (0, at)),
            pl.BlockSpec((rows, 1), lambda j: (at, 0)),
        ],
        scratch_shapes=[
            pltpu.VMEM((rows, width + LANES), BF16),
            pltpu.VMEM((rows, 1), F32),
            pltpu.SemaphoreType.DMA((len(pieces),)),
        ],
        input_output_aliases={3 + i: i for i in range(len(before))},
        compiler_params=params(room(rows, width)),
        cost_estimate=cost(4 * rows * units * width, 4 * units * width + 4 * rows * width),
        name="hidden_units",
    )(w_gate, w_up, hg, *before, *pieces)


def far_grads_kernel(x_ref, gate_ref, up_ref, other, mine):
    gate = jnp.dot(x_ref[...], gate_ref[...], preferred_element_type=F32).astype(BF16)
    up = jnp.dot(x_ref[...], up_ref[...], preferred_element_type=F32).astype(BF16)

    @pl.when(pl.program_id(0) == 0)
    def _():
        other[0] = gate
        other[1] = up

    @pl.when(pl.program_id(0) == 1)
    def _():
        mine[0] = gate
        mine[1] = up


def far_grads(turned_x, gate_grad, up_grad, n_dp):
    rows, units = gate_grad.shape
    width = turned_x.shape[0]
    n_z, shard = n_dp // CORES, width // n_dp
    out = pl.BlockSpec((2, shard, units), lambda k: (0, 0, 0))
    whole = pl.BlockSpec((rows, units), lambda k: (0, 0))
    return pl.pallas_call(
        far_grads_kernel,
        grid=(CORES,),
        in_specs=[pl.BlockSpec((shard, rows), lambda k: (k * n_z, 0)), whole, whole],
        out_specs=[out, out],
        out_shape=[pltpu.HBM((2, shard, units), BF16)] * 2,
        compiler_params=params(BIG),
        cost_estimate=cost(8 * rows * units * shard, 16 * units * shard + 4 * rows * units),
        name="far_grads",
    )(turned_x, gate_grad, up_grad)


def rest_grads_kernel(shard, x_ref, gate_ref, up_ref, _, other, mine):
    count = other.shape[0]
    for k, out in enumerate((other, mine)):
        x = x_ref[pl.ds((k * (count + 1) + 1) * shard, count * shard), :]
        for p, grad in enumerate((gate_ref, up_ref)):
            value = jnp.dot(x, grad[...], preferred_element_type=F32).astype(BF16)
            for b in range(count):
                out[b, p] = value[b * shard : (b + 1) * shard]


def rest_grads(turned_x, gate_grad, up_grad, after, n_dp):
    rows, units = gate_grad.shape
    width = turned_x.shape[0]
    n_z, shard = n_dp // CORES, width // n_dp
    tile = 256
    columns = pl.BlockSpec((rows, tile), lambda j: (0, j))
    out = pl.BlockSpec((n_z - 1, 2, shard, tile), lambda j: (0, 0, 0, j))
    return pl.pallas_call(
        functools.partial(rest_grads_kernel, shard),
        grid=(units // tile,),
        in_specs=[pl.BlockSpec((width, rows), lambda j: (0, 0)), columns, columns, hbm()],
        out_specs=[out, out],
        out_shape=[pltpu.HBM((n_z - 1, 2, shard, units), BF16)] * 2,
        compiler_params=params(room(rows, width)),
        cost_estimate=cost(4 * rows * units * width, 4 * units * width + 4 * rows * units),
        name="rest_grads",
    )(turned_x, gate_grad, up_grad, after)


def row_grad_kernel(hid_ref, dy_ref, other, mine):
    n_z, shard, tile = mine.shape
    value = jnp.dot(hid_ref[...], dy_ref[...], preferred_element_type=F32).astype(BF16)
    for k, out in enumerate((other, mine)):
        for b in range(n_z):
            at = (k * n_z + b) * shard
            out[b] = value[at : at + shard]


def row_grad(turned_hid, dy, n_dp):
    units, rows = turned_hid.shape
    width = dy.shape[1]
    n_z, shard = n_dp // CORES, units // n_dp
    tile = 1024
    block = pl.BlockSpec((n_z, shard, tile), lambda j: (0, 0, j))
    return pl.pallas_call(
        row_grad_kernel,
        grid=(width // tile,),
        in_specs=[pl.BlockSpec((units, rows), lambda j: (0, 0)), pl.BlockSpec((rows, tile), lambda j: (0, j))],
        out_specs=[block, block],
        out_shape=[pltpu.HBM((n_z, shard, width), BF16)] * 2,
        compiler_params=params(room(rows, width)),
        cost_estimate=cost(2 * rows * units * width, 2 * units * width + 2 * rows * width),
        name="row_grad",
    )(turned_hid, dy)


def outputs_kernel(layer_groups, grad_groups, hid_ref, gates_ref, gate_ref, up_ref, wd_ref, wg_ref, wu_ref, _, *outs):
    layer = jnp.dot(hid_ref[...], wd_ref[...], preferred_element_type=F32) * gates_ref[...]
    value = contract(gate_ref[...], wg_ref[...], 1, 1) + contract(up_ref[...], wu_ref[...], 1, 1)
    size = outs[0].shape[1]
    for result, groups, refs in (
        (layer.astype(BF16), layer_groups, outs[: len(layer_groups)]),
        (value.astype(BF16), grad_groups, outs[len(layer_groups) :]),
    ):
        for group, out in zip(groups, refs):
            for n, i in enumerate(group):
                out[n] = result[i * size : (i + 1) * size]


def outputs(hid, gates, gate_grad, up_grad, w_down, w_gate, w_up, after, n_ex, layer_groups, grad_groups):
    rows, units = hid.shape
    width = w_down.shape[1]
    tile = 512
    size = rows // n_ex
    whole = pl.BlockSpec((rows, units), lambda j: (0, 0))
    columns = pl.BlockSpec((units, tile), lambda j: (0, j))
    weights = pl.BlockSpec((tile, units), lambda j: (j, 0))
    counts = [len(group) for group in layer_groups + grad_groups]
    return pl.pallas_call(
        functools.partial(outputs_kernel, layer_groups, grad_groups),
        grid=(width // tile,),
        out_shape=[jax.ShapeDtypeStruct((n, size, width), BF16) for n in counts],
        in_specs=[whole, pl.BlockSpec((rows, 1), lambda j: (0, 0)), whole, whole, columns, weights, weights, hbm()],
        out_specs=[pl.BlockSpec((n, size, tile), lambda j: (0, 0, j)) for n in counts],
        compiler_params=params(room(rows, width)),
        cost_estimate=cost(6 * rows * units * width, 6 * units * width + 4 * rows * width),
        name="outputs",
    )(hid, gates, gate_grad, up_grad, w_down, w_gate, w_up, after)


def add(*parts):
    return sum(part.astype(F32) for part in parts).astype(BF16)


def outputs_home(hid, gates, gate_grad, up_grad, w_down, w_gate, w_up, after, n_ex):
    weights = (hid, gates, gate_grad, up_grad, w_down, w_gate, w_up, after, n_ex)
    if n_ex != 4:
        single = [[i] for i in range(n_ex)]
        parts = outputs(*weights, single, single)
        layer, grad = [], []
        for i in range(n_ex):
            layer.append(swap(parts[i][0], i, n_ex) if i else parts[i][0])
            grad.append(swap(parts[n_ex + i][0], i, n_ex) if i else parts[n_ex + i][0])
        return add(*layer), add(*grad), []
    layer0, layer2, layer13, grad0, grad1, grad23 = outputs(*weights, [[0], [2], [1, 3]], [[0], [1], [2, 3]])
    layer_got = swap(layer13, 1, n_ex)
    grad_got = swap(grad23, 2, n_ex)
    layer_last = swap(add(layer2[0], layer_got[1]), 2, n_ex)
    grad_last = swap(add(grad1[0], grad_got[1]), 1, n_ex)
    layer, grad = add(layer0[0], layer_got[0], layer_last), add(grad0[0], grad_got[0], grad_last)
    return layer, grad, [layer_last, grad_last]


def fold_kernel(gu_mine, gu_got, row_mine, row_got, *refs):
    out = refs[-1]
    step = pl.program_id(0)

    def put(mine, got):
        value = (mine.astype(F32) + got.astype(F32)).astype(BF16)
        rows, columns = value.shape
        for i in range(columns // LANES):
            out[0, i * rows : (i + 1) * rows, :] = value[:, i * LANES : (i + 1) * LANES]

    @pl.when(step < 2)
    def _():
        put(gu_mine[0, 0], gu_got[0, 0])

    @pl.when(step == 2)
    def _():
        put(row_mine[0], row_got[0])


def fold(gu_mine, gu_got, row_mine, row_got, gu_at, row_at, piece, pieces, after):
    _, _, shard, units = gu_mine.shape
    _, row_shard, width = row_mine.shape
    per = shard * units // LANES // pieces
    gu = pl.BlockSpec((1, 1, shard, units // pieces), lambda j: (gu_at, jnp.minimum(j, 1), 0, piece))
    row = pl.BlockSpec((1, row_shard, width // pieces), lambda j: (row_at, 0, piece))
    return pl.pallas_call(
        fold_kernel,
        grid=(3,),
        in_specs=[gu, gu, row, row] + [hbm()] * len(after),
        out_specs=pl.BlockSpec((1, per, LANES), lambda j: (j, 0, 0)),
        out_shape=jax.ShapeDtypeStruct((3, per, LANES), BF16),
        compiler_params=params(16),
        cost_estimate=cost(6 * per * LANES, 18 * per * LANES),
        name="fold",
    )(gu_mine, gu_got, row_mine, row_got, *after)


def pass_on_kernel(own, got, *refs):
    refs[-1][...] = (own[...].astype(F32) + got[...].astype(F32)).astype(BF16)


def pass_on(own, got, piece, pieces, whole, after, weight=1):
    per, count = whole // pieces, got.shape[0]

    def part(array):
        at = piece if array.shape[1] > per else 0
        return pl.BlockSpec((count, per, LANES), lambda j: (0, at, 0))

    return pl.pallas_call(
        pass_on_kernel,
        grid=(1,),
        in_specs=[part(own), part(got)] + [hbm()] * len(after),
        out_specs=pl.BlockSpec((count, per, LANES), lambda j: (0, 0, 0)),
        out_shape=jax.ShapeDtypeStruct((count, per, LANES), BF16),
        compiler_params=params(16),
        cost_estimate=cost(2 * weight * got.size, 6 * weight * got.size),
        name="pass_on",
    )(own, got, *after)


def choose_kernel(place_ref, one, other, *refs):
    refs[-1][...] = jnp.where(place_ref[0] > 0, one[...].astype(F32), other[...].astype(F32)).astype(BF16)


def choose(place, one, other, after):
    block = pl.BlockSpec((1,) + one.shape[1:], lambda j, place: (j, 0, 0))
    return pl.pallas_call(
        choose_kernel,
        grid_spec=pltpu.PrefetchScalarGridSpec(
            num_scalar_prefetch=1,
            grid=(one.shape[0],),
            in_specs=[block, block] + [hbm()] * len(after),
            out_specs=block,
        ),
        out_shape=jax.ShapeDtypeStruct(one.shape, BF16),
        compiler_params=params(16),
        cost_estimate=cost(one.size, 6 * one.size),
        name="choose",
    )(place.reshape(1).astype(jnp.int32), one, other, *after)


def unfold_kernel(counts, *refs):
    parts, outs = refs[: sum(counts)], refs[sum(counts) :]
    for j, out in enumerate(outs):
        total, at = None, 0
        for count in counts:
            pieces = [part[j].astype(F32) for part in parts[at : at + count]]
            value = pieces[0] if count == 1 else jnp.concatenate(pieces, axis=0)
            total = value if total is None else total + value
            at += count
        total = total.astype(BF16)
        rows, columns = out.shape[1:]
        for i in range(columns // LANES):
            out[0, :, i * LANES : (i + 1) * LANES] = total[i * rows : (i + 1) * rows]


def unfold(groups, shapes):
    parts = [part for group in groups for part in group]
    return pl.pallas_call(
        functools.partial(unfold_kernel, [len(group) for group in groups]),
        grid=(1,),
        in_specs=[pl.BlockSpec(part.shape, lambda j: (0, 0, 0)) for part in parts],
        out_specs=[pl.BlockSpec(shape, lambda j: (0, 0, 0)) for shape in shapes],
        out_shape=[jax.ShapeDtypeStruct(shape, BF16) for shape in shapes],
        compiler_params=params(24),
        cost_estimate=cost(4 * parts[0].size, 10 * parts[0].size),
        name="unfold",
    )(*parts)


def chips_permute(value, pairs, n_dp):
    return lax.ppermute(value, "dp", [(CORES * a + c, CORES * b + c) for a, b in pairs for c in range(CORES)])


def on_device(
    gen_rows, gen_lengths, gen_adv, destination, expert_ids, gate_values, cotangent, w_gate, w_up, w_down
):
    n_dp = lax.axis_size("dp")
    n_ex = lax.axis_size("expert")
    n_z = n_dp // CORES
    size = cotangent.shape[0]
    slot = gen_rows.shape[0] // destination.shape[2]
    weight_gate, weight_up, weight_down = w_gate[0], w_up[0], w_down[0]
    g = lax.axis_index("dp")
    z = g // CORES
    near = jnp.minimum(z, n_z - 1 - z)
    other_core = [(d, d ^ 1) for d in range(n_dp)]

    def swap_core(value):
        return lax.ppermute(value, "dp", other_core)

    pieces = send_sequences(gen_rows, gen_lengths, gen_adv, destination, n_dp)
    cot_pieces = gather_rows(tie(cotangent, pieces[0]), n_ex)
    mine, other = regroup(pieces, cot_pieces[1:3])
    other = swap_core(other)
    low, high = place_sequences(mine, other, n_dp, destination.shape[2], expert_ids, gate_values)
    hg, dy_all = hidden_grad(cot_pieces, weight_down)
    x_pieces = gather_halves(low, high, n_ex, hg)
    early, late = with_last(x_pieces, size)
    before = hidden_units(early, weight_gate, weight_up, hg, slot, n_dp)
    gate_grad, up_grad, hid, turned_hs, turned_x, gates = hidden_units(
        late, weight_gate, weight_up, hg, slot, n_dp, before
    )

    far = n_z - 1
    rest = list(range(far - 1, -1, -1))
    far_other, far_mine = far_grads(turned_x, gate_grad, up_grad, n_dp)
    far_got = swap_core(far_other)
    row_other, row_mine = row_grad(tie(turned_hs, far_other), dy_all, n_dp)
    row_got = swap_core(row_other)
    whole = w_gate.shape[1] * w_gate.shape[2] // n_dp // LANES
    far_sum = fold(far_mine[None], far_got[None], row_mine, row_got, 0, 0, 0, 1, [])
    rest_other, rest_mine = rest_grads(turned_x, gate_grad, up_grad, far_got, n_dp)
    rest_got = swap_core(rest_other)

    def block(k, *after):
        return fold(rest_mine, rest_got, row_mine, row_got, far - 1 - k, far - k, 0, 1, after)

    if n_z == 4:
        outward, across = [(0, 1), (3, 2)], [(0, 1), (1, 0), (2, 3), (3, 2)]
        three = chips_permute(far_sum, outward, n_dp)
        sum_two = block(2)
        two = chips_permute(sum_two, outward, n_dp)
        sum_one, sum_none = block(1), block(0)
        three_sum = pass_on(far_sum, three, 0, 1, whole, [sum_two])
        three_on = chips_permute(three_sum, [(1, 3), (2, 0)], n_dp)
        two_sum = pass_on(sum_two, two, 0, 1, whole, [])
        two_on = chips_permute(tie(two_sum, three_on), [(1, 2), (2, 1)], n_dp)
        last = chips_permute(choose(near, sum_none, sum_one, [two]), across, n_dp)
        own = add(jnp.where(near > 0, sum_one, sum_none), three_on)
        ends = [[last], [two_on]]
    else:
        sums = [block(k) for k in range(far)] + [far_sum]
        passed, ends = {}, []
        for link in range(far):
            for d in range(far, link, -1):
                value = sums[d if link < n_z // 2 else far - d]
                if link > 0:
                    value = pass_on(value, passed[link - 1, d], 0, 1, whole, [])
                pairs = [(link, link + 1), (far - link, far - 1 - link)]
                passed[link, d] = chips_permute(value, pairs, n_dp)
                if d == link + 1:
                    ends.append([passed[link, d]])
        own = sums[0]
        for k in range(1, (n_z + 1) // 2):
            own = jnp.where(near == k, sums[k], own)
    shapes = [(1, w_gate.shape[1] // n_dp, w_gate.shape[2])] * 2 + [(1, w_down.shape[1] // n_dp, w_down.shape[2])]
    totals = unfold([[own]] + ends, shapes)

    layer_out, input_grad, _ = outputs_home(
        hid, gates, gate_grad, up_grad, weight_down, weight_gate, weight_up, far_sum, n_ex
    )
    return layer_out, input_grad, *totals


def solution(mesh):
    rows = P(("dp", "expert"), None)
    seqs = P("dp", "expert", None)
    weights = P("expert", None, None)
    shards = P("expert", "dp", None)
    return jax.shard_map(
        on_device,
        mesh=mesh,
        in_specs=(rows, seqs, seqs, seqs, rows, rows, rows, weights, weights, weights),
        out_specs=(rows, rows, shards, shards, shards),
        check_vma=False,
    )
```
